32 devices in a mesh: grp: 2 (over y), ep: 4 (over z), hd: 2 (over x), sub: 2 (over core).
Axes of the slice: x: 2, y: 2, z: 4, core: 2. Of those that a mesh axis runs over, the one named last changes fastest.
Arguments:
- queries: bfloat16 [2048, 4096], P(('grp', 'ep'), 'hd'), parts along dimension 0, may hold values from -1024 to 1024
- cache_keys: bfloat16 [2048, 512], P(('grp', 'ep', 'sub')), parts along dimension 0, may hold values from -4 to 4
- cache_values: bfloat16 [2048, 512], P(('grp', 'ep', 'sub')), parts along dimension 0, may hold values from -12 to 12
- page_len: int32 [16], P(('grp', 'ep', 'sub')), parts along dimension 0, may hold values from 1 to 128, 512 in all
- new_keys: bfloat16 [2048, 512], P(('grp', 'ep', 'sub')), parts along dimension 0, may hold values from -6 to 6
- new_values: bfloat16 [2048, 512], P(('grp', 'ep', 'sub')), parts along dimension 0, may hold values from -6 to 6
- out_proj: bfloat16 [4096, 2048], P('hd', 'sub'), may hold values from -0.09375 to 0.09375
- residual: bfloat16 [2048, 2048], P(('grp', 'ep', 'hd'), 'sub'), parts along dimension 0, may hold values from -6 to 6
- norm_gain: bfloat16 [2048], replicated, may hold values from 0.099609375 to 1.8984375
- gate_up: bfloat16 [8, 2, 384, 2048], P(('ep', 'hd'), None, 'sub'), may hold values from -0.125 to 0.125
- w_down: bfloat16 [8, 384, 2048], P(('ep', 'hd'), 'sub'), may hold values from -0.3125 to 0.3125
- expert_ids: int32 [2048, 8], P(('grp', 'ep', 'hd')), parts along dimension 0, may hold values from 0 to 7, as said below
- gates: bfloat16 [2048, 8], P(('grp', 'ep', 'hd')), parts along dimension 0, may hold values from 0.049804688 to 0.5
Outputs:
- layer_out: bfloat16 [2048, 2048], P(('grp', 'ep', 'hd'), 'sub'), parts along dimension 0
The draws below stay inside these ranges and needn't reach their ends.
There are 2 independent parts, one for each index of `grp`. The reference program is written for one: setup_inputs(seed, part) draws one part's arguments, and reference() takes and returns one part's arrays. A program takes and returns all parts, laid end to end along the dimension named above; an argument that names none is the same for every part. Nothing has to cross between parts.
Inputs may be any that keep to these rules, and one draw needn't show every extreme that they name: `expert_ids`: expert x belongs to group x // 2. Each row names 8 different experts, exactly two in each of 4 different groups. Among the rows of one block b (rows b * 128 to (b + 1) * 128 - 1), each group is named by at most 128 rows and each expert by at most 128; in every block some group is named by exactly 128 rows and some expert by exactly 128.
All inputs are finite; a program needn't handle non-finite values. No bound on the sum of `page_len` on one device may be relied on, other than what follows from the above.
Results may differ from the reference program's by a relative error of at most 0.02.
Values may be sent and summed in bfloat16 or wider, within the bound.
No kernel may reach another device: no remote copies, remote signals or barrier semaphores. Data moves between devices by JAX's collectives and lax.ppermute only.
A program may use at most 64 MiB of HBM per device.

```python
import math
import jax
import jax.numpy as jnp
import numpy as np
from jax import lax

D = 2048
QH = 32
KVH = 4
HD = 128
FF = 384
TOPK = 8
GROUPS_ROW = 4
CACHE_DEV = 128
ROWS = 1024
PAGES = 8
CACHE = 1024
GROUPS = 4
GROUP_EXPERTS = 2
EXPERTS = 8
RM = 128
CAPG = 128
CAP = 128


def drawn_fields(key):
    key_field = jnp.clip(jax.random.normal(jax.random.fold_in(key, 101), (CACHE, KVH * HD), jnp.float32), -4.0, 4.0)
    query_field = jnp.clip(jax.random.normal(jax.random.fold_in(key, 102), (ROWS, QH * HD), jnp.float32), -4.0, 4.0)
    return (query_field, key_field)


def draw_queries(key, part):
    return drawn_fields(key)[0].astype(jnp.bfloat16)


def draw_cache_keys(key, part):
    return drawn_fields(key)[1].astype(jnp.bfloat16)


def draw_expert_ids(key, part):
    blocks = ROWS // RM
    order_keys = jax.random.split(jax.random.fold_in(key, 301), blocks)
    row_keys = jax.random.split(jax.random.fold_in(key, 302), blocks)
    group_orders = jax.vmap(lambda one_key: jax.random.permutation(one_key, GROUPS))(order_keys).astype(jnp.int32)
    row_orders = jax.vmap(lambda one_key: jax.random.permutation(one_key, RM))(row_keys).astype(jnp.int32)
    hot_group = group_orders[:, 0]
    others = group_orders[:, 1:]
    is_hot = (row_orders < CAPG).astype(jnp.int32)
    needed = GROUPS_ROW - is_hot
    offsets = jax.random.randint(jax.random.fold_in(key, 303), (blocks, 1), 0, GROUPS - 1).astype(jnp.int32)
    first_pick = jnp.cumsum(needed, axis=1) - needed + offsets
    columns = jnp.arange(GROUPS_ROW, dtype=jnp.int32)
    pick_index = (first_pick[:, :, None] + columns[None, None, :] - is_hot[:, :, None]) % (GROUPS - 1)
    other_pick = jnp.take_along_axis(jnp.broadcast_to(others[:, None, :], (blocks, RM, GROUPS - 1)), pick_index, axis=2)
    use_hot = (is_hot[:, :, None] > 0) & (columns[None, None, :] == 0)
    group_ids = jnp.where(use_hot, hot_group[:, None, None], other_pick).astype(jnp.int32)
    member = (group_ids[:, :, :, None] == jnp.arange(GROUPS, dtype=jnp.int32)[None, None, None, :]).astype(jnp.int32)
    row_member = jnp.sum(member, axis=2)
    ordinal_all = jnp.cumsum(row_member, axis=1) - row_member
    ordinal = jnp.sum(member * ordinal_all[:, :, None, :], axis=3)
    shifts = jax.random.randint(jax.random.fold_in(key, 304), (blocks, GROUPS), 0, GROUP_EXPERTS).astype(jnp.int32)
    shift_chosen = jnp.sum(member * shifts[:, None, None, :], axis=3)
    first_local = (2 * ordinal + shift_chosen) % GROUP_EXPERTS
    second_local = (2 * ordinal + 1 + shift_chosen) % GROUP_EXPERTS
    expert_pair = jnp.stack([group_ids * GROUP_EXPERTS + first_local, group_ids * GROUP_EXPERTS + second_local], axis=3)
    return expert_pair.reshape(ROWS, TOPK).astype(jnp.int32)


def level_of(key, extent, shards, low, high):
    gain, own = 1.0, jax.random.fold_in(key, 6)
    for position, shards_of in shards:
        heights = jnp.exp(jax.random.uniform(jax.random.fold_in(own, position), (shards_of,), jnp.float32, low / len(shards), high / len(shards)))
        gain = gain * jnp.repeat(heights, extent[position] // shards_of).reshape([-1 if axis == position else 1 for axis in range(len(extent))])
    return gain


def length_profile(amount, total, bound, skew):
    loads = [(1 << 20) // math.isqrt(rank ** skew) + 1 for rank in range(2, amount + 1)]
    rest, counts = total - bound - (amount - 1), [1] * (amount - 1)
    while rest > 0:
        movable = [i for i in range(amount - 1) if counts[i] < bound]
        mass, left = sum([loads[i] for i in movable]), rest
        for i in movable:
            more = min(bound - counts[i], max(1, left * loads[i] // mass), rest)
            counts[i] = counts[i] + more
            rest = rest - more
    return np.array([bound] + counts)


def uneven(key, number_of, total, reach, skew):
    if number_of == 2:
        one = jax.random.randint(key, (), max(1, total - reach), min(reach, total - 1) + 1)
        return jnp.stack([one, total - one])
    sizes = jnp.asarray(length_profile(number_of, total, reach, skew), jnp.int32)
    couples = (number_of - 1) // 2
    donor, sink = sizes[1:1 + 2 * couples:2], sizes[2:2 + 2 * couples:2]
    room = jnp.minimum(donor - 1, reach - sink)
    passed = jax.random.randint(jax.random.fold_in(key, 1), (couples,), 0, 1 << 20) % (room + 1)
    sizes = sizes.at[1:1 + 2 * couples:2].set(donor - passed).at[2:2 + 2 * couples:2].set(sink + passed)
    return sizes[jax.random.permutation(jax.random.fold_in(key, 2), number_of)]


def centred(stream_key, extent, width, bound, shards=(), held_as=jnp.bfloat16):
    array = width * jax.random.normal(stream_key, extent, jnp.float32)
    if shards:
        array = array * level_of(stream_key, extent, shards, -0.22, 0.18)
    return jnp.clip(array, -bound, bound).astype(held_as)


def setup_inputs(seed: int = 0, part: int = 0) -> dict:
    keys = jax.random.split(jax.random.key(seed), 14)
    own_keys = jax.random.split(jax.random.fold_in(keys[13], part), 14)
    return {
        "queries": draw_queries(jax.random.fold_in(jax.random.fold_in(keys[13], part), 71), part),
        "cache_keys": draw_cache_keys(jax.random.fold_in(jax.random.fold_in(keys[13], part), 71), part),
        "cache_values": centred(own_keys[2], (CACHE, KVH * HD), 2.0, 12.0, ((0, 8),)),
        "page_len": uneven(own_keys[3], PAGES, PAGES * CACHE_DEV // 2, CACHE_DEV, 2).astype(jnp.int32),
        "new_keys": centred(own_keys[4], (ROWS, KVH * HD), 1.0, 6.0, ((0, 8),)),
        "new_values": centred(own_keys[5], (ROWS, KVH * HD), 1.0, 6.0, ((0, 8),)),
        "out_proj": centred(keys[6], (QH * HD, D), (QH * HD) ** -0.5, 0.09375, ((0, 2), (1, 2))),
        "residual": centred(own_keys[7], (ROWS, D), 1.0, 6.0, ((0, 8), (1, 2))),
        "norm_gain": jnp.clip(1.0 + 0.18 * jax.random.normal(keys[8], (D,), jnp.float32), 0.099609375, 1.8984375).astype(jnp.bfloat16),
        "gate_up": centred(keys[9], (EXPERTS, 2, FF, D), D ** -0.5, 0.125, ((0, 8), (2, 2))),
        "w_down": centred(keys[10], (EXPERTS, FF, D), FF ** -0.5, 0.3125, ((0, 8), (1, 2))),
        "expert_ids": draw_expert_ids(jax.random.fold_in(jax.random.fold_in(keys[13], part), 71), part),
        "gates": jnp.clip(jnp.exp(math.log(0.5) - 2.306499 * jax.random.uniform(own_keys[12], (ROWS, TOPK), jnp.float32) ** level_of(own_keys[12], (ROWS, TOPK), ((0, 8),), -0.2, 0.2)), 0.049804688, 0.5).astype(jnp.bfloat16),
    }


EPSILON = 1e-06

def visible_mask(page_len):
    positions = jnp.arange(CACHE, dtype=jnp.int32)
    cache_ok = positions % CACHE_DEV < page_len[positions // CACHE_DEV]
    row_index = jnp.arange(ROWS, dtype=jnp.int32)
    causal = row_index[None, :] <= row_index[:, None]
    return jnp.concatenate([jnp.broadcast_to(cache_ok[None, :], (ROWS, CACHE)), causal], axis=1)

def attention(queries, joined_keys, joined_values, visible):
    score_scale = 1.0 / math.sqrt(HD)
    per_group = QH // KVH

    def one_head(head_index):
        kv_index = head_index // per_group
        query_head = lax.dynamic_slice_in_dim(queries, head_index * HD, HD, 1)
        key_head = lax.dynamic_slice_in_dim(joined_keys, kv_index * HD, HD, 1)
        value_head = lax.dynamic_slice_in_dim(joined_values, kv_index * HD, HD, 1)
        scores = jnp.dot(query_head, key_head.T, preferred_element_type=jnp.float32) * score_scale
        masked = jnp.where(visible, scores, -jnp.inf)
        row_max = lax.optimization_barrier(jnp.max(masked, axis=1, keepdims=True))
        exp_terms = jnp.where(visible, jnp.exp(scores - row_max), 0.0)
        weight_sum = lax.optimization_barrier(jnp.sum(exp_terms, axis=1, keepdims=True))
        mixed = jnp.dot(exp_terms.astype(jnp.bfloat16), value_head, preferred_element_type=jnp.float32)
        return mixed / weight_sum
    heads_out = lax.map(one_head, jnp.arange(QH, dtype=jnp.int32))
    return jnp.transpose(heads_out, (1, 0, 2)).reshape(ROWS, QH * HD).astype(jnp.bfloat16)

def experts_apply(normed, expert_ids, gates, gate_up, w_down):
    blocks = ROWS // RM
    flat_ids = expert_ids.reshape(blocks, RM * TOPK)
    onehot = (flat_ids[:, :, None] == jnp.arange(EXPERTS, dtype=jnp.int32)[None, None, :]).astype(jnp.int32)
    before = jnp.cumsum(onehot, axis=1) - onehot
    slot_index = lax.optimization_barrier(jnp.sum(before * onehot, axis=2))
    block_index = jnp.arange(blocks, dtype=jnp.int32)[:, None]
    row_index = block_index * RM + jnp.arange(RM * TOPK, dtype=jnp.int32)[None, :] // TOPK
    target = ((flat_ids * blocks + block_index) * CAP + slot_index).reshape(-1).astype(jnp.int32)
    table_rows = jnp.zeros((EXPERTS * blocks * CAP,), jnp.int32).at[target].set(row_index.reshape(-1).astype(jnp.int32))
    table_gates = jnp.zeros((EXPERTS * blocks * CAP,), jnp.float32).at[target].set(gates.reshape(-1).astype(jnp.float32))

    def one_expert(accumulated, operands):
        rows_x, gates_x, weight_pair, weight_down = operands
        inputs = normed[rows_x]
        gate_part = jnp.dot(inputs, weight_pair[0].T, preferred_element_type=jnp.float32)
        up_part = jnp.dot(inputs, weight_pair[1].T, preferred_element_type=jnp.float32)
        activation = (jax.nn.silu(gate_part) * up_part).astype(jnp.bfloat16)
        result = jnp.dot(activation, weight_down, preferred_element_type=jnp.float32).astype(jnp.bfloat16)
        accumulated = accumulated.at[rows_x].add(gates_x[:, None] * result.astype(jnp.float32))
        return (accumulated, None)
    accumulated, _ = lax.scan(one_expert, jnp.zeros((ROWS, D), jnp.float32), (table_rows.reshape(EXPERTS, blocks * CAP), table_gates.reshape(EXPERTS, blocks * CAP), gate_up, w_down))
    return accumulated

def reference(queries, cache_keys, cache_values, page_len, new_keys, new_values, out_proj, residual, norm_gain, gate_up, w_down, expert_ids, gates):
    visible = visible_mask(page_len)
    joined_keys = jnp.concatenate([cache_keys, new_keys], axis=0)
    joined_values = jnp.concatenate([cache_values, new_values], axis=0)
    attended = attention(queries, joined_keys, joined_values, visible)
    projected = jnp.dot(attended, out_proj, preferred_element_type=jnp.float32)
    hidden_state = (residual.astype(jnp.float32) + projected).astype(jnp.bfloat16)
    widened = hidden_state.astype(jnp.float32)
    mean_square = lax.optimization_barrier(jnp.mean(widened * widened, axis=1, keepdims=True))
    normed = (widened * lax.rsqrt(mean_square + EPSILON) * norm_gain.astype(jnp.float32)).astype(jnp.bfloat16)
    mixture = experts_apply(normed, expert_ids, gates, gate_up, w_down)
    return (widened + mixture).astype(jnp.bfloat16)
```

```python
import math

import jax
import jax.numpy as jnp
from jax import lax
from jax.experimental import pallas as pl
from jax.experimental.pallas import tpu as pltpu
from jax.sharding import PartitionSpec as P

QH = 32
KVH = 4
HD = 128
GROUPS_ROW = 4
NEG_FILL = -1e30
EPSILON = 1e-06
MASK_ROWS = 16
LANES = 128
MIB = 1024 * 1024
CONTRACT_LAST = (((1,), (1,)), ((), ()))


def block_sizes(block_rows, group_total, experts_group):
    group_slots = min(block_rows, 3 * GROUPS_ROW * block_rows // (2 * group_total))
    return (group_slots, 2 * group_slots // experts_group)


def cycle(size, step=1):
    return [(i, (i + step) % size) for i in range(size)]


def sub_copies(x):
    size = lax.axis_size("sub")
    return [x] + [lax.ppermute(x, "sub", cycle(size, step)) for step in range(1, size)]


def by_sub(copies):
    size = len(copies)
    me = lax.axis_index("sub")
    ordered = []
    for target in range(size):
        value = copies[0]
        for step in range(1, size):
            value = jnp.where((me - step) % size == target, copies[step], value)
        ordered.append(value)
    return ordered


def sub_exchange(x, axis):
    size = lax.axis_size("sub")
    me = lax.axis_index("sub")
    length = x.shape[axis] // size

    def part(index):
        return lax.dynamic_slice_in_dim(x, index * length, length, axis)

    came = [part(me)]
    for step in range(1, size):
        came.append(lax.ppermute(part((me + step) % size), "sub", cycle(size, step)))
    return came


def pack_keys(cache_keys, cache_values, new_keys, new_values, page_len, kv_heads, heads_here):
    width = kv_heads * HD
    cache_rows, new_rows = cache_keys.shape[0], new_keys.shape[0]
    group_width = QH // KVH
    rows = cache_rows + new_rows + MASK_ROWS

    def kernel(page_ref, ck_ref, cv_ref, nk_ref, nv_ref, out_ref):
        first = lax.axis_index("hd") * heads_here // group_width
        columns = pl.ds(pl.multiple_of(first * HD, HD), width)
        out_ref[:cache_rows, :width] = ck_ref[:, columns]
        out_ref[:cache_rows, width:] = cv_ref[:, columns]
        out_ref[cache_rows : cache_rows + new_rows, :width] = nk_ref[:, columns]
        out_ref[cache_rows : cache_rows + new_rows, width:] = nv_ref[:, columns]
        lane = lax.broadcasted_iota(jnp.int32, (MASK_ROWS, 2 * width), 1)
        bias = jnp.where(lane < page_ref[0], 0.0, NEG_FILL)
        out_ref[cache_rows + new_rows :, :] = bias.astype(out_ref.dtype)

    vmem = pl.BlockSpec(memory_space=pltpu.VMEM)
    return pl.pallas_call(
        kernel,
        out_shape=jax.ShapeDtypeStruct((rows, 2 * width), cache_keys.dtype),
        in_specs=[pl.BlockSpec(memory_space=pltpu.SMEM)] + [vmem] * 4,
        out_specs=vmem,
        name="pack_keys",
    )(page_len, cache_keys, cache_values, new_keys, new_values)


def attend(queries, stages, state, cache_rows, kv_heads, last):
    n_hd, n_sub, rows, columns = queries.shape
    heads = columns // HD
    per_kv = heads // kv_heads
    width = kv_heads * HD
    stack = 2 if per_kv % 2 == 0 else 1
    all_rows = n_hd * rows
    hops = [hop for hop, blocks in stages for _ in blocks]
    sources = [step for _, blocks in stages for step in range(len(blocks))]
    blocks = [block for _, stage_blocks in stages for block in stage_blocks]
    new_rows = blocks[0].shape[0] - cache_rows - MASK_ROWS
    keys = cache_rows + new_rows
    factor = math.log2(math.e) / math.sqrt(HD)
    relative = n_hd == 2

    def kernel(*refs):
        q_ref, refs = refs[0], refs[1:]
        block_refs, refs = refs[: len(blocks)], refs[len(blocks) :]
        if state is not None:
            (m_in, acc_in), refs = refs[:2], refs[2:]
        sub = lax.axis_index("sub")
        ep = lax.axis_index("ep")
        hd = lax.axis_index("hd")
        places = [(hd + j) % n_hd if relative else j for j in range(n_hd)]
        biases = []
        for hop, step, block in zip(hops, sources, block_refs):
            cache_bias = block[keys : keys + 1, :cache_rows].astype(jnp.float32)
            if hop == 0:
                key_id = ((sub - step) % n_sub) * new_rows + lax.broadcasted_iota(
                    jnp.int32, (rows, new_rows), 1
                )
                row_id = lax.broadcasted_iota(jnp.int32, (rows, new_rows), 0)
                parts = [
                    jnp.where(
                        key_id <= row_id + (place * n_sub + sub) * rows, 0.0, NEG_FILL
                    )
                    for place in places
                ]
                new_bias = jnp.concatenate(parts * stack, axis=0)
                cache_bias = jnp.broadcast_to(cache_bias, (stack * all_rows, cache_rows))
            else:
                new_bias = jnp.full(
                    (1, new_rows), jnp.where(ep >= hop, 0.0, NEG_FILL), jnp.float32
                )
            biases.append(jnp.concatenate([cache_bias, new_bias], axis=1))
        ones = jnp.ones((keys, HD), jnp.bfloat16)
        for kv in range(kv_heads):
            key_parts = [block[:keys, kv * HD : (kv + 1) * HD] for block in block_refs]
            value_parts = [
                jnp.concatenate(
                    [block[:keys, width + kv * HD : width + (kv + 1) * HD], ones], axis=1
                )
                for block in block_refs
            ]
            for first in range(kv * per_kv, (kv + 1) * per_kv, stack):
                q = jnp.concatenate(
                    [
                        q_ref[place, sub, :, h * HD : (h + 1) * HD]
                        for h in range(first, first + stack)
                        for place in places
                    ],
                    axis=0,
                )
                terms = [
                    lax.dot_general(q, k, CONTRACT_LAST, preferred_element_type=jnp.float32)
                    * factor
                    + bias
                    for k, bias in zip(key_parts, biases)
                ]
                top = jnp.max(terms[0], axis=1, keepdims=True)
                for term in terms[1:]:
                    top = jnp.maximum(top, jnp.max(term, axis=1, keepdims=True))
                if state is not None:
                    top_in = m_in[first * all_rows : (first + stack) * all_rows, :]
                    top = jnp.maximum(top, top_in)[:, :1]
                acc = None
                for term, v in zip(terms, value_parts):
                    weights = jnp.exp2(term - top).astype(jnp.bfloat16)
                    product = jnp.dot(weights, v, preferred_element_type=jnp.float32)
                    acc = product if acc is None else acc + product
                if state is not None:
                    scale = jnp.exp2(top_in[:, :1] - top)
                    acc = acc + scale * acc_in[first * all_rows : (first + stack) * all_rows, :]
                if last:
                    out = (acc[:, :HD] / acc[:, HD:]).astype(jnp.bfloat16)
                    for s in range(stack):
                        refs[0][:, (first + s) * HD : (first + s + 1) * HD] = out[
                            s * all_rows : (s + 1) * all_rows
                        ]
                else:
                    refs[0][first * all_rows : (first + stack) * all_rows, :] = jnp.broadcast_to(
                        top, (stack * all_rows, LANES)
                    )
                    refs[1][first * all_rows : (first + stack) * all_rows, :] = acc

    vmem = pl.BlockSpec(memory_space=pltpu.VMEM)
    if last:
        out_shape = jax.ShapeDtypeStruct((all_rows, columns), jnp.bfloat16)
        out_specs = vmem
    else:
        out_shape = (
            jax.ShapeDtypeStruct((heads * all_rows, LANES), jnp.float32),
            jax.ShapeDtypeStruct((heads * all_rows, 2 * HD), jnp.float32),
        )
        out_specs = (vmem, vmem)
    operands = [queries] + blocks + (list(state) if state is not None else [])
    scores = all_rows * heads * keys * len(blocks)
    return pl.pallas_call(
        kernel,
        out_shape=out_shape,
        in_specs=[vmem] * len(operands),
        out_specs=out_specs,
        compiler_params=pltpu.CompilerParams(vmem_limit_bytes=24 * MIB),
        cost_estimate=pl.CostEstimate(
            flops=6 * scores * HD, bytes_accessed=4 * MIB, transcendentals=scores
        ),
        name="attend",
    )(*operands)


def apply_expert(inputs, gate_up, w_down):
    features = w_down[0].shape[1]
    hidden = w_down[0].shape[0]
    rows = sum(x.shape[0] for x in inputs)

    def kernel(*refs):
        x_refs, refs = refs[: len(inputs)], refs[len(inputs) :]
        gu_refs, refs = refs[: len(gate_up)], refs[len(gate_up) :]
        down_refs, (out_ref,) = refs[: len(w_down)], refs[len(w_down) :]
        mine = lax.axis_index("ep") * lax.axis_size("hd") + lax.axis_index("hd")
        joined = jnp.concatenate([x[...] for x in x_refs], axis=0)
        x = joined[:, :features]
        table = joined[:, features:].astype(jnp.float32)
        lane = lax.broadcasted_iota(jnp.int32, table.shape, 1)
        gate = jnp.sum(jnp.where(lane == mine, table, 0.0), axis=1, keepdims=True)
        total = None
        for gu, down in zip(gu_refs, down_refs):
            gate_part = lax.dot_general(
                x, gu[0], CONTRACT_LAST, preferred_element_type=jnp.float32
            )
            up_part = lax.dot_general(x, gu[1], CONTRACT_LAST, preferred_element_type=jnp.float32)
            activation = (gate_part / (1.0 + jnp.exp(-gate_part)) * up_part).astype(jnp.bfloat16)
            product = jnp.dot(activation, down[...], preferred_element_type=jnp.float32)
            total = product if total is None else total + product
        out_ref[...] = gate * total.astype(jnp.bfloat16).astype(jnp.float32)

    vmem = pl.BlockSpec(memory_space=pltpu.VMEM)
    operands = list(inputs) + list(gate_up) + list(w_down)
    return pl.pallas_call(
        kernel,
        out_shape=jax.ShapeDtypeStruct((rows, features), jnp.float32),
        in_specs=[vmem] * len(operands),
        out_specs=vmem,
        compiler_params=pltpu.CompilerParams(vmem_limit_bytes=24 * MIB),
        cost_estimate=pl.CostEstimate(
            flops=6 * rows * hidden * len(w_down) * features,
            bytes_accessed=6 * MIB,
            transcendentals=rows * hidden * len(w_down),
        ),
        name="apply_expert",
    )(*operands)


def chip_ring(n_ep, n_hd):
    if n_hd == 2:
        return [z * 2 for z in range(n_ep)] + [z * 2 + 1 for z in reversed(range(n_ep))]
    return list(range(n_ep * n_hd))


def dense_experts(normed, gate_table, gate_up, w_down):
    axes = ("ep", "hd")
    walk = chip_ring(lax.axis_size("ep"), lax.axis_size("hd"))
    size = len(walk)
    ahead = [(walk[i], walk[(i + 1) % size]) for i in range(size)]
    back = [(b, a) for a, b in ahead]
    rows, features = normed.shape
    half = rows // 2
    reach = size // 2
    own = jnp.concatenate([normed, gate_table], axis=1)
    from_back, from_ahead = [own], [own]
    for hop in range(1, reach + 1):
        behind, before = from_back[-1], from_ahead[-1]
        if hop == reach:
            behind, before = behind[:half], before[half:]
        from_back.append(lax.ppermute(behind, axes, ahead))
        from_ahead.append(lax.ppermute(before, axes, back))
    mine = apply_expert([own], gate_up, w_down)
    outs = []
    for hop in range(1, reach + 1):
        both = apply_expert([from_back[hop], from_ahead[hop]], gate_up, w_down)
        cut = both.shape[0] // 2
        outs.append((both[:cut], both[cut:]))
    to_back, to_ahead = outs[-1]
    for hop in range(reach - 1, -1, -1):
        to_back = lax.ppermute(to_back.astype(jnp.bfloat16), axes, back).astype(jnp.float32)
        to_ahead = lax.ppermute(to_ahead.astype(jnp.bfloat16), axes, ahead).astype(jnp.float32)
        if hop == reach - 1:
            empty = jnp.zeros((rows - half, features), jnp.float32)
            to_back = jnp.concatenate([to_back, empty], axis=0)
            to_ahead = jnp.concatenate([empty, to_ahead], axis=0)
        if hop > 0:
            to_back = to_back + outs[hop - 1][0]
            to_ahead = to_ahead + outs[hop - 1][1]
    return mine + to_back + to_ahead


def sparse_experts(widened, normed, gate_up, w_down, expert_ids, gates, features):
    half_width = normed.shape[1]
    pair_weights = gate_up[0].reshape(-1, features)
    hidden_units = w_down.shape[1]
    group_total = lax.axis_size("ep")
    group_experts = lax.axis_size("hd")
    all_experts = group_total * group_experts
    block_rows = expert_ids.shape[0]
    group_slots, expert_slots = block_sizes(block_rows, group_total, group_experts)
    chosen = (
        expert_ids[:, :, None] == jnp.arange(all_experts, dtype=jnp.int32)[None, None, :]
    ).astype(jnp.int32)
    named_count = jnp.sum(chosen, axis=1)
    earlier = jnp.cumsum(named_count, axis=0) - named_count
    slot_index = jnp.sum(chosen * earlier[:, None, :], axis=2)
    position = expert_ids * expert_slots + slot_index
    slot_columns = jnp.arange(all_experts * expert_slots, dtype=jnp.int32)
    gate_table = jnp.sum(
        jnp.where(
            position[:, :, None] == slot_columns[None, None, :],
            gates.astype(jnp.float32)[:, :, None],
            0.0,
        ),
        axis=1,
    ).astype(jnp.bfloat16)
    placed = (gate_table != 0).astype(jnp.bfloat16)
    outgoing = jnp.einsum("rq,rd->qd", placed, normed, preferred_element_type=jnp.float32).astype(
        jnp.bfloat16
    )
    outgoing = outgoing.reshape(all_experts, expert_slots, normed.shape[1])
    arrived = lax.all_to_all(outgoing, ("ep", "hd"), split_axis=0, concat_axis=0, tiled=True)
    lead_shape = arrived.shape[:-1]
    rows_in = arrived.reshape(-1, arrived.shape[-1])
    rows_in = lax.all_gather(rows_in, "sub", axis=1, tiled=True)
    projected_pair = jnp.einsum(
        "rd,fd->rf", rows_in, pair_weights, preferred_element_type=jnp.float32
    )
    activation = (
        jax.nn.silu(projected_pair[:, :hidden_units]) * projected_pair[:, hidden_units:]
    ).astype(jnp.bfloat16)
    partial_out = jnp.dot(activation, w_down[0], preferred_element_type=jnp.float32)
    expert_out = lax.psum_scatter(
        partial_out.astype(jnp.bfloat16), "sub", scatter_dimension=1, tiled=True
    )
    results = expert_out.reshape(lead_shape + (expert_out.shape[1],))
    returned = lax.all_to_all(results, ("ep", "hd"), split_axis=0, concat_axis=0, tiled=True)
    mixture = jnp.dot(
        gate_table,
        returned.reshape(all_experts * expert_slots, half_width),
        preferred_element_type=jnp.float32,
    )
    return (widened + mixture).astype(jnp.bfloat16)


def shards(
    queries,
    cache_keys,
    cache_values,
    page_len,
    new_keys,
    new_values,
    out_proj,
    residual,
    norm_gain,
    gate_up,
    w_down,
    expert_ids,
    gates,
):
    n_ep, n_hd, n_sub = lax.axis_size("ep"), lax.axis_size("hd"), lax.axis_size("sub")
    sub = lax.axis_index("sub")
    query_rows = queries.shape[0]
    heads_here = queries.shape[1] // HD
    kv_heads = max(1, heads_here // (QH // KVH))
    rows = query_rows // (n_hd * n_sub)
    features = norm_gain.shape[0]
    cache_rows = cache_keys.shape[0]
    all_experts = n_ep * n_hd * gate_up.shape[0]
    dense = (
        expert_ids.shape[1] == all_experts
        and gate_up.shape[0] == 1
        and n_ep * n_hd % 2 == 0
        and rows % 32 == 0
    )

    packed = pack_keys(
        cache_keys, cache_values, new_keys, new_values, page_len, kv_heads, heads_here
    )
    query_blocks = queries.reshape(n_hd, n_sub, rows, heads_here * HD)
    stages = [(0, sub_copies(packed))]
    travelling = packed
    for hop in range(1, n_ep):
        travelling = lax.ppermute(travelling, "ep", cycle(n_ep))
        stages.append((hop, sub_copies(travelling)))
    projections = sub_copies(out_proj)
    residual_parts = sub_exchange(residual, 0)
    if dense:
        gate_up_parts = sub_copies(gate_up[0])
        w_down_parts = sub_copies(w_down[0])
    state = None
    for index, stage in enumerate(stages):
        state = attend(
            query_blocks, [stage], state, cache_rows, kv_heads, index == len(stages) - 1
        )
    attended = state

    def project(x):
        return jnp.concatenate(
            [jnp.dot(x, w, preferred_element_type=jnp.float32) for w in projections], axis=1
        )

    if n_hd == 2:
        came = lax.ppermute(
            project(attended[rows:]).astype(jnp.bfloat16), "hd", cycle(n_hd)
        )
        projected = project(attended[:rows]) + came.astype(jnp.float32)
    else:
        projected = lax.psum_scatter(
            project(attended).astype(jnp.bfloat16), "hd", scatter_dimension=0, tiled=True
        ).astype(jnp.float32)
    residual_rows = jnp.concatenate(residual_parts, axis=1).astype(jnp.float32)
    hidden = (residual_rows + projected).astype(jnp.bfloat16)
    hidden = jnp.concatenate(by_sub(jnp.split(hidden, n_sub, axis=1)), axis=1)
    widened = hidden.astype(jnp.float32)
    square_sum = jnp.sum(widened * widened, axis=1, keepdims=True)
    normed = (
        widened * lax.rsqrt(square_sum / features + EPSILON) * norm_gain.astype(jnp.float32)
    ).astype(jnp.bfloat16)

    if not dense:
        own_columns = [
            jnp.concatenate(by_sub(sub_exchange(x, 1)), axis=0) for x in (hidden, normed)
        ]
        return sparse_experts(
            own_columns[0].astype(jnp.float32),
            own_columns[1],
            gate_up,
            w_down,
            expert_ids,
            gates,
            features,
        )
    ids_here = lax.dynamic_slice_in_dim(expert_ids, sub * rows, rows, 0)
    gates_here = lax.dynamic_slice_in_dim(gates, sub * rows, rows, 0).astype(jnp.float32)
    gate_table = jnp.sum(
        jnp.where(
            ids_here[:, :, None] == jnp.arange(LANES, dtype=jnp.int32)[None, None, :],
            gates_here[:, :, None],
            0.0,
        ),
        axis=1,
    ).astype(jnp.bfloat16)
    mixture = dense_experts(normed, gate_table, gate_up_parts, w_down_parts)
    layer_rows = (widened + mixture).astype(jnp.bfloat16)
    return jnp.concatenate(by_sub(sub_exchange(layer_rows, 1)), axis=0)


def solution(mesh):
    return jax.shard_map(
        shards,
        mesh=mesh,
        in_specs=(
            P(("grp", "ep"), "hd"),
            P(("grp", "ep", "sub"), None),
            P(("grp", "ep", "sub"), None),
            P(("grp", "ep", "sub")),
            P(("grp", "ep", "sub"), None),
            P(("grp", "ep", "sub"), None),
            P("hd", "sub"),
            P(("grp", "ep", "hd"), "sub"),
            P(),
            P(("ep", "hd"), None, "sub", None),
            P(("ep", "hd"), "sub", None),
            P(("grp", "ep", "hd"), None),
            P(("grp", "ep", "hd"), None),
        ),
        out_specs=P(("grp", "ep", "hd"), "sub"),
        check_vma=False,
    )
```

```python
import functools
import math

import jax
import jax.numpy as jnp
from jax import lax
from jax.experimental import pallas as pl
from jax.experimental.pallas import tpu as pltpu
from jax.sharding import PartitionSpec as P

QH = 32
KVH = 4
HD = 128
GROUPS_ROW = 4
NEG_FILL = -1e30
EPSILON = 1e-06
MASK_ROWS = 16
LANES = 128
MIB = 1024 * 1024
CONTRACT_LAST = (((1,), (1,)), ((), ()))


def block_sizes(block_rows, group_total, experts_group):
    group_slots = min(block_rows, 3 * GROUPS_ROW * block_rows // (2 * group_total))
    return (group_slots, 2 * group_slots // experts_group)


def cycle(size, step=1):
    return [(i, (i + step) % size) for i in range(size)]


def sub_copies(x):
    size = lax.axis_size("sub")
    return [x] + [lax.ppermute(x, "sub", cycle(size, step)) for step in range(1, size)]


def by_sub(copies):
    size = len(copies)
    me = lax.axis_index("sub")
    ordered = []
    for target in range(size):
        value = copies[0]
        for step in range(1, size):
            value = jnp.where((me - step) % size == target, copies[step], value)
        ordered.append(value)
    return ordered


def sub_exchange(x, axis):
    size = lax.axis_size("sub")
    me = lax.axis_index("sub")
    length = x.shape[axis] // size

    def part(index):
        return lax.dynamic_slice_in_dim(x, index * length, length, axis)

    came = [part(me)]
    for step in range(1, size):
        came.append(lax.ppermute(part((me + step) % size), "sub", cycle(size, step)))
    return came


def pack_keys(cache_keys, cache_values, new_keys, new_values, page_len, kv_heads, heads_here):
    cache_rows, new_rows = cache_keys.shape[0], new_keys.shape[0]
    group_width = QH // KVH
    rows = cache_rows + new_rows + MASK_ROWS

    def kernel(page_ref, ck_ref, cv_ref, nk_ref, nv_ref, *out_refs):
        first = lax.axis_index("hd") * heads_here // group_width
        lane = lax.broadcasted_iota(jnp.int32, (MASK_ROWS, 2 * HD), 1)
        bias = jnp.where(lane < page_ref[0], 0.0, NEG_FILL).astype(jnp.bfloat16)
        for kv, out_ref in enumerate(out_refs):
            columns = pl.ds(pl.multiple_of((first + kv) * HD, HD), HD)
            out_ref[:cache_rows, :HD] = ck_ref[:, columns]
            out_ref[:cache_rows, HD:] = cv_ref[:, columns]
            out_ref[cache_rows : cache_rows + new_rows, :HD] = nk_ref[:, columns]
            out_ref[cache_rows : cache_rows + new_rows, HD:] = nv_ref[:, columns]
            out_ref[cache_rows + new_rows :, :] = bias

    vmem = pl.BlockSpec(memory_space=pltpu.VMEM)
    return pl.pallas_call(
        kernel,
        out_shape=[jax.ShapeDtypeStruct((rows, 2 * HD), cache_keys.dtype)] * kv_heads,
        in_specs=[pl.BlockSpec(memory_space=pltpu.SMEM)] + [vmem] * 4,
        out_specs=[vmem] * kv_heads,
        name="pack_keys",
    )(page_len, cache_keys, cache_values, new_keys, new_values)


def attend(queries, kv, hop, blocks, state, cache_rows, kv_heads, finish=None):
    n_hd, n_sub, rows, columns = queries.shape
    per_kv = columns // HD // kv_heads
    stack = 2 if per_kv % 2 == 0 else 1
    all_rows = n_hd * rows
    part = stack * all_rows
    new_rows = blocks[0].shape[0] - cache_rows - MASK_ROWS
    keys = cache_rows + new_rows
    factor = math.log2(math.e) / math.sqrt(HD)
    relative = n_hd == 2
    last = finish is not None
    weights, earlier = finish if last else ([], None)
    head_columns = per_kv * HD
    final = last and kv == kv_heads - 1
    kept_rows = rows if relative else 0

    def kernel(*refs):
        q_ref, refs = refs[0], refs[1:]
        block_refs, refs = refs[: len(blocks)], refs[len(blocks) :]
        if state is not None:
            (m_in, acc_in), refs = refs[:2], refs[2:]
        weight_refs, refs = refs[: len(weights)], refs[len(weights) :]
        if earlier is not None:
            earlier_ref, refs = refs[0], refs[1:]
        if last:
            results = 1 + (kept_rows > 0 and final)
            result_refs, refs = refs[:results], refs[results:]
            head_ref, refs = refs[0], refs[1:]
            held_refs, sems = refs[: len(weights)], refs[len(weights)]
            copies = [
                pltpu.make_async_copy(
                    w.at[pl.ds(kv * head_columns, head_columns), :], held, sems.at[i]
                )
                for i, (w, held) in enumerate(zip(weight_refs, held_refs))
            ]
            for copy in copies:
                copy.start()
        else:
            m_out, acc_out = refs
        sub = lax.axis_index("sub")
        ep = lax.axis_index("ep")
        hd = lax.axis_index("hd")
        places = [(hd + j) % n_hd if relative else j for j in range(n_hd)]
        biases = []
        for step, block in enumerate(block_refs):
            cache_bias = block[keys : keys + 1, :cache_rows].astype(jnp.float32)
            if hop == 0:
                key_id = ((sub - step) % n_sub) * new_rows + lax.broadcasted_iota(
                    jnp.int32, (rows, new_rows), 1
                )
                row_id = lax.broadcasted_iota(jnp.int32, (rows, new_rows), 0)
                seen = [
                    jnp.where(
                        key_id <= row_id + (place * n_sub + sub) * rows, 0.0, NEG_FILL
                    )
                    for place in places
                ]
                new_bias = jnp.concatenate(seen * stack, axis=0)
                cache_bias = jnp.broadcast_to(cache_bias, (part, cache_rows))
            else:
                new_bias = jnp.full(
                    (1, new_rows), jnp.where(ep >= hop, 0.0, NEG_FILL), jnp.float32
                )
            biases.append(jnp.concatenate([cache_bias, new_bias], axis=1))
        ones = jnp.ones((keys, HD), jnp.bfloat16)
        key_parts = [block[:keys, :HD] for block in block_refs]
        value_parts = [
            jnp.concatenate([block[:keys, HD:], ones], axis=1) for block in block_refs
        ]
        for index in range(per_kv // stack):
            here = slice(index * part, (index + 1) * part)
            heads = range(kv * per_kv + index * stack, kv * per_kv + (index + 1) * stack)
            q = jnp.concatenate(
                [q_ref[p, sub, :, h * HD : (h + 1) * HD] for h in heads for p in places], axis=0
            )
            terms = [
                lax.dot_general(q, k, CONTRACT_LAST, preferred_element_type=jnp.float32) * factor
                + bias
                for k, bias in zip(key_parts, biases)
            ]
            top = jnp.max(functools.reduce(jnp.maximum, terms), axis=1, keepdims=True)
            top = jnp.broadcast_to(top, (part, LANES))
            if state is not None:
                top_in = m_in[here, :]
                top = jnp.maximum(top, top_in)
            wide_top = jnp.concatenate([top] * (keys // LANES), axis=1)
            acc = None
            for term, v in zip(terms, value_parts):
                exp_terms = jnp.exp2(term - wide_top).astype(jnp.bfloat16)
                product = jnp.dot(exp_terms, v, preferred_element_type=jnp.float32)
                acc = product if acc is None else acc + product
            if state is not None:
                scale = jnp.exp2(top_in - top)
                acc = acc + jnp.concatenate([scale, scale], axis=1) * acc_in[here, :]
            if last:
                out = (acc[:, :HD] / acc[:, HD:]).astype(jnp.bfloat16)
                for s in range(stack):
                    first = (index * stack + s) * HD
                    head_ref[:, first : first + HD] = out[s * all_rows : (s + 1) * all_rows]
            else:
                m_out[here, :] = top
                acc_out[here, :] = acc
        if last:
            for copy in copies:
                copy.wait()
            source = head_ref[...]
            width = held_refs[0].shape[1]
            for i, held in enumerate(held_refs):
                here = slice(i * width, (i + 1) * width)
                product = jnp.dot(source, held[...], preferred_element_type=jnp.float32)
                if earlier is not None:
                    product = product + earlier_ref[:, here]
                if final:
                    result_refs[-1][:, here] = product[kept_rows:].astype(jnp.bfloat16)
                    if kept_rows:
                        result_refs[0][:, here] = product[:kept_rows]
                else:
                    result_refs[0][:, here] = product

    vmem = pl.BlockSpec(memory_space=pltpu.VMEM)
    anywhere = pl.BlockSpec(memory_space=pl.ANY)
    scratch = []
    if last:
        features = sum(w.shape[1] for w in weights)
        if final:
            out_shape = (
                jax.ShapeDtypeStruct((kept_rows, features), jnp.float32),
                jax.ShapeDtypeStruct((all_rows - kept_rows, features), jnp.bfloat16),
            )[0 if kept_rows else 1 :]
        else:
            out_shape = (jax.ShapeDtypeStruct((all_rows, features), jnp.float32),)
        scratch = [pltpu.VMEM((all_rows, head_columns), jnp.bfloat16)]
        scratch += [pltpu.VMEM((head_columns, w.shape[1]), w.dtype) for w in weights]
        scratch += [pltpu.SemaphoreType.DMA((len(weights),))]
    else:
        out_shape = (
            jax.ShapeDtypeStruct((per_kv * all_rows, LANES), jnp.float32),
            jax.ShapeDtypeStruct((per_kv * all_rows, 2 * HD), jnp.float32),
        )
    operands = [queries] + list(blocks) + (list(state) if state is not None else [])
    in_specs = [vmem] * len(operands) + [anywhere] * len(weights)
    operands += list(weights)
    if earlier is not None:
        operands.append(earlier)
        in_specs.append(vmem)
    scores = all_rows * per_kv * keys * len(blocks)
    return pl.pallas_call(
        kernel,
        out_shape=out_shape,
        in_specs=in_specs,
        out_specs=tuple(vmem for _ in out_shape),
        scratch_shapes=scratch,
        compiler_params=pltpu.CompilerParams(vmem_limit_bytes=16 * MIB),
        cost_estimate=pl.CostEstimate(
            flops=6 * scores * HD, bytes_accessed=4 * MIB, transcendentals=scores
        ),
        name="attend",
    )(*operands)


def apply_expert(inputs, gate_up, w_down):
    features = w_down[0].shape[1]
    hidden = w_down[0].shape[0]
    rows = sum(x.shape[0] for x in inputs)

    def kernel(*refs):
        x_refs, refs = refs[: len(inputs)], refs[len(inputs) :]
        gu_refs, refs = refs[: len(gate_up)], refs[len(gate_up) :]
        down_refs, (out_ref,) = refs[: len(w_down)], refs[len(w_down) :]
        mine = lax.axis_index("ep") * lax.axis_size("hd") + lax.axis_index("hd")
        joined = jnp.concatenate([x[...] for x in x_refs], axis=0)
        x = joined[:, :features]
        table = joined[:, features:].astype(jnp.float32)
        lane = lax.broadcasted_iota(jnp.int32, table.shape, 1)
        gate = jnp.sum(jnp.where(lane == mine, table, 0.0), axis=1, keepdims=True)
        total = None
        for gu, down in zip(gu_refs, down_refs):
            gate_part = lax.dot_general(
                x, gu[0], CONTRACT_LAST, preferred_element_type=jnp.float32
            )
            up_part = lax.dot_general(x, gu[1], CONTRACT_LAST, preferred_element_type=jnp.float32)
            activation = (gate_part / (1.0 + jnp.exp(-gate_part)) * up_part).astype(jnp.bfloat16)
            product = jnp.dot(activation, down[...], preferred_element_type=jnp.float32)
            total = product if total is None else total + product
        out_ref[...] = gate * total.astype(jnp.bfloat16).astype(jnp.float32)

    vmem = pl.BlockSpec(memory_space=pltpu.VMEM)
    operands = list(inputs) + list(gate_up) + list(w_down)
    return pl.pallas_call(
        kernel,
        out_shape=jax.ShapeDtypeStruct((rows, features), jnp.float32),
        in_specs=[vmem] * len(operands),
        out_specs=vmem,
        compiler_params=pltpu.CompilerParams(vmem_limit_bytes=16 * MIB),
        cost_estimate=pl.CostEstimate(
            flops=6 * rows * hidden * len(w_down) * features,
            bytes_accessed=6 * MIB,
            transcendentals=rows * hidden * len(w_down),
        ),
        name="apply_expert",
    )(*operands)


def chip_ring(n_ep, n_hd):
    if n_hd == 2:
        return [z * 2 for z in range(n_ep)] + [z * 2 + 1 for z in reversed(range(n_ep))]
    return list(range(n_ep * n_hd))


def dense_experts(normed, gate_table, gate_up, w_down):
    axes = ("ep", "hd")
    walk = chip_ring(lax.axis_size("ep"), lax.axis_size("hd"))
    size = len(walk)
    ahead = [(walk[i], walk[(i + 1) % size]) for i in range(size)]
    back = [(b, a) for a, b in ahead]
    rows, features = normed.shape
    half = rows // 2
    reach = size // 2
    own = jnp.concatenate([normed, gate_table], axis=1)
    behind, before, waiting = own, own, [own]
    outs = []
    for hop in range(1, reach + 1):
        if hop == reach:
            behind, before = behind[:half], before[half:]
        behind = lax.ppermute(behind, axes, ahead)
        before = lax.ppermute(before, axes, back)
        out = apply_expert(waiting, gate_up, w_down)
        behind, before, out = lax.optimization_barrier((behind, before, out))
        outs.append(out)
        waiting = [behind, before]
    outs.append(apply_expert(waiting, gate_up, w_down))
    mine = outs[0]
    outs = [(x[: x.shape[0] // 2], x[x.shape[0] // 2 :]) for x in outs[1:]]
    to_back, to_ahead = outs[-1]
    for hop in range(reach - 1, -1, -1):
        to_back = lax.ppermute(to_back.astype(jnp.bfloat16), axes, back).astype(jnp.float32)
        to_ahead = lax.ppermute(to_ahead.astype(jnp.bfloat16), axes, ahead).astype(jnp.float32)
        if hop == reach - 1:
            empty = jnp.zeros((rows - half, features), jnp.float32)
            to_back = jnp.concatenate([to_back, empty], axis=0)
            to_ahead = jnp.concatenate([empty, to_ahead], axis=0)
        if hop > 0:
            to_back = to_back + outs[hop - 1][0]
            to_ahead = to_ahead + outs[hop - 1][1]
    return mine + to_back + to_ahead


def sparse_experts(widened, normed, gate_up, w_down, expert_ids, gates, features):
    half_width = normed.shape[1]
    pair_weights = gate_up[0].reshape(-1, features)
    hidden_units = w_down.shape[1]
    group_total = lax.axis_size("ep")
    group_experts = lax.axis_size("hd")
    all_experts = group_total * group_experts
    block_rows = expert_ids.shape[0]
    group_slots, expert_slots = block_sizes(block_rows, group_total, group_experts)
    chosen = (
        expert_ids[:, :, None] == jnp.arange(all_experts, dtype=jnp.int32)[None, None, :]
    ).astype(jnp.int32)
    named_count = jnp.sum(chosen, axis=1)
    earlier = jnp.cumsum(named_count, axis=0) - named_count
    slot_index = jnp.sum(chosen * earlier[:, None, :], axis=2)
    position = expert_ids * expert_slots + slot_index
    slot_columns = jnp.arange(all_experts * expert_slots, dtype=jnp.int32)
    gate_table = jnp.sum(
        jnp.where(
            position[:, :, None] == slot_columns[None, None, :],
            gates.astype(jnp.float32)[:, :, None],
            0.0,
        ),
        axis=1,
    ).astype(jnp.bfloat16)
    placed = (gate_table != 0).astype(jnp.bfloat16)
    outgoing = jnp.einsum("rq,rd->qd", placed, normed, preferred_element_type=jnp.float32).astype(
        jnp.bfloat16
    )
    outgoing = outgoing.reshape(all_experts, expert_slots, normed.shape[1])
    arrived = lax.all_to_all(outgoing, ("ep", "hd"), split_axis=0, concat_axis=0, tiled=True)
    lead_shape = arrived.shape[:-1]
    rows_in = arrived.reshape(-1, arrived.shape[-1])
    rows_in = lax.all_gather(rows_in, "sub", axis=1, tiled=True)
    projected_pair = jnp.einsum(
        "rd,fd->rf", rows_in, pair_weights, preferred_element_type=jnp.float32
    )
    activation = (
        jax.nn.silu(projected_pair[:, :hidden_units]) * projected_pair[:, hidden_units:]
    ).astype(jnp.bfloat16)
    partial_out = jnp.dot(activation, w_down[0], preferred_element_type=jnp.float32)
    expert_out = lax.psum_scatter(
        partial_out.astype(jnp.bfloat16), "sub", scatter_dimension=1, tiled=True
    )
    results = expert_out.reshape(lead_shape + (expert_out.shape[1],))
    returned = lax.all_to_all(results, ("ep", "hd"), split_axis=0, concat_axis=0, tiled=True)
    mixture = jnp.dot(
        gate_table,
        returned.reshape(all_experts * expert_slots, half_width),
        preferred_element_type=jnp.float32,
    )
    return (widened + mixture).astype(jnp.bfloat16)


def shards(
    queries,
    cache_keys,
    cache_values,
    page_len,
    new_keys,
    new_values,
    out_proj,
    residual,
    norm_gain,
    gate_up,
    w_down,
    expert_ids,
    gates,
):
    n_ep, n_hd, n_sub = lax.axis_size("ep"), lax.axis_size("hd"), lax.axis_size("sub")
    sub = lax.axis_index("sub")
    query_rows = queries.shape[0]
    heads_here = queries.shape[1] // HD
    kv_heads = max(1, heads_here // (QH // KVH))
    rows = query_rows // (n_hd * n_sub)
    features = norm_gain.shape[0]
    cache_rows = cache_keys.shape[0]
    all_experts = n_ep * n_hd * gate_up.shape[0]
    dense = (
        expert_ids.shape[1] == all_experts
        and gate_up.shape[0] == 1
        and n_ep * n_hd % 2 == 0
        and rows % 32 == 0
    )

    packed = pack_keys(
        cache_keys, cache_values, new_keys, new_values, page_len, kv_heads, heads_here
    )
    query_blocks = queries.reshape(n_hd, n_sub, rows, heads_here * HD)
    projections = sub_copies(out_proj)
    residual_parts = sub_exchange(residual, 0)
    if dense:
        gate_up_parts = sub_copies(gate_up[0])
        w_down_parts = sub_copies(w_down[0])
    travelling = list(packed)
    states = [None] * kv_heads
    earlier = None
    for hop in range(n_ep):
        blocks = [sub_copies(x) for x in travelling]
        onward = [lax.ppermute(x, "ep", cycle(n_ep)) for x in travelling] if hop < n_ep - 1 else []
        for kv in range(kv_heads):
            finish = (projections, earlier) if hop == n_ep - 1 else None
            states[kv] = attend(
                query_blocks, kv, hop, blocks[kv], states[kv], cache_rows, kv_heads, finish
            )
            if finish:
                earlier = states[kv][0]
            else:
                onward[kv], states[kv] = lax.optimization_barrier((onward[kv], states[kv]))
        travelling = onward
    sent = states[-1][-1]
    if n_hd == 2:
        came = lax.ppermute(sent, "hd", cycle(n_hd))
        projected = earlier + came.astype(jnp.float32)
    else:
        projected = lax.psum_scatter(sent, "hd", scatter_dimension=0, tiled=True).astype(
            jnp.float32
        )
    residual_rows = jnp.concatenate(residual_parts, axis=1).astype(jnp.float32)
    hidden = (residual_rows + projected).astype(jnp.bfloat16)
    hidden = jnp.concatenate(by_sub(jnp.split(hidden, n_sub, axis=1)), axis=1)
    widened = hidden.astype(jnp.float32)
    square_sum = jnp.sum(widened * widened, axis=1, keepdims=True)
    normed = (
        widened * lax.rsqrt(square_sum / features + EPSILON) * norm_gain.astype(jnp.float32)
    ).astype(jnp.bfloat16)

    if not dense:
        own_columns = [
            jnp.concatenate(by_sub(sub_exchange(x, 1)), axis=0) for x in (hidden, normed)
        ]
        return sparse_experts(
            own_columns[0].astype(jnp.float32),
            own_columns[1],
            gate_up,
            w_down,
            expert_ids,
            gates,
            features,
        )
    ids_here = lax.dynamic_slice_in_dim(expert_ids, sub * rows, rows, 0)
    gates_here = lax.dynamic_slice_in_dim(gates, sub * rows, rows, 0).astype(jnp.float32)
    gate_table = jnp.sum(
        jnp.where(
            ids_here[:, :, None] == jnp.arange(LANES, dtype=jnp.int32)[None, None, :],
            gates_here[:, :, None],
            0.0,
        ),
        axis=1,
    ).astype(jnp.bfloat16)
    mixture = dense_experts(normed, gate_table, gate_up_parts, w_down_parts)
    layer_rows = (widened + mixture).astype(jnp.bfloat16)
    return jnp.concatenate(by_sub(sub_exchange(layer_rows, 1)), axis=0)


def solution(mesh):
    return jax.shard_map(
        shards,
        mesh=mesh,
        in_specs=(
            P(("grp", "ep"), "hd"),
            P(("grp", "ep", "sub"), None),
            P(("grp", "ep", "sub"), None),
            P(("grp", "ep", "sub")),
            P(("grp", "ep", "sub"), None),
            P(("grp", "ep", "sub"), None),
            P("hd", "sub"),
            P(("grp", "ep", "hd"), "sub"),
            P(),
            P(("ep", "hd"), None, "sub", None),
            P(("ep", "hd"), "sub", None),
            P(("grp", "ep", "hd"), None),
            P(("grp", "ep", "hd"), None),
        ),
        out_specs=P(("grp", "ep", "hd"), "sub"),
        check_vma=False,
    )
```

```python
import functools
import math

import jax
import jax.numpy as jnp
from jax import lax
from jax.experimental import pallas as pl
from jax.experimental.pallas import tpu as pltpu
from jax.sharding import PartitionSpec as P

QH = 32
KVH = 4
HD = 128
GROUPS_ROW = 4
NEG_FILL = -1e30
EPSILON = 1e-06
MASK_ROWS = 16
LANES = 128
MIB = 1024 * 1024
CONTRACT_LAST = (((1,), (1,)), ((), ()))


def block_sizes(block_rows, group_total, experts_group):
    group_slots = min(block_rows, 3 * GROUPS_ROW * block_rows // (2 * group_total))
    return (group_slots, 2 * group_slots // experts_group)


def cycle(size, step=1):
    return [(i, (i + step) % size) for i in range(size)]


def sub_copies(x):
    size = lax.axis_size("sub")
    return [x] + [lax.ppermute(x, "sub", cycle(size, step)) for step in range(1, size)]


def by_sub(copies):
    size = len(copies)
    me = lax.axis_index("sub")
    ordered = []
    for target in range(size):
        value = copies[0]
        for step in range(1, size):
            value = jnp.where((me - step) % size == target, copies[step], value)
        ordered.append(value)
    return ordered


def sub_exchange(x, axis):
    size = lax.axis_size("sub")
    me = lax.axis_index("sub")
    length = x.shape[axis] // size

    def part(index):
        return lax.dynamic_slice_in_dim(x, index * length, length, axis)

    came = [part(me)]
    for step in range(1, size):
        came.append(lax.ppermute(part((me + step) % size), "sub", cycle(size, step)))
    return came


def pack_keys(cache_keys, cache_values, new_keys, new_values, page_len, kv_heads, heads_here):
    cache_rows, new_rows = cache_keys.shape[0], new_keys.shape[0]
    group_width = QH // KVH
    rows = cache_rows + new_rows + MASK_ROWS

    def kernel(page_ref, ck_ref, cv_ref, nk_ref, nv_ref, *refs):
        out_refs, (mask_ref, sems) = refs[:kv_heads], refs[kv_heads:]
        first = lax.axis_index("hd") * heads_here // group_width
        copies = []
        for kv, out_ref in enumerate(out_refs):
            columns = pl.ds(pl.multiple_of((first + kv) * HD, HD), HD)
            cached, new = pl.ds(0, cache_rows), pl.ds(cache_rows, new_rows)
            for i, (ref, here, lanes) in enumerate(
                [(ck_ref, cached, 0), (cv_ref, cached, HD), (nk_ref, new, 0), (nv_ref, new, HD)]
            ):
                copies.append(
                    pltpu.make_async_copy(
                        ref.at[:, columns], out_ref.at[here, pl.ds(lanes, HD)], sems.at[kv, i]
                    )
                )
                copies[-1].start()
        lane = lax.broadcasted_iota(jnp.int32, (MASK_ROWS, 2 * HD), 1)
        mask_ref[...] = jnp.where(lane < page_ref[0], 0.0, NEG_FILL).astype(jnp.bfloat16)
        for kv, out_ref in enumerate(out_refs):
            copies.append(
                pltpu.make_async_copy(
                    mask_ref, out_ref.at[pl.ds(cache_rows + new_rows, MASK_ROWS), :], sems.at[kv, 4]
                )
            )
            copies[-1].start()
        for copy in copies:
            copy.wait()

    anywhere = pl.BlockSpec(memory_space=pl.ANY)
    return pl.pallas_call(
        kernel,
        out_shape=[jax.ShapeDtypeStruct((rows, 2 * HD), cache_keys.dtype)] * kv_heads,
        in_specs=[pl.BlockSpec(memory_space=pltpu.SMEM)] + [anywhere] * 4,
        out_specs=[anywhere] * kv_heads,
        scratch_shapes=[
            pltpu.VMEM((MASK_ROWS, 2 * HD), jnp.bfloat16),
            pltpu.SemaphoreType.DMA((kv_heads, 5)),
        ],
        compiler_params=pltpu.CompilerParams(vmem_limit_bytes=4 * MIB),
        name="pack_keys",
    )(page_len, cache_keys, cache_values, new_keys, new_values)


def small_kernel(kernel, out_shape, operands, name):
    vmem = pl.BlockSpec(memory_space=pltpu.VMEM)
    return pl.pallas_call(
        kernel,
        out_shape=out_shape,
        in_specs=[vmem] * len(operands),
        out_specs=[vmem] * len(out_shape),
        compiler_params=pltpu.CompilerParams(vmem_limit_bytes=8 * MIB),
        cost_estimate=pl.CostEstimate(flops=MIB, bytes_accessed=MIB, transcendentals=0),
        name=name,
    )(*operands)


def hand_over(parts):
    size = len(parts)
    return [parts[0]] + [
        lax.ppermute(part, "sub", cycle(size, step)) for step, part in enumerate(parts) if step
    ]


def split_rows(residual, n_sub):
    rows, columns = residual.shape[0] // n_sub, residual.shape[1]

    def kernel(in_ref, *out_refs):
        sub = lax.axis_index("sub")
        for step, out_ref in enumerate(out_refs):
            first = pl.multiple_of((sub + step) % n_sub * rows, rows)
            out_ref[...] = in_ref[pl.ds(first, rows), :]

    shape = jax.ShapeDtypeStruct((rows, columns), residual.dtype)
    return small_kernel(kernel, [shape] * n_sub, [residual], "split_rows")


def gates_by_expert(expert_ids, gates, rows):
    choices, block_rows = expert_ids.shape[1], expert_ids.shape[0]

    def kernel(ids_ref, gates_ref, out_ref):
        sub = lax.axis_index("sub")
        expert = lax.broadcasted_iota(jnp.int32, (LANES, block_rows), 0)
        weights = gates_ref[...].astype(jnp.float32)
        ids = ids_ref[...]
        table = jnp.zeros((LANES, block_rows), jnp.float32)
        for k in range(choices):
            table = table + jnp.where(ids[k : k + 1, :] == expert, weights[k : k + 1, :], 0.0)
        table = table.T
        chosen = table[:rows]
        for place in range(1, block_rows // rows):
            chosen = jnp.where(sub == place, table[place * rows : (place + 1) * rows], chosen)
        out_ref[...] = chosen.astype(jnp.bfloat16)

    shape = jax.ShapeDtypeStruct((rows, LANES), jnp.bfloat16)
    return small_kernel(kernel, [shape], [expert_ids.T, gates.T], "gates_by_expert")[0]


def normalise(kept, came, residual_parts, gain, gate_table):
    n_sub = len(residual_parts)
    rows, width = residual_parts[0].shape
    features = n_sub * width
    extra = 0 if gate_table is None else LANES

    def kernel(*refs):
        refs = list(refs)
        kept_ref = refs.pop(0) if kept is not None else None
        came_ref = refs.pop(0)
        part_refs = [refs.pop(0) for _ in residual_parts]
        gain_ref = refs.pop(0)
        if extra:
            gate_ref = refs.pop(0)
        hidden_ref, normed_ref = refs
        sub = lax.axis_index("sub")
        hidden, places, squares = [], [], 0.0
        for step, part_ref in enumerate(part_refs):
            here = slice(step * width, (step + 1) * width)
            projected = came_ref[:, here].astype(jnp.float32)
            if kept is not None:
                projected = kept_ref[:, here] + projected
            value = (part_ref[...].astype(jnp.float32) + projected).astype(jnp.bfloat16)
            hidden.append(value)
            place = pl.ds(pl.multiple_of((sub - step) % n_sub * width, width), width)
            places.append(place)
            hidden_ref[:, place] = value
            wide = value.astype(jnp.float32)
            squares = squares + jnp.sum(wide * wide, axis=1, keepdims=True)
        scale = lax.rsqrt(squares / features + EPSILON)
        for value, place in zip(hidden, places):
            normed = value.astype(jnp.float32) * scale * gain_ref[:, place].astype(jnp.float32)
            normed_ref[:, place] = normed.astype(jnp.bfloat16)
        if extra:
            normed_ref[:, features:] = gate_ref[...]

    operands = ([kept] if kept is not None else []) + [came] + list(residual_parts)
    operands.append(gain.reshape(1, features))
    if extra:
        operands.append(gate_table)
    out_shape = [
        jax.ShapeDtypeStruct((rows, features), jnp.bfloat16),
        jax.ShapeDtypeStruct((rows, features + extra), jnp.bfloat16),
    ]
    return small_kernel(kernel, out_shape, operands, "normalise")


def add_up(hidden, mine, to_back, to_ahead, n_sub):
    rows, features = hidden.shape
    width = features // n_sub

    def kernel(hidden_ref, mine_ref, back_ref, ahead_ref, *out_refs):
        sub = lax.axis_index("sub")
        for step, out_ref in enumerate(out_refs):
            place = pl.ds(pl.multiple_of((sub + step) % n_sub * width, width), width)
            mixture = mine_ref[:, place] + back_ref[:, place].astype(jnp.float32)
            mixture = mixture + ahead_ref[:, place].astype(jnp.float32)
            total = hidden_ref[:, place].astype(jnp.float32) + mixture
            out_ref[...] = total.astype(jnp.bfloat16)

    shape = jax.ShapeDtypeStruct((rows, width), jnp.bfloat16)
    return small_kernel(kernel, [shape] * n_sub, [hidden, mine, to_back, to_ahead], "add_up")


def stack_rows(parts):
    n_sub = len(parts)
    rows, width = parts[0].shape

    def kernel(*refs):
        sub = lax.axis_index("sub")
        for step, part_ref in enumerate(refs[:-1]):
            first = pl.multiple_of((sub - step) % n_sub * rows, rows)
            refs[-1][pl.ds(first, rows), :] = part_ref[...]

    shape = jax.ShapeDtypeStruct((n_sub * rows, width), parts[0].dtype)
    return small_kernel(kernel, [shape], parts, "stack_rows")[0]


def attend(queries, kv, hop, blocks, state, cache_rows, kv_heads, finish=None):
    n_hd, n_sub, rows, columns = queries.shape
    per_kv = columns // HD // kv_heads
    stack = 2 if per_kv % 2 == 0 else 1
    all_rows = n_hd * rows
    part = stack * all_rows
    new_rows = blocks[0].shape[0] - cache_rows - MASK_ROWS
    keys = cache_rows + new_rows
    factor = math.log2(math.e) / math.sqrt(HD)
    relative = n_hd == 2
    last = finish is not None
    weights, earlier = finish if last else ([], None)
    head_columns = per_kv * HD
    final = last and kv == kv_heads - 1
    kept_rows = rows if relative else 0

    def kernel(*refs):
        q_ref, refs = refs[0], refs[1:]
        block_refs, refs = refs[: len(blocks)], refs[len(blocks) :]
        if state is not None:
            (m_in, acc_in), refs = refs[:2], refs[2:]
        weight_refs, refs = refs[: len(weights)], refs[len(weights) :]
        if earlier is not None:
            earlier_ref, refs = refs[0], refs[1:]
        if last:
            results = 1 + (kept_rows > 0 and final)
            result_refs, refs = refs[:results], refs[results:]
            head_ref, refs = refs[0], refs[1:]
            held_refs, sems = refs[: len(weights)], refs[len(weights)]
            copies = [
                pltpu.make_async_copy(
                    w.at[pl.ds(kv * head_columns, head_columns), :], held, sems.at[i]
                )
                for i, (w, held) in enumerate(zip(weight_refs, held_refs))
            ]
            for copy in copies:
                copy.start()
        else:
            m_out, acc_out = refs
        sub = lax.axis_index("sub")
        ep = lax.axis_index("ep")
        hd = lax.axis_index("hd")
        places = [(hd + j) % n_hd if relative else j for j in range(n_hd)]
        biases = []
        for step, block in enumerate(block_refs):
            cache_bias = block[keys : keys + 1, :cache_rows].astype(jnp.float32)
            if hop == 0:
                key_id = ((sub - step) % n_sub) * new_rows + lax.broadcasted_iota(
                    jnp.int32, (rows, new_rows), 1
                )
                row_id = lax.broadcasted_iota(jnp.int32, (rows, new_rows), 0)
                seen = [
                    jnp.where(
                        key_id <= row_id + (place * n_sub + sub) * rows, 0.0, NEG_FILL
                    )
                    for place in places
                ]
                new_bias = jnp.concatenate(seen * stack, axis=0)
                cache_bias = jnp.broadcast_to(cache_bias, (part, cache_rows))
            else:
                new_bias = jnp.full(
                    (1, new_rows), jnp.where(ep >= hop, 0.0, NEG_FILL), jnp.float32
                )
            biases.append(jnp.concatenate([cache_bias, new_bias], axis=1))
        ones = jnp.ones((keys, HD), jnp.bfloat16)
        key_parts = [block[:keys, :HD] for block in block_refs]
        value_parts = [
            jnp.concatenate([block[:keys, HD:], ones], axis=1) for block in block_refs
        ]
        for index in range(per_kv // stack):
            here = slice(index * part, (index + 1) * part)
            heads = range(kv * per_kv + index * stack, kv * per_kv + (index + 1) * stack)
            q = jnp.concatenate(
                [q_ref[p, sub, :, h * HD : (h + 1) * HD] for h in heads for p in places], axis=0
            )
            terms = [
                lax.dot_general(q, k, CONTRACT_LAST, preferred_element_type=jnp.float32) * factor
                + bias
                for k, bias in zip(key_parts, biases)
            ]
            top = jnp.max(functools.reduce(jnp.maximum, terms), axis=1, keepdims=True)
            top = jnp.broadcast_to(top, (part, LANES))
            if state is not None:
                top_in = m_in[here, :]
                top = jnp.maximum(top, top_in)
            wide_top = jnp.concatenate([top] * (keys // LANES), axis=1)
            acc = None
            for term, v in zip(terms, value_parts):
                exp_terms = jnp.exp2(term - wide_top).astype(jnp.bfloat16)
                product = jnp.dot(exp_terms, v, preferred_element_type=jnp.float32)
                acc = product if acc is None else acc + product
            if state is not None:
                scale = jnp.exp2(top_in - top)
                acc = acc + jnp.concatenate([scale, scale], axis=1) * acc_in[here, :]
            if last:
                out = (acc[:, :HD] / acc[:, HD:]).astype(jnp.bfloat16)
                for s in range(stack):
                    first = (index * stack + s) * HD
                    head_ref[:, first : first + HD] = out[s * all_rows : (s + 1) * all_rows]
            else:
                m_out[here, :] = top
                acc_out[here, :] = acc
        if last:
            for copy in copies:
                copy.wait()
            source = head_ref[...]
            width = held_refs[0].shape[1]
            for i, held in enumerate(held_refs):
                here = slice(i * width, (i + 1) * width)
                product = jnp.dot(source, held[...], preferred_element_type=jnp.float32)
                if earlier is not None:
                    product = product + earlier_ref[:, here]
                if final:
                    result_refs[-1][:, here] = product[kept_rows:].astype(jnp.bfloat16)
                    if kept_rows:
                        result_refs[0][:, here] = product[:kept_rows]
                else:
                    result_refs[0][:, here] = product

    vmem = pl.BlockSpec(memory_space=pltpu.VMEM)
    anywhere = pl.BlockSpec(memory_space=pl.ANY)
    scratch = []
    if last:
        features = sum(w.shape[1] for w in weights)
        if final:
            out_shape = (
                jax.ShapeDtypeStruct((kept_rows, features), jnp.float32),
                jax.ShapeDtypeStruct((all_rows - kept_rows, features), jnp.bfloat16),
            )[0 if kept_rows else 1 :]
        else:
            out_shape = (jax.ShapeDtypeStruct((all_rows, features), jnp.float32),)
        scratch = [pltpu.VMEM((all_rows, head_columns), jnp.bfloat16)]
        scratch += [pltpu.VMEM((head_columns, w.shape[1]), w.dtype) for w in weights]
        scratch += [pltpu.SemaphoreType.DMA((len(weights),))]
    else:
        out_shape = (
            jax.ShapeDtypeStruct((per_kv * all_rows, LANES), jnp.float32),
            jax.ShapeDtypeStruct((per_kv * all_rows, 2 * HD), jnp.float32),
        )
    operands = [queries] + list(blocks) + (list(state) if state is not None else [])
    in_specs = [vmem] * len(operands) + [anywhere] * len(weights)
    operands += list(weights)
    if earlier is not None:
        operands.append(earlier)
        in_specs.append(vmem)
    scores = all_rows * per_kv * keys * len(blocks)
    return pl.pallas_call(
        kernel,
        out_shape=out_shape,
        in_specs=in_specs,
        out_specs=tuple(vmem for _ in out_shape),
        scratch_shapes=scratch,
        compiler_params=pltpu.CompilerParams(vmem_limit_bytes=16 * MIB),
        cost_estimate=pl.CostEstimate(
            flops=6 * scores * HD, bytes_accessed=4 * MIB, transcendentals=scores
        ),
        name="attend",
    )(*operands)


def apply_expert(inputs, gate_up, w_down):
    features = w_down[0].shape[1]
    hidden = w_down[0].shape[0]
    rows = sum(x.shape[0] for x in inputs)

    def kernel(*refs):
        x_refs, refs = refs[: len(inputs)], refs[len(inputs) :]
        gu_refs, refs = refs[: len(gate_up)], refs[len(gate_up) :]
        down_refs, (out_ref,) = refs[: len(w_down)], refs[len(w_down) :]
        mine = lax.axis_index("ep") * lax.axis_size("hd") + lax.axis_index("hd")
        joined = jnp.concatenate([x[...] for x in x_refs], axis=0)
        x = joined[:, :features]
        table = joined[:, features:].astype(jnp.float32)
        lane = lax.broadcasted_iota(jnp.int32, table.shape, 1)
        gate = jnp.sum(jnp.where(lane == mine, table, 0.0), axis=1, keepdims=True)
        total = None
        for gu, down in zip(gu_refs, down_refs):
            gate_part = lax.dot_general(
                x, gu[0], CONTRACT_LAST, preferred_element_type=jnp.float32
            )
            up_part = lax.dot_general(x, gu[1], CONTRACT_LAST, preferred_element_type=jnp.float32)
            activation = (gate_part / (1.0 + jnp.exp(-gate_part)) * up_part).astype(jnp.bfloat16)
            product = jnp.dot(activation, down[...], preferred_element_type=jnp.float32)
            total = product if total is None else total + product
        out_ref[...] = gate * total.astype(jnp.bfloat16).astype(jnp.float32)

    vmem = pl.BlockSpec(memory_space=pltpu.VMEM)
    operands = list(inputs) + list(gate_up) + list(w_down)
    return pl.pallas_call(
        kernel,
        out_shape=jax.ShapeDtypeStruct((rows, features), jnp.float32),
        in_specs=[vmem] * len(operands),
        out_specs=vmem,
        compiler_params=pltpu.CompilerParams(vmem_limit_bytes=16 * MIB),
        cost_estimate=pl.CostEstimate(
            flops=6 * rows * hidden * len(w_down) * features,
            bytes_accessed=6 * MIB,
            transcendentals=rows * hidden * len(w_down),
        ),
        name="apply_expert",
    )(*operands)


def chip_ring(n_ep, n_hd):
    if n_hd == 2:
        return [z * 2 for z in range(n_ep)] + [z * 2 + 1 for z in reversed(range(n_ep))]
    return list(range(n_ep * n_hd))


def dense_experts(own, gate_up, w_down):
    axes = ("ep", "hd")
    walk = chip_ring(lax.axis_size("ep"), lax.axis_size("hd"))
    size = len(walk)
    ahead = [(walk[i], walk[(i + 1) % size]) for i in range(size)]
    back = [(b, a) for a, b in ahead]
    rows, features = own.shape[0], w_down[0].shape[1]
    half = rows // 2
    reach = size // 2
    behind, before, waiting = own, own, [own]
    outs = []
    for hop in range(1, reach + 1):
        if hop == reach:
            behind, before = behind[:half], before[half:]
        behind = lax.ppermute(behind, axes, ahead)
        before = lax.ppermute(before, axes, back)
        out = apply_expert(waiting, gate_up, w_down)
        behind, out = lax.optimization_barrier((behind, out))
        outs.append(out)
        waiting = [behind, before]
    outs.append(apply_expert(waiting, gate_up, w_down))
    mine = outs[0]
    outs = [(x[: x.shape[0] // 2], x[x.shape[0] // 2 :]) for x in outs[1:]]
    to_back, to_ahead = [x.astype(jnp.bfloat16) for x in outs[-1]]
    for hop in range(reach - 1, -1, -1):
        to_back = lax.ppermute(to_back, axes, back)
        to_ahead = lax.ppermute(to_ahead, axes, ahead)
        if hop == 0:
            break
        sums = []
        for came, first, share in [(to_back, 0, outs[hop - 1][0]), (to_ahead, half, outs[hop - 1][1])]:
            came = came.astype(jnp.float32)
            if hop == reach - 1:
                came = jnp.pad(came, ((first, rows - half - first), (0, 0)))
            sums.append(lax.optimization_barrier((came + share).astype(jnp.bfloat16)))
        to_back, to_ahead = sums
    return mine, to_back, to_ahead


def sparse_experts(widened, normed, gate_up, w_down, expert_ids, gates, features):
    half_width = normed.shape[1]
    pair_weights = gate_up[0].reshape(-1, features)
    hidden_units = w_down.shape[1]
    group_total = lax.axis_size("ep")
    group_experts = lax.axis_size("hd")
    all_experts = group_total * group_experts
    block_rows = expert_ids.shape[0]
    group_slots, expert_slots = block_sizes(block_rows, group_total, group_experts)
    chosen = (
        expert_ids[:, :, None] == jnp.arange(all_experts, dtype=jnp.int32)[None, None, :]
    ).astype(jnp.int32)
    named_count = jnp.sum(chosen, axis=1)
    earlier = jnp.cumsum(named_count, axis=0) - named_count
    slot_index = jnp.sum(chosen * earlier[:, None, :], axis=2)
    position = expert_ids * expert_slots + slot_index
    slot_columns = jnp.arange(all_experts * expert_slots, dtype=jnp.int32)
    gate_table = jnp.sum(
        jnp.where(
            position[:, :, None] == slot_columns[None, None, :],
            gates.astype(jnp.float32)[:, :, None],
            0.0,
        ),
        axis=1,
    ).astype(jnp.bfloat16)
    placed = (gate_table != 0).astype(jnp.bfloat16)
    outgoing = jnp.einsum("rq,rd->qd", placed, normed, preferred_element_type=jnp.float32).astype(
        jnp.bfloat16
    )
    outgoing = outgoing.reshape(all_experts, expert_slots, normed.shape[1])
    arrived = lax.all_to_all(outgoing, ("ep", "hd"), split_axis=0, concat_axis=0, tiled=True)
    lead_shape = arrived.shape[:-1]
    rows_in = arrived.reshape(-1, arrived.shape[-1])
    rows_in = lax.all_gather(rows_in, "sub", axis=1, tiled=True)
    projected_pair = jnp.einsum(
        "rd,fd->rf", rows_in, pair_weights, preferred_element_type=jnp.float32
    )
    activation = (
        jax.nn.silu(projected_pair[:, :hidden_units]) * projected_pair[:, hidden_units:]
    ).astype(jnp.bfloat16)
    partial_out = jnp.dot(activation, w_down[0], preferred_element_type=jnp.float32)
    expert_out = lax.psum_scatter(
        partial_out.astype(jnp.bfloat16), "sub", scatter_dimension=1, tiled=True
    )
    results = expert_out.reshape(lead_shape + (expert_out.shape[1],))
    returned = lax.all_to_all(results, ("ep", "hd"), split_axis=0, concat_axis=0, tiled=True)
    mixture = jnp.dot(
        gate_table,
        returned.reshape(all_experts * expert_slots, half_width),
        preferred_element_type=jnp.float32,
    )
    return (widened + mixture).astype(jnp.bfloat16)


def shards(
    queries,
    cache_keys,
    cache_values,
    page_len,
    new_keys,
    new_values,
    out_proj,
    residual,
    norm_gain,
    gate_up,
    w_down,
    expert_ids,
    gates,
):
    n_ep, n_hd, n_sub = lax.axis_size("ep"), lax.axis_size("hd"), lax.axis_size("sub")
    query_rows = queries.shape[0]
    heads_here = queries.shape[1] // HD
    kv_heads = max(1, heads_here // (QH // KVH))
    rows = query_rows // (n_hd * n_sub)
    features = norm_gain.shape[0]
    cache_rows = cache_keys.shape[0]
    all_experts = n_ep * n_hd * gate_up.shape[0]
    dense = (
        expert_ids.shape[1] == all_experts
        and gate_up.shape[0] == 1
        and n_ep * n_hd % 2 == 0
        and rows % 32 == 0
    )

    packed = pack_keys(
        cache_keys, cache_values, new_keys, new_values, page_len, kv_heads, heads_here
    )
    query_blocks = queries.reshape(n_hd, n_sub, rows, heads_here * HD)
    projections = sub_copies(out_proj)
    residual_parts = hand_over(split_rows(residual, n_sub))
    gate_table = gates_by_expert(expert_ids, gates, rows) if dense else None
    if dense:
        gate_up_parts = sub_copies(gate_up[0])
        w_down_parts = sub_copies(w_down[0])
    travelling = list(packed)
    states = [None] * kv_heads
    earlier = None
    for hop in range(n_ep):
        blocks = [sub_copies(x) for x in travelling]
        onward = [lax.ppermute(x, "ep", cycle(n_ep)) for x in travelling] if hop < n_ep - 1 else []
        for kv in range(kv_heads):
            finish = (projections, earlier) if hop == n_ep - 1 else None
            states[kv] = attend(
                query_blocks, kv, hop, blocks[kv], states[kv], cache_rows, kv_heads, finish
            )
            if finish:
                earlier = states[kv][0]
            else:
                onward[kv], states[kv] = lax.optimization_barrier((onward[kv], states[kv]))
        travelling = onward
    sent = states[-1][-1]
    if n_hd == 2:
        came = lax.ppermute(sent, "hd", cycle(n_hd))
    else:
        came = lax.psum_scatter(sent, "hd", scatter_dimension=0, tiled=True)
    hidden, normed = normalise(
        earlier if n_hd == 2 else None, came, residual_parts, norm_gain, gate_table
    )
    if not dense:
        own_columns = [
            jnp.concatenate(by_sub(sub_exchange(x, 1)), axis=0) for x in (hidden, normed)
        ]
        return sparse_experts(
            own_columns[0].astype(jnp.float32),
            own_columns[1],
            gate_up,
            w_down,
            expert_ids,
            gates,
            features,
        )
    mine, to_back, to_ahead = dense_experts(normed, gate_up_parts, w_down_parts)
    return stack_rows(hand_over(add_up(hidden, mine, to_back, to_ahead, n_sub)))


def solution(mesh):
    return jax.shard_map(
        shards,
        mesh=mesh,
        in_specs=(
            P(("grp", "ep"), "hd"),
            P(("grp", "ep", "sub"), None),
            P(("grp", "ep", "sub"), None),
            P(("grp", "ep", "sub")),
            P(("grp", "ep", "sub"), None),
            P(("grp", "ep", "sub"), None),
            P("hd", "sub"),
            P(("grp", "ep", "hd"), "sub"),
            P(),
            P(("ep", "hd"), None, "sub", None),
            P(("ep", "hd"), "sub", None),
            P(("grp", "ep", "hd"), None),
            P(("grp", "ep", "hd"), None),
        ),
        out_specs=P(("grp", "ep", "hd"), "sub"),
        check_vma=False,
    )
```

```python
import functools
import math

import jax
import jax.numpy as jnp
from jax import lax
from jax.experimental import pallas as pl
from jax.experimental.pallas import tpu as pltpu
from jax.sharding import PartitionSpec as P

QH = 32
KVH = 4
HD = 128
GROUPS_ROW = 4
NEG_FILL = -1e30
EPSILON = 1e-06
MASK_ROWS = 16
LANES = 128
MIB = 1024 * 1024
CONTRACT_LAST = (((1,), (1,)), ((), ()))


def block_sizes(block_rows, group_total, experts_group):
    group_slots = min(block_rows, 3 * GROUPS_ROW * block_rows // (2 * group_total))
    return (group_slots, 2 * group_slots // experts_group)


def cycle(size, step=1):
    return [(i, (i + step) % size) for i in range(size)]


def sub_copies(x):
    size = lax.axis_size("sub")
    return [x] + [lax.ppermute(x, "sub", cycle(size, step)) for step in range(1, size)]


def by_sub(copies):
    size = len(copies)
    me = lax.axis_index("sub")
    ordered = []
    for target in range(size):
        value = copies[0]
        for step in range(1, size):
            value = jnp.where((me - step) % size == target, copies[step], value)
        ordered.append(value)
    return ordered


def sub_exchange(x, axis):
    size = lax.axis_size("sub")
    me = lax.axis_index("sub")
    length = x.shape[axis] // size

    def part(index):
        return lax.dynamic_slice_in_dim(x, index * length, length, axis)

    came = [part(me)]
    for step in range(1, size):
        came.append(lax.ppermute(part((me + step) % size), "sub", cycle(size, step)))
    return came


def pack_keys(cache_keys, cache_values, new_keys, new_values, page_len, kv_heads, heads_here):
    cache_rows, new_rows = cache_keys.shape[0], new_keys.shape[0]
    group_width = QH // KVH
    rows = cache_rows + new_rows + MASK_ROWS

    def kernel(page_ref, ck_ref, cv_ref, nk_ref, nv_ref, *out_refs):
        first = lax.axis_index("hd") * heads_here // group_width
        lane = lax.broadcasted_iota(jnp.int32, (MASK_ROWS, 2 * HD), 1)
        bias = jnp.where(lane < page_ref[0], 0.0, NEG_FILL).astype(jnp.bfloat16)
        for kv, out_ref in enumerate(out_refs):
            columns = pl.ds(pl.multiple_of((first + kv) * HD, HD), HD)
            out_ref[:cache_rows, :HD] = ck_ref[:, columns]
            out_ref[:cache_rows, HD:] = cv_ref[:, columns]
            out_ref[cache_rows : cache_rows + new_rows, :HD] = nk_ref[:, columns]
            out_ref[cache_rows : cache_rows + new_rows, HD:] = nv_ref[:, columns]
            out_ref[cache_rows + new_rows :, :] = bias

    vmem = pl.BlockSpec(memory_space=pltpu.VMEM)
    return pl.pallas_call(
        kernel,
        out_shape=[jax.ShapeDtypeStruct((rows, 2 * HD), cache_keys.dtype)] * kv_heads,
        in_specs=[pl.BlockSpec(memory_space=pltpu.SMEM)] + [vmem] * 4,
        out_specs=[vmem] * kv_heads,
        name="pack_keys",
    )(page_len, cache_keys, cache_values, new_keys, new_values)


def small_kernel(kernel, out_shape, operands, name):
    vmem = pl.BlockSpec(memory_space=pltpu.VMEM)
    return pl.pallas_call(
        kernel,
        out_shape=out_shape,
        in_specs=[vmem] * len(operands),
        out_specs=[vmem] * len(out_shape),
        compiler_params=pltpu.CompilerParams(vmem_limit_bytes=8 * MIB),
        cost_estimate=pl.CostEstimate(flops=MIB, bytes_accessed=MIB, transcendentals=0),
        name=name,
    )(*operands)


def hand_over(parts):
    size = len(parts)
    return [parts[0]] + [
        lax.ppermute(part, "sub", cycle(size, step)) for step, part in enumerate(parts) if step
    ]


def choose_queries(queries):
    n_hd, n_sub, rows, columns = queries.shape

    def kernel(in_ref, out_ref, sems):
        sub = lax.axis_index("sub")
        hd = lax.axis_index("hd")
        copies = []
        for j in range(n_hd):
            place = (hd + j) % n_hd if n_hd == 2 else j
            copies.append(
                pltpu.make_async_copy(
                    in_ref.at[place, sub], out_ref.at[pl.ds(j * rows, rows), :], sems.at[j]
                )
            )
            copies[-1].start()
        for copy in copies:
            copy.wait()

    return pl.pallas_call(
        kernel,
        out_shape=jax.ShapeDtypeStruct((n_hd * rows, columns), queries.dtype),
        in_specs=[pl.BlockSpec(memory_space=pltpu.HBM)],
        out_specs=pl.BlockSpec(memory_space=pltpu.VMEM),
        scratch_shapes=[pltpu.SemaphoreType.DMA((n_hd,))],
        compiler_params=pltpu.CompilerParams(vmem_limit_bytes=8 * MIB),
        name="choose_queries",
    )(queries)


def split_rows(residual, n_sub):
    rows, columns = residual.shape[0] // n_sub, residual.shape[1]

    def kernel(in_ref, *out_refs):
        sub = lax.axis_index("sub")
        for step, out_ref in enumerate(out_refs):
            first = pl.multiple_of((sub + step) % n_sub * rows, rows)
            out_ref[...] = in_ref[pl.ds(first, rows), :]

    shape = jax.ShapeDtypeStruct((rows, columns), residual.dtype)
    return small_kernel(kernel, [shape] * n_sub, [residual], "split_rows")


def gates_by_expert(expert_ids, gates, rows):
    choices, block_rows = expert_ids.shape[1], expert_ids.shape[0]

    def kernel(ids_ref, gates_ref, out_ref):
        sub = lax.axis_index("sub")
        expert = lax.broadcasted_iota(jnp.int32, (LANES, block_rows), 0)
        weights = gates_ref[...].astype(jnp.float32)
        ids = ids_ref[...]
        table = jnp.zeros((LANES, block_rows), jnp.float32)
        for k in range(choices):
            table = table + jnp.where(ids[k : k + 1, :] == expert, weights[k : k + 1, :], 0.0)
        table = table.T
        chosen = table[:rows]
        for place in range(1, block_rows // rows):
            chosen = jnp.where(sub == place, table[place * rows : (place + 1) * rows], chosen)
        out_ref[...] = chosen.astype(jnp.bfloat16)

    shape = jax.ShapeDtypeStruct((rows, LANES), jnp.bfloat16)
    return small_kernel(kernel, [shape], [expert_ids.T, gates.T], "gates_by_expert")[0]


def normalise(kept, came, residual_parts, gain, gate_table, first):
    n_sub = len(residual_parts)
    rows, width = came.shape[0], residual_parts[0].shape[1]
    chunk = slice(first, first + rows)
    features = n_sub * width
    extra = 0 if gate_table is None else LANES

    def kernel(*refs):
        refs = list(refs)
        kept_ref = refs.pop(0) if kept is not None else None
        came_ref = refs.pop(0)
        part_refs = [refs.pop(0) for _ in residual_parts]
        gain_ref = refs.pop(0)
        if extra:
            gate_ref = refs.pop(0)
        hidden_ref, normed_ref = refs
        sub = lax.axis_index("sub")
        hidden, places, squares = [], [], 0.0
        for step, part_ref in enumerate(part_refs):
            here = slice(step * width, (step + 1) * width)
            projected = came_ref[:, here].astype(jnp.float32)
            if kept is not None:
                projected = kept_ref[:, here] + projected
            value = (part_ref[chunk, :].astype(jnp.float32) + projected).astype(jnp.bfloat16)
            hidden.append(value)
            place = pl.ds(pl.multiple_of((sub - step) % n_sub * width, width), width)
            places.append(place)
            hidden_ref[:, place] = value
            wide = value.astype(jnp.float32)
            squares = squares + jnp.sum(wide * wide, axis=1, keepdims=True)
        scale = lax.rsqrt(squares / features + EPSILON)
        for value, place in zip(hidden, places):
            normed = value.astype(jnp.float32) * scale * gain_ref[:, place].astype(jnp.float32)
            normed_ref[:, place] = normed.astype(jnp.bfloat16)
        if extra:
            normed_ref[:, features:] = gate_ref[chunk, :]

    operands = ([kept] if kept is not None else []) + [came] + list(residual_parts)
    operands.append(gain.reshape(1, features))
    if extra:
        operands.append(gate_table)
    out_shape = [
        jax.ShapeDtypeStruct((rows, features), jnp.bfloat16),
        jax.ShapeDtypeStruct((rows, features + extra), jnp.bfloat16),
    ]
    return small_kernel(kernel, out_shape, operands, "normalise")


def add_up(hidden, mine, to_back, to_ahead, n_sub):
    chunks = len(hidden)
    rows, features = hidden[0].shape
    width = features // n_sub

    def kernel(*refs):
        terms, out_refs = refs[: 4 * chunks], refs[4 * chunks :]
        sub = lax.axis_index("sub")
        for step, out_ref in enumerate(out_refs):
            place = pl.ds(pl.multiple_of((sub + step) % n_sub * width, width), width)
            for chunk in range(chunks):
                hidden_ref, mine_ref, back_ref, ahead_ref = terms[chunk::chunks]
                mixture = mine_ref[:, place] + back_ref[:, place].astype(jnp.float32)
                mixture = mixture + ahead_ref[:, place].astype(jnp.float32)
                total = hidden_ref[:, place].astype(jnp.float32) + mixture
                out_ref[chunk * rows : (chunk + 1) * rows, :] = total.astype(jnp.bfloat16)

    shape = jax.ShapeDtypeStruct((chunks * rows, width), jnp.bfloat16)
    operands = [*hidden, *mine, *to_back, *to_ahead]
    return small_kernel(kernel, [shape] * n_sub, operands, "add_up")


def stack_rows(parts):
    n_sub = len(parts)
    rows, width = parts[0].shape

    def kernel(*refs):
        sub = lax.axis_index("sub")
        for step, part_ref in enumerate(refs[:-1]):
            first = pl.multiple_of((sub - step) % n_sub * rows, rows)
            refs[-1][pl.ds(first, rows), :] = part_ref[...]

    shape = jax.ShapeDtypeStruct((n_sub * rows, width), parts[0].dtype)
    return small_kernel(kernel, [shape], parts, "stack_rows")[0]


def attend(queries, kv, hop, blocks, state, cache_rows, kv_heads, n_hd, chunks, finish=None):
    all_rows, columns = queries.shape
    rows, n_sub = all_rows // n_hd, len(blocks)
    per_kv = columns // HD // kv_heads
    stack = 2 if per_kv % 2 == 0 else 1
    part = stack * all_rows
    new_rows = blocks[0].shape[0] - cache_rows - MASK_ROWS
    keys = cache_rows + new_rows
    factor = math.log2(math.e) / math.sqrt(HD)
    relative = n_hd == 2
    last = finish is not None
    weights, earlier = finish if last else ([], None)
    head_columns = per_kv * HD
    final = last and kv == kv_heads - 1
    kept_rows = rows if relative else 0
    chunk_rows = rows // chunks if relative else all_rows

    def kernel(*refs):
        q_ref, refs = refs[0], refs[1:]
        block_refs, refs = refs[: len(blocks)], refs[len(blocks) :]
        if state is not None:
            (m_in, acc_in), refs = refs[:2], refs[2:]
        weight_refs, refs = refs[: len(weights)], refs[len(weights) :]
        if earlier is not None:
            earlier_ref, refs = refs[0], refs[1:]
        if last:
            results = len(out_shape)
            result_refs, refs = refs[:results], refs[results:]
            head_ref, refs = refs[0], refs[1:]
            held_refs, sems = refs[: len(weights)], refs[len(weights)]
            copies = [
                pltpu.make_async_copy(
                    w.at[pl.ds(kv * head_columns, head_columns), :], held, sems.at[i]
                )
                for i, (w, held) in enumerate(zip(weight_refs, held_refs))
            ]
            for copy in copies:
                copy.start()
        else:
            m_out, acc_out = refs
        sub = lax.axis_index("sub")
        ep = lax.axis_index("ep")
        hd = lax.axis_index("hd")
        places = [(hd + j) % n_hd if relative else j for j in range(n_hd)]
        biases = []
        for step, block in enumerate(block_refs):
            cache_bias = block[keys : keys + 1, :cache_rows].astype(jnp.float32)
            if hop == 0:
                key_id = ((sub - step) % n_sub) * new_rows + lax.broadcasted_iota(
                    jnp.int32, (rows, new_rows), 1
                )
                row_id = lax.broadcasted_iota(jnp.int32, (rows, new_rows), 0)
                seen = [
                    jnp.where(
                        key_id <= row_id + (place * n_sub + sub) * rows, 0.0, NEG_FILL
                    )
                    for place in places
                ]
                new_bias = jnp.concatenate(seen * stack, axis=0)
                cache_bias = jnp.broadcast_to(cache_bias, (part, cache_rows))
            else:
                new_bias = jnp.full(
                    (1, new_rows), jnp.where(ep >= hop, 0.0, NEG_FILL), jnp.float32
                )
            biases.append(jnp.concatenate([cache_bias, new_bias], axis=1))
        ones = jnp.ones((keys, HD), jnp.bfloat16)
        key_parts = [block[:keys, :HD] for block in block_refs]
        value_parts = [
            jnp.concatenate([block[:keys, HD:], ones], axis=1) for block in block_refs
        ]
        for index in range(per_kv // stack):
            here = slice(index * part, (index + 1) * part)
            heads = range(kv * per_kv + index * stack, kv * per_kv + (index + 1) * stack)
            q = jnp.concatenate([q_ref[:, h * HD : (h + 1) * HD] for h in heads], axis=0)
            terms = [
                lax.dot_general(q, k, CONTRACT_LAST, preferred_element_type=jnp.float32) * factor
                + bias
                for k, bias in zip(key_parts, biases)
            ]
            top = jnp.max(functools.reduce(jnp.maximum, terms), axis=1, keepdims=True)
            top = jnp.broadcast_to(top, (part, LANES))
            if state is not None:
                top_in = m_in[here, :]
                top = jnp.maximum(top, top_in)
            wide_top = jnp.concatenate([top] * (keys // LANES), axis=1)
            acc = None
            for term, v in zip(terms, value_parts):
                exp_terms = jnp.exp2(term - wide_top).astype(jnp.bfloat16)
                product = jnp.dot(exp_terms, v, preferred_element_type=jnp.float32)
                acc = product if acc is None else acc + product
            if state is not None:
                scale = jnp.exp2(top_in - top)
                acc = acc + jnp.concatenate([scale, scale], axis=1) * acc_in[here, :]
            if last:
                out = (acc[:, :HD] / acc[:, HD:]).astype(jnp.bfloat16)
                for s in range(stack):
                    first = (index * stack + s) * HD
                    head_ref[:, first : first + HD] = out[s * all_rows : (s + 1) * all_rows]
            else:
                m_out[here, :] = top
                acc_out[here, :] = acc
        if last:
            for copy in copies:
                copy.wait()
            source = head_ref[...]
            width = held_refs[0].shape[1]
            for i, held in enumerate(held_refs):
                here = slice(i * width, (i + 1) * width)
                product = jnp.dot(source, held[...], preferred_element_type=jnp.float32)
                if earlier is not None:
                    product = product + earlier_ref[:, here]
                if final:
                    for j, result_ref in enumerate(result_refs):
                        share = product[j * chunk_rows : (j + 1) * chunk_rows]
                        result_ref[:, here] = share.astype(result_ref.dtype)
                else:
                    result_refs[0][:, here] = product

    vmem = pl.BlockSpec(memory_space=pltpu.VMEM)
    anywhere = pl.BlockSpec(memory_space=pl.ANY)
    scratch = []
    if last:
        features = sum(w.shape[1] for w in weights)
        if final:
            out_shape = [
                jax.ShapeDtypeStruct((chunk_rows, features), kind)
                for kind, count in [
                    (jnp.float32, kept_rows // chunk_rows),
                    (jnp.bfloat16, (all_rows - kept_rows) // chunk_rows),
                ]
                for _ in range(count)
            ]
        else:
            out_shape = (jax.ShapeDtypeStruct((all_rows, features), jnp.float32),)
        scratch = [pltpu.VMEM((all_rows, head_columns), jnp.bfloat16)]
        scratch += [pltpu.VMEM((head_columns, w.shape[1]), w.dtype) for w in weights]
        scratch += [pltpu.SemaphoreType.DMA((len(weights),))]
    else:
        out_shape = (
            jax.ShapeDtypeStruct((per_kv * all_rows, LANES), jnp.float32),
            jax.ShapeDtypeStruct((per_kv * all_rows, 2 * HD), jnp.float32),
        )
    operands = [queries] + list(blocks) + (list(state) if state is not None else [])
    in_specs = [vmem] * len(operands) + [anywhere] * len(weights)
    operands += list(weights)
    if earlier is not None:
        operands.append(earlier)
        in_specs.append(vmem)
    scores = all_rows * per_kv * keys * len(blocks)
    return pl.pallas_call(
        kernel,
        out_shape=out_shape,
        in_specs=in_specs,
        out_specs=tuple(vmem for _ in out_shape),
        scratch_shapes=scratch,
        compiler_params=pltpu.CompilerParams(vmem_limit_bytes=16 * MIB),
        cost_estimate=pl.CostEstimate(
            flops=6 * scores * HD, bytes_accessed=4 * MIB, transcendentals=scores
        ),
        name="attend",
    )(*operands)


def apply_expert(inputs, gate_up, w_down):
    features = w_down[0].shape[1]
    hidden = w_down[0].shape[0]
    rows = sum(x.shape[0] for x in inputs)

    def kernel(*refs):
        x_refs, refs = refs[: len(inputs)], refs[len(inputs) :]
        gu_refs, refs = refs[: len(gate_up)], refs[len(gate_up) :]
        down_refs, out_refs = refs[: len(w_down)], refs[len(w_down) :]
        mine = lax.axis_index("ep") * lax.axis_size("hd") + lax.axis_index("hd")
        joined = jnp.concatenate([x[...] for x in x_refs], axis=0)
        x = joined[:, :features]
        table = joined[:, features:].astype(jnp.float32)
        lane = lax.broadcasted_iota(jnp.int32, table.shape, 1)
        gate = jnp.sum(jnp.where(lane == mine, table, 0.0), axis=1, keepdims=True)
        total = None
        for gu, down in zip(gu_refs, down_refs):
            gate_part = lax.dot_general(
                x, gu[0], CONTRACT_LAST, preferred_element_type=jnp.float32
            )
            up_part = lax.dot_general(x, gu[1], CONTRACT_LAST, preferred_element_type=jnp.float32)
            activation = (gate_part / (1.0 + jnp.exp(-gate_part)) * up_part).astype(jnp.bfloat16)
            product = jnp.dot(activation, down[...], preferred_element_type=jnp.float32)
            total = product if total is None else total + product
        total = gate * total.astype(jnp.bfloat16).astype(jnp.float32)
        first = 0
        for out_ref in out_refs:
            out_ref[...] = total[first : first + out_ref.shape[0]]
            first += out_ref.shape[0]

    vmem = pl.BlockSpec(memory_space=pltpu.VMEM)
    operands = list(inputs) + list(gate_up) + list(w_down)
    return pl.pallas_call(
        kernel,
        out_shape=[jax.ShapeDtypeStruct((x.shape[0], features), jnp.float32) for x in inputs],
        in_specs=[vmem] * len(operands),
        out_specs=[vmem] * len(inputs),
        compiler_params=pltpu.CompilerParams(vmem_limit_bytes=16 * MIB),
        cost_estimate=pl.CostEstimate(
            flops=6 * rows * hidden * len(w_down) * features,
            bytes_accessed=6 * MIB,
            transcendentals=rows * hidden * len(w_down),
        ),
        name="apply_expert",
    )(*operands)


def chip_ring(n_ep, n_hd):
    if n_hd == 2:
        return [z * 2 for z in range(n_ep)] + [z * 2 + 1 for z in reversed(range(n_ep))]
    return list(range(n_ep * n_hd))


def add_share(came, share):
    def kernel(came_ref, share_ref, out_ref):
        total = came_ref[...].astype(jnp.float32) + share_ref[...]
        out_ref[...] = total.astype(jnp.bfloat16)

    shape = jax.ShapeDtypeStruct(share.shape, jnp.bfloat16)
    return small_kernel(kernel, [shape], [came, share], "add_share")[0]


def dense_experts(own, gate_up, w_down):
    axes = ("ep", "hd")
    walk = chip_ring(lax.axis_size("ep"), lax.axis_size("hd"))
    size = len(walk)
    ahead = [(walk[i], walk[(i + 1) % size]) for i in range(size)]
    back = [(b, a) for a, b in ahead]
    reach = size // 2
    behind, before, waiting = list(own), list(own), None
    outs = [None]
    for hop in range(1, reach + 1):
        behind[0] = lax.ppermute(behind[0], axes, ahead)
        before[1] = lax.ppermute(before[1], axes, back)
        if hop < reach:
            behind[1] = lax.ppermute(behind[1], axes, ahead)
            before[0] = lax.ppermute(before[0], axes, back)
        if waiting:
            out = apply_expert(waiting, gate_up, w_down)
            behind[0], out = lax.optimization_barrier((behind[0], out))
            outs.append(out)
        waiting = [behind[0], before[1]] + ([behind[1], before[0]] if hop < reach else [])
    outs.append(apply_expert(waiting, gate_up, w_down))
    to_back, to_ahead = [None, None], [None, None]
    for hop in range(reach, 0, -1):
        shares = outs[hop]
        for chunks, chunk, way, share in [
            (to_back, 0, back, 0),
            (to_ahead, 1, ahead, 1),
            (to_back, 1, back, 2),
            (to_ahead, 0, ahead, 3),
        ]:
            if share >= len(shares):
                continue
            if chunks[chunk] is None:
                sum_here = shares[share].astype(jnp.bfloat16)
            else:
                sum_here = add_share(chunks[chunk], shares[share])
            chunks[chunk] = lax.ppermute(sum_here, axes, way)
            if hop == min(2, reach) and share == 0:
                chunks[chunk], own = lax.optimization_barrier((chunks[chunk], own))
    return apply_expert(own, gate_up, w_down), to_back, to_ahead


def sparse_experts(widened, normed, gate_up, w_down, expert_ids, gates, features):
    half_width = normed.shape[1]
    pair_weights = gate_up[0].reshape(-1, features)
    hidden_units = w_down.shape[1]
    group_total = lax.axis_size("ep")
    group_experts = lax.axis_size("hd")
    all_experts = group_total * group_experts
    block_rows = expert_ids.shape[0]
    group_slots, expert_slots = block_sizes(block_rows, group_total, group_experts)
    chosen = (
        expert_ids[:, :, None] == jnp.arange(all_experts, dtype=jnp.int32)[None, None, :]
    ).astype(jnp.int32)
    named_count = jnp.sum(chosen, axis=1)
    earlier = jnp.cumsum(named_count, axis=0) - named_count
    slot_index = jnp.sum(chosen * earlier[:, None, :], axis=2)
    position = expert_ids * expert_slots + slot_index
    slot_columns = jnp.arange(all_experts * expert_slots, dtype=jnp.int32)
    gate_table = jnp.sum(
        jnp.where(
            position[:, :, None] == slot_columns[None, None, :],
            gates.astype(jnp.float32)[:, :, None],
            0.0,
        ),
        axis=1,
    ).astype(jnp.bfloat16)
    placed = (gate_table != 0).astype(jnp.bfloat16)
    outgoing = jnp.einsum("rq,rd->qd", placed, normed, preferred_element_type=jnp.float32).astype(
        jnp.bfloat16
    )
    outgoing = outgoing.reshape(all_experts, expert_slots, normed.shape[1])
    arrived = lax.all_to_all(outgoing, ("ep", "hd"), split_axis=0, concat_axis=0, tiled=True)
    lead_shape = arrived.shape[:-1]
    rows_in = arrived.reshape(-1, arrived.shape[-1])
    rows_in = lax.all_gather(rows_in, "sub", axis=1, tiled=True)
    projected_pair = jnp.einsum(
        "rd,fd->rf", rows_in, pair_weights, preferred_element_type=jnp.float32
    )
    activation = (
        jax.nn.silu(projected_pair[:, :hidden_units]) * projected_pair[:, hidden_units:]
    ).astype(jnp.bfloat16)
    partial_out = jnp.dot(activation, w_down[0], preferred_element_type=jnp.float32)
    expert_out = lax.psum_scatter(
        partial_out.astype(jnp.bfloat16), "sub", scatter_dimension=1, tiled=True
    )
    results = expert_out.reshape(lead_shape + (expert_out.shape[1],))
    returned = lax.all_to_all(results, ("ep", "hd"), split_axis=0, concat_axis=0, tiled=True)
    mixture = jnp.dot(
        gate_table,
        returned.reshape(all_experts * expert_slots, half_width),
        preferred_element_type=jnp.float32,
    )
    return (widened + mixture).astype(jnp.bfloat16)


def shards(
    queries,
    cache_keys,
    cache_values,
    page_len,
    new_keys,
    new_values,
    out_proj,
    residual,
    norm_gain,
    gate_up,
    w_down,
    expert_ids,
    gates,
):
    n_ep, n_hd, n_sub = lax.axis_size("ep"), lax.axis_size("hd"), lax.axis_size("sub")
    query_rows = queries.shape[0]
    heads_here = queries.shape[1] // HD
    kv_heads = max(1, heads_here // (QH // KVH))
    rows = query_rows // (n_hd * n_sub)
    features = norm_gain.shape[0]
    cache_rows = cache_keys.shape[0]
    all_experts = n_ep * n_hd * gate_up.shape[0]
    dense = (
        expert_ids.shape[1] == all_experts
        and gate_up.shape[0] == 1
        and n_ep * n_hd % 2 == 0
        and rows % 32 == 0
    )

    projections = sub_copies(out_proj)
    packed = pack_keys(
        cache_keys, cache_values, new_keys, new_values, page_len, kv_heads, heads_here
    )
    query_rows_here = choose_queries(queries.reshape(n_hd, n_sub, rows, heads_here * HD))
    travelling = list(packed)
    states = [None] * kv_heads
    earlier = None
    for hop in range(n_ep):
        blocks = [sub_copies(x) for x in travelling]
        onward = [lax.ppermute(x, "ep", cycle(n_ep)) for x in travelling] if hop < n_ep - 1 else []
        if hop == min(2, n_ep - 1):
            residual, gate_up, w_down, blocks = lax.optimization_barrier(
                (residual, gate_up, w_down, blocks)
            )
            residual_parts = hand_over(split_rows(residual, n_sub))
            gate_table = gates_by_expert(expert_ids, gates, rows) if dense else None
            if dense:
                gate_up_parts = sub_copies(gate_up[0])
                w_down_parts = sub_copies(w_down[0])
        for kv in range(kv_heads):
            finish = (projections, earlier) if hop == n_ep - 1 else None
            states[kv] = attend(
                query_rows_here,
                kv,
                hop,
                blocks[kv],
                states[kv],
                cache_rows,
                kv_heads,
                n_hd,
                2 if dense else 1,
                finish,
            )
            if finish:
                earlier = states[kv][0]
            else:
                onward[kv], states[kv] = lax.optimization_barrier((onward[kv], states[kv]))
        travelling = onward
    parts = states[-1]
    if n_hd == 2:
        kept, sent = parts[: len(parts) // 2], parts[len(parts) // 2 :]
        came = [lax.ppermute(x, "hd", cycle(n_hd)) for x in sent]
    else:
        kept = [None]
        came = [lax.psum_scatter(parts[0], "hd", scatter_dimension=0, tiled=True)]
    hidden, normed = [], []
    for index, (kept_chunk, came_chunk) in enumerate(zip(kept, came)):
        pair = normalise(
            kept_chunk,
            came_chunk,
            residual_parts,
            norm_gain,
            gate_table,
            index * came_chunk.shape[0],
        )
        hidden.append(pair[0])
        normed.append(pair[1])
    if not dense:
        own_columns = [
            jnp.concatenate(by_sub(sub_exchange(x, 1)), axis=0) for x in (hidden[0], normed[0])
        ]
        return sparse_experts(
            own_columns[0].astype(jnp.float32),
            own_columns[1],
            gate_up,
            w_down,
            expert_ids,
            gates,
            features,
        )
    mine, to_back, to_ahead = dense_experts(normed, gate_up_parts, w_down_parts)
    return stack_rows(hand_over(add_up(hidden, mine, to_back, to_ahead, n_sub)))


def solution(mesh):
    return jax.shard_map(
        shards,
        mesh=mesh,
        in_specs=(
            P(("grp", "ep"), "hd"),
            P(("grp", "ep", "sub"), None),
            P(("grp", "ep", "sub"), None),
            P(("grp", "ep", "sub")),
            P(("grp", "ep", "sub"), None),
            P(("grp", "ep", "sub"), None),
            P("hd", "sub"),
            P(("grp", "ep", "hd"), "sub"),
            P(),
            P(("ep", "hd"), None, "sub", None),
            P(("ep", "hd"), "sub", None),
            P(("grp", "ep", "hd"), None),
            P(("grp", "ep", "hd"), None),
        ),
        out_specs=P(("grp", "ep", "hd"), "sub"),
        check_vma=False,
    )
```

```python
import functools
import math

import jax
import jax.numpy as jnp
from jax import lax
from jax.experimental import pallas as pl
from jax.experimental.pallas import tpu as pltpu
from jax.sharding import PartitionSpec as P

QH = 32
KVH = 4
HD = 128
GROUPS_ROW = 4
NEG_FILL = -1e30
EPSILON = 1e-06
MASK_ROWS = 16
LANES = 128
MIB = 1024 * 1024
CONTRACT_LAST = (((1,), (1,)), ((), ()))


def block_sizes(block_rows, group_total, experts_group):
    group_slots = min(block_rows, 3 * GROUPS_ROW * block_rows // (2 * group_total))
    return (group_slots, 2 * group_slots // experts_group)


def cycle(size, step=1):
    return [(i, (i + step) % size) for i in range(size)]


def sub_copies(x):
    size = lax.axis_size("sub")
    return [x] + [lax.ppermute(x, "sub", cycle(size, step)) for step in range(1, size)]


def by_sub(copies):
    size = len(copies)
    me = lax.axis_index("sub")
    ordered = []
    for target in range(size):
        value = copies[0]
        for step in range(1, size):
            value = jnp.where((me - step) % size == target, copies[step], value)
        ordered.append(value)
    return ordered


def sub_exchange(x, axis):
    size = lax.axis_size("sub")
    me = lax.axis_index("sub")
    length = x.shape[axis] // size

    def part(index):
        return lax.dynamic_slice_in_dim(x, index * length, length, axis)

    came = [part(me)]
    for step in range(1, size):
        came.append(lax.ppermute(part((me + step) % size), "sub", cycle(size, step)))
    return came


def pack_keys(cache_keys, cache_values, new_keys, new_values, page_len, kv_heads, heads_here):
    cache_rows, new_rows = cache_keys.shape[0], new_keys.shape[0]
    group_width = QH // KVH
    rows = cache_rows + new_rows + MASK_ROWS

    def kernel(page_ref, ck_ref, cv_ref, nk_ref, nv_ref, *out_refs):
        first = lax.axis_index("hd") * heads_here // group_width
        lane = lax.broadcasted_iota(jnp.int32, (MASK_ROWS, 2 * HD), 1)
        bias = jnp.where(lane < page_ref[0], 0.0, NEG_FILL).astype(jnp.bfloat16)
        for kv, out_ref in enumerate(out_refs):
            columns = pl.ds(pl.multiple_of((first + kv) * HD, HD), HD)
            out_ref[:cache_rows, :HD] = ck_ref[:, columns]
            out_ref[:cache_rows, HD:] = cv_ref[:, columns]
            out_ref[cache_rows : cache_rows + new_rows, :HD] = nk_ref[:, columns]
            out_ref[cache_rows : cache_rows + new_rows, HD:] = nv_ref[:, columns]
            out_ref[cache_rows + new_rows :, :] = bias

    vmem = pl.BlockSpec(memory_space=pltpu.VMEM)
    return pl.pallas_call(
        kernel,
        out_shape=[jax.ShapeDtypeStruct((rows, 2 * HD), cache_keys.dtype)] * kv_heads,
        in_specs=[pl.BlockSpec(memory_space=pltpu.SMEM)] + [vmem] * 4,
        out_specs=[vmem] * kv_heads,
        name="pack_keys",
    )(page_len, cache_keys, cache_values, new_keys, new_values)


def small_kernel(kernel, out_shape, operands, name):
    vmem = pl.BlockSpec(memory_space=pltpu.VMEM)
    return pl.pallas_call(
        kernel,
        out_shape=out_shape,
        in_specs=[vmem] * len(operands),
        out_specs=[vmem] * len(out_shape),
        compiler_params=pltpu.CompilerParams(vmem_limit_bytes=8 * MIB),
        cost_estimate=pl.CostEstimate(flops=MIB, bytes_accessed=MIB, transcendentals=0),
        name=name,
    )(*operands)


def hand_over(parts):
    size = len(parts)
    return [parts[0]] + [
        lax.ppermute(part, "sub", cycle(size, step)) for step, part in enumerate(parts) if step
    ]


def choose_queries(queries):
    n_hd, n_sub, rows, columns = queries.shape

    def kernel(in_ref, out_ref, sems):
        sub = lax.axis_index("sub")
        hd = lax.axis_index("hd")
        copies = []
        for j in range(n_hd):
            place = (hd + j) % n_hd if n_hd == 2 else j
            copies.append(
                pltpu.make_async_copy(
                    in_ref.at[place, sub], out_ref.at[pl.ds(j * rows, rows), :], sems.at[j]
                )
            )
            copies[-1].start()
        for copy in copies:
            copy.wait()

    return pl.pallas_call(
        kernel,
        out_shape=jax.ShapeDtypeStruct((n_hd * rows, columns), queries.dtype),
        in_specs=[pl.BlockSpec(memory_space=pltpu.HBM)],
        out_specs=pl.BlockSpec(memory_space=pltpu.VMEM),
        scratch_shapes=[pltpu.SemaphoreType.DMA((n_hd,))],
        compiler_params=pltpu.CompilerParams(vmem_limit_bytes=8 * MIB),
        name="choose_queries",
    )(queries)


def split_rows(residual, n_sub):
    rows, columns = residual.shape[0] // n_sub, residual.shape[1]

    def kernel(in_ref, *out_refs):
        sub = lax.axis_index("sub")
        for step, out_ref in enumerate(out_refs):
            first = pl.multiple_of((sub + step) % n_sub * rows, rows)
            out_ref[...] = in_ref[pl.ds(first, rows), :]

    shape = jax.ShapeDtypeStruct((rows, columns), residual.dtype)
    return small_kernel(kernel, [shape] * n_sub, [residual], "split_rows")


def gates_by_expert(expert_ids, gates, rows):
    choices, block_rows = expert_ids.shape[1], expert_ids.shape[0]

    def kernel(ids_ref, gates_ref, out_ref):
        sub = lax.axis_index("sub")
        expert = lax.broadcasted_iota(jnp.int32, (LANES, block_rows), 0)
        weights = gates_ref[...].astype(jnp.float32)
        ids = ids_ref[...]
        table = jnp.zeros((LANES, block_rows), jnp.float32)
        for k in range(choices):
            table = table + jnp.where(ids[k : k + 1, :] == expert, weights[k : k + 1, :], 0.0)
        table = table.T
        chosen = table[:rows]
        for place in range(1, block_rows // rows):
            chosen = jnp.where(sub == place, table[place * rows : (place + 1) * rows], chosen)
        out_ref[...] = chosen.astype(jnp.bfloat16)

    shape = jax.ShapeDtypeStruct((rows, LANES), jnp.bfloat16)
    return small_kernel(kernel, [shape], [expert_ids.T, gates.T], "gates_by_expert")[0]


def normalise(kept, came, residual_parts, gain, gate_table, first):
    n_sub = len(residual_parts)
    rows, width = came.shape[0], residual_parts[0].shape[1]
    chunk = slice(first, first + rows)
    features = n_sub * width
    extra = 0 if gate_table is None else LANES

    def kernel(*refs):
        refs = list(refs)
        kept_ref = refs.pop(0) if kept is not None else None
        came_ref = refs.pop(0)
        part_refs = [refs.pop(0) for _ in residual_parts]
        gain_ref = refs.pop(0)
        if extra:
            gate_ref = refs.pop(0)
        hidden_ref, normed_ref = refs
        sub = lax.axis_index("sub")
        hidden, places, squares = [], [], 0.0
        for step, part_ref in enumerate(part_refs):
            here = slice(step * width, (step + 1) * width)
            projected = came_ref[:, here].astype(jnp.float32)
            if kept is not None:
                projected = kept_ref[:, here] + projected
            value = (part_ref[chunk, :].astype(jnp.float32) + projected).astype(jnp.bfloat16)
            hidden.append(value)
            place = pl.ds(pl.multiple_of((sub - step) % n_sub * width, width), width)
            places.append(place)
            hidden_ref[:, place] = value
            wide = value.astype(jnp.float32)
            squares = squares + jnp.sum(wide * wide, axis=1, keepdims=True)
        scale = lax.rsqrt(squares / features + EPSILON)
        for value, place in zip(hidden, places):
            normed = value.astype(jnp.float32) * scale * gain_ref[:, place].astype(jnp.float32)
            normed_ref[:, place] = normed.astype(jnp.bfloat16)
        if extra:
            normed_ref[:, features:] = gate_ref[chunk, :]

    operands = ([kept] if kept is not None else []) + [came] + list(residual_parts)
    operands.append(gain.reshape(1, features))
    if extra:
        operands.append(gate_table)
    out_shape = [
        jax.ShapeDtypeStruct((rows, features), jnp.bfloat16),
        jax.ShapeDtypeStruct((rows, features + extra), jnp.bfloat16),
    ]
    return small_kernel(kernel, out_shape, operands, "normalise")


def add_up(hidden, mine, to_back, to_ahead, n_sub):
    chunks = len(hidden)
    rows, features = hidden[0].shape
    width = features // n_sub

    def kernel(*refs):
        terms, out_refs = refs[: 4 * chunks], refs[4 * chunks :]
        sub = lax.axis_index("sub")
        for step, out_ref in enumerate(out_refs):
            place = pl.ds(pl.multiple_of((sub + step) % n_sub * width, width), width)
            for chunk in range(chunks):
                hidden_ref, mine_ref, back_ref, ahead_ref = terms[chunk::chunks]
                mixture = mine_ref[:, place] + back_ref[:, place].astype(jnp.float32)
                mixture = mixture + ahead_ref[:, place].astype(jnp.float32)
                total = hidden_ref[:, place].astype(jnp.float32) + mixture
                out_ref[chunk * rows : (chunk + 1) * rows, :] = total.astype(jnp.bfloat16)

    shape = jax.ShapeDtypeStruct((chunks * rows, width), jnp.bfloat16)
    operands = [*hidden, *mine, *to_back, *to_ahead]
    return small_kernel(kernel, [shape] * n_sub, operands, "add_up")


def stack_rows(parts):
    n_sub = len(parts)
    rows, width = parts[0].shape

    def kernel(*refs):
        sub = lax.axis_index("sub")
        for step, part_ref in enumerate(refs[:-1]):
            first = pl.multiple_of((sub - step) % n_sub * rows, rows)
            refs[-1][pl.ds(first, rows), :] = part_ref[...]

    shape = jax.ShapeDtypeStruct((n_sub * rows, width), parts[0].dtype)
    return small_kernel(kernel, [shape], parts, "stack_rows")[0]


def attend(queries, kv, stages, state, cache_rows, kv_heads, n_hd, chunks, finish=None):
    all_rows, columns = queries.shape
    rows, n_sub = all_rows // n_hd, len(stages[0][1])
    blocks = [block for _, stage_blocks in stages for block in stage_blocks]
    origins = [(hop, step) for hop, _ in stages for step in range(n_sub)]
    per_kv = columns // HD // kv_heads
    stack = 2 if per_kv % 2 == 0 else 1
    part = stack * all_rows
    new_rows = blocks[0].shape[0] - cache_rows - MASK_ROWS
    keys = cache_rows + new_rows
    factor = math.log2(math.e) / math.sqrt(HD)
    relative = n_hd == 2
    last = finish is not None
    weights, earlier = finish if last else ([], None)
    head_columns = per_kv * HD
    final = last and kv == kv_heads - 1
    kept_rows = rows if relative else 0
    chunk_rows = rows // chunks if relative else all_rows

    def kernel(*refs):
        q_ref, refs = refs[0], refs[1:]
        block_refs, refs = refs[: len(blocks)], refs[len(blocks) :]
        if state is not None:
            (m_in, acc_in), refs = refs[:2], refs[2:]
        weight_refs, refs = refs[: len(weights)], refs[len(weights) :]
        if earlier is not None:
            earlier_ref, refs = refs[0], refs[1:]
        if last:
            results = len(out_shape)
            result_refs, refs = refs[:results], refs[results:]
            head_ref, refs = refs[0], refs[1:]
            held_refs, sems = refs[: len(weights)], refs[len(weights)]
            copies = [
                pltpu.make_async_copy(
                    w.at[pl.ds(kv * head_columns, head_columns), :], held, sems.at[i]
                )
                for i, (w, held) in enumerate(zip(weight_refs, held_refs))
            ]
            for copy in copies:
                copy.start()
        else:
            m_out, acc_out = refs
        sub = lax.axis_index("sub")
        ep = lax.axis_index("ep")
        hd = lax.axis_index("hd")
        places = [(hd + j) % n_hd if relative else j for j in range(n_hd)]
        biases = []
        for (hop, step), block in zip(origins, block_refs):
            cache_bias = block[keys : keys + 1, :cache_rows].astype(jnp.float32)
            if hop == 0:
                key_id = ((sub - step) % n_sub) * new_rows + lax.broadcasted_iota(
                    jnp.int32, (rows, new_rows), 1
                )
                row_id = lax.broadcasted_iota(jnp.int32, (rows, new_rows), 0)
                seen = [
                    jnp.where(
                        key_id <= row_id + (place * n_sub + sub) * rows, 0.0, NEG_FILL
                    )
                    for place in places
                ]
                new_bias = jnp.concatenate(seen * stack, axis=0)
                cache_bias = jnp.broadcast_to(cache_bias, (part, cache_rows))
            else:
                new_bias = jnp.full(
                    (1, new_rows), jnp.where(ep >= hop, 0.0, NEG_FILL), jnp.float32
                )
            biases.append(jnp.concatenate([cache_bias, new_bias], axis=1))
        ones = jnp.ones((keys, HD), jnp.bfloat16)
        key_parts = [block[:keys, :HD] for block in block_refs]
        value_parts = [
            jnp.concatenate([block[:keys, HD:], ones], axis=1) for block in block_refs
        ]
        for index in range(per_kv // stack):
            here = slice(index * part, (index + 1) * part)
            heads = range(kv * per_kv + index * stack, kv * per_kv + (index + 1) * stack)
            q = jnp.concatenate([q_ref[:, h * HD : (h + 1) * HD] for h in heads], axis=0)
            terms = [
                lax.dot_general(q, k, CONTRACT_LAST, preferred_element_type=jnp.float32) * factor
                + bias
                for k, bias in zip(key_parts, biases)
            ]
            top = jnp.max(functools.reduce(jnp.maximum, terms), axis=1, keepdims=True)
            top = jnp.broadcast_to(top, (part, LANES))
            if state is not None:
                top_in = m_in[here, :]
                top = jnp.maximum(top, top_in)
            wide_top = jnp.concatenate([top] * (keys // LANES), axis=1)
            acc = None
            for term, v in zip(terms, value_parts):
                exp_terms = jnp.exp2(term - wide_top).astype(jnp.bfloat16)
                product = jnp.dot(exp_terms, v, preferred_element_type=jnp.float32)
                acc = product if acc is None else acc + product
            if state is not None:
                scale = jnp.exp2(top_in - top)
                acc = acc + jnp.concatenate([scale, scale], axis=1) * acc_in[here, :]
            if last:
                out = (acc[:, :HD] / acc[:, HD:]).astype(jnp.bfloat16)
                for s in range(stack):
                    first = (index * stack + s) * HD
                    head_ref[:, first : first + HD] = out[s * all_rows : (s + 1) * all_rows]
            else:
                m_out[here, :] = top
                acc_out[here, :] = acc
        if last:
            for copy in copies:
                copy.wait()
            source = head_ref[...]
            width = held_refs[0].shape[1]
            for i, held in enumerate(held_refs):
                here = slice(i * width, (i + 1) * width)
                product = jnp.dot(source, held[...], preferred_element_type=jnp.float32)
                if earlier is not None:
                    product = product + earlier_ref[:, here]
                if final:
                    for j, result_ref in enumerate(result_refs):
                        share = product[j * chunk_rows : (j + 1) * chunk_rows]
                        result_ref[:, here] = share.astype(result_ref.dtype)
                else:
                    result_refs[0][:, here] = product

    vmem = pl.BlockSpec(memory_space=pltpu.VMEM)
    anywhere = pl.BlockSpec(memory_space=pl.ANY)
    scratch = []
    if last:
        features = sum(w.shape[1] for w in weights)
        if final:
            out_shape = [
                jax.ShapeDtypeStruct((chunk_rows, features), kind)
                for kind, count in [
                    (jnp.float32, kept_rows // chunk_rows),
                    (jnp.bfloat16, (all_rows - kept_rows) // chunk_rows),
                ]
                for _ in range(count)
            ]
        else:
            out_shape = (jax.ShapeDtypeStruct((all_rows, features), jnp.float32),)
        scratch = [pltpu.VMEM((all_rows, head_columns), jnp.bfloat16)]
        scratch += [pltpu.VMEM((head_columns, w.shape[1]), w.dtype) for w in weights]
        scratch += [pltpu.SemaphoreType.DMA((len(weights),))]
    else:
        out_shape = (
            jax.ShapeDtypeStruct((per_kv * all_rows, LANES), jnp.float32),
            jax.ShapeDtypeStruct((per_kv * all_rows, 2 * HD), jnp.float32),
        )
    operands = [queries] + list(blocks) + (list(state) if state is not None else [])
    in_specs = [vmem] * len(operands) + [anywhere] * len(weights)
    operands += list(weights)
    if earlier is not None:
        operands.append(earlier)
        in_specs.append(vmem)
    scores = all_rows * per_kv * keys * len(blocks)
    return pl.pallas_call(
        kernel,
        out_shape=out_shape,
        in_specs=in_specs,
        out_specs=tuple(vmem for _ in out_shape),
        scratch_shapes=scratch,
        compiler_params=pltpu.CompilerParams(vmem_limit_bytes=16 * MIB),
        cost_estimate=pl.CostEstimate(
            flops=6 * scores * HD, bytes_accessed=4 * MIB, transcendentals=scores
        ),
        name="attend",
    )(*operands)


def apply_expert(inputs, gate_up, w_down):
    features = w_down[0].shape[1]
    hidden = w_down[0].shape[0]
    rows = sum(x.shape[0] for x in inputs)

    def kernel(*refs):
        x_refs, refs = refs[: len(inputs)], refs[len(inputs) :]
        gu_refs, refs = refs[: len(gate_up)], refs[len(gate_up) :]
        down_refs, out_refs = refs[: len(w_down)], refs[len(w_down) :]
        mine = lax.axis_index("ep") * lax.axis_size("hd") + lax.axis_index("hd")
        joined = jnp.concatenate([x[...] for x in x_refs], axis=0)
        x = joined[:, :features]
        table = joined[:, features:].astype(jnp.float32)
        lane = lax.broadcasted_iota(jnp.int32, table.shape, 1)
        gate = jnp.sum(jnp.where(lane == mine, table, 0.0), axis=1, keepdims=True)
        total = None
        for gu, down in zip(gu_refs, down_refs):
            gate_part = lax.dot_general(
                x, gu[0], CONTRACT_LAST, preferred_element_type=jnp.float32
            )
            up_part = lax.dot_general(x, gu[1], CONTRACT_LAST, preferred_element_type=jnp.float32)
            activation = (gate_part / (1.0 + jnp.exp(-gate_part)) * up_part).astype(jnp.bfloat16)
            product = jnp.dot(activation, down[...], preferred_element_type=jnp.float32)
            total = product if total is None else total + product
        total = gate * total.astype(jnp.bfloat16).astype(jnp.float32)
        first = 0
        for out_ref in out_refs:
            out_ref[...] = total[first : first + out_ref.shape[0]]
            first += out_ref.shape[0]

    vmem = pl.BlockSpec(memory_space=pltpu.VMEM)
    operands = list(inputs) + list(gate_up) + list(w_down)
    return pl.pallas_call(
        kernel,
        out_shape=[jax.ShapeDtypeStruct((x.shape[0], features), jnp.float32) for x in inputs],
        in_specs=[vmem] * len(operands),
        out_specs=[vmem] * len(inputs),
        compiler_params=pltpu.CompilerParams(vmem_limit_bytes=16 * MIB),
        cost_estimate=pl.CostEstimate(
            flops=6 * rows * hidden * len(w_down) * features,
            bytes_accessed=6 * MIB,
            transcendentals=rows * hidden * len(w_down),
        ),
        name="apply_expert",
    )(*operands)


def chip_ring(n_ep, n_hd):
    if n_hd == 2:
        return [z * 2 for z in range(n_ep)] + [z * 2 + 1 for z in reversed(range(n_ep))]
    return list(range(n_ep * n_hd))


def add_share(came, share):
    def kernel(came_ref, share_ref, out_ref):
        total = came_ref[...].astype(jnp.float32) + share_ref[...]
        out_ref[...] = total.astype(jnp.bfloat16)

    shape = jax.ShapeDtypeStruct(share.shape, jnp.bfloat16)
    return small_kernel(kernel, [shape], [came, share], "add_share")[0]


def dense_experts(own, gate_up, w_down):
    axes = ("ep", "hd")
    walk = chip_ring(lax.axis_size("ep"), lax.axis_size("hd"))
    size = len(walk)
    ahead = [(walk[i], walk[(i + 1) % size]) for i in range(size)]
    back = [(b, a) for a, b in ahead]
    reach = size // 2
    behind, before, waiting = list(own), list(own), None
    outs = [None]
    for hop in range(1, reach + 1):
        behind[0] = lax.ppermute(behind[0], axes, ahead)
        before[1] = lax.ppermute(before[1], axes, back)
        if hop < reach:
            behind[1] = lax.ppermute(behind[1], axes, ahead)
            before[0] = lax.ppermute(before[0], axes, back)
        if waiting:
            out = apply_expert(waiting, gate_up, w_down)
            behind[0], out = lax.optimization_barrier((behind[0], out))
            outs.append(out)
        waiting = [behind[0], before[1]] + ([behind[1], before[0]] if hop < reach else [])
    outs.append(apply_expert(waiting, gate_up, w_down))
    to_back, to_ahead = [None, None], [None, None]
    for hop in range(reach, 0, -1):
        shares = outs[hop]
        for chunks, chunk, way, share in [
            (to_back, 0, back, 0),
            (to_ahead, 1, ahead, 1),
            (to_back, 1, back, 2),
            (to_ahead, 0, ahead, 3),
        ]:
            if share >= len(shares):
                continue
            if chunks[chunk] is None:
                sum_here = shares[share].astype(jnp.bfloat16)
            else:
                sum_here = add_share(chunks[chunk], shares[share])
            chunks[chunk] = lax.ppermute(sum_here, axes, way)
            if hop == min(2, reach) and share == 0:
                chunks[chunk], own = lax.optimization_barrier((chunks[chunk], own))
    return apply_expert(own, gate_up, w_down), to_back, to_ahead


def sparse_experts(widened, normed, gate_up, w_down, expert_ids, gates, features):
    half_width = normed.shape[1]
    pair_weights = gate_up[0].reshape(-1, features)
    hidden_units = w_down.shape[1]
    group_total = lax.axis_size("ep")
    group_experts = lax.axis_size("hd")
    all_experts = group_total * group_experts
    block_rows = expert_ids.shape[0]
    group_slots, expert_slots = block_sizes(block_rows, group_total, group_experts)
    chosen = (
        expert_ids[:, :, None] == jnp.arange(all_experts, dtype=jnp.int32)[None, None, :]
    ).astype(jnp.int32)
    named_count = jnp.sum(chosen, axis=1)
    earlier = jnp.cumsum(named_count, axis=0) - named_count
    slot_index = jnp.sum(chosen * earlier[:, None, :], axis=2)
    position = expert_ids * expert_slots + slot_index
    slot_columns = jnp.arange(all_experts * expert_slots, dtype=jnp.int32)
    gate_table = jnp.sum(
        jnp.where(
            position[:, :, None] == slot_columns[None, None, :],
            gates.astype(jnp.float32)[:, :, None],
            0.0,
        ),
        axis=1,
    ).astype(jnp.bfloat16)
    placed = (gate_table != 0).astype(jnp.bfloat16)
    outgoing = jnp.einsum("rq,rd->qd", placed, normed, preferred_element_type=jnp.float32).astype(
        jnp.bfloat16
    )
    outgoing = outgoing.reshape(all_experts, expert_slots, normed.shape[1])
    arrived = lax.all_to_all(outgoing, ("ep", "hd"), split_axis=0, concat_axis=0, tiled=True)
    lead_shape = arrived.shape[:-1]
    rows_in = arrived.reshape(-1, arrived.shape[-1])
    rows_in = lax.all_gather(rows_in, "sub", axis=1, tiled=True)
    projected_pair = jnp.einsum(
        "rd,fd->rf", rows_in, pair_weights, preferred_element_type=jnp.float32
    )
    activation = (
        jax.nn.silu(projected_pair[:, :hidden_units]) * projected_pair[:, hidden_units:]
    ).astype(jnp.bfloat16)
    partial_out = jnp.dot(activation, w_down[0], preferred_element_type=jnp.float32)
    expert_out = lax.psum_scatter(
        partial_out.astype(jnp.bfloat16), "sub", scatter_dimension=1, tiled=True
    )
    results = expert_out.reshape(lead_shape + (expert_out.shape[1],))
    returned = lax.all_to_all(results, ("ep", "hd"), split_axis=0, concat_axis=0, tiled=True)
    mixture = jnp.dot(
        gate_table,
        returned.reshape(all_experts * expert_slots, half_width),
        preferred_element_type=jnp.float32,
    )
    return (widened + mixture).astype(jnp.bfloat16)


def shards(
    queries,
    cache_keys,
    cache_values,
    page_len,
    new_keys,
    new_values,
    out_proj,
    residual,
    norm_gain,
    gate_up,
    w_down,
    expert_ids,
    gates,
):
    n_ep, n_hd, n_sub = lax.axis_size("ep"), lax.axis_size("hd"), lax.axis_size("sub")
    query_rows = queries.shape[0]
    heads_here = queries.shape[1] // HD
    kv_heads = max(1, heads_here // (QH // KVH))
    rows = query_rows // (n_hd * n_sub)
    features = norm_gain.shape[0]
    cache_rows = cache_keys.shape[0]
    all_experts = n_ep * n_hd * gate_up.shape[0]
    dense = (
        expert_ids.shape[1] == all_experts
        and gate_up.shape[0] == 1
        and n_ep * n_hd % 2 == 0
        and rows % 32 == 0
    )

    packed = pack_keys(
        cache_keys, cache_values, new_keys, new_values, page_len, kv_heads, heads_here
    )
    query_rows_here = choose_queries(queries.reshape(n_hd, n_sub, rows, heads_here * HD))
    reach = n_ep // 2
    up, down = list(packed), list(packed)
    arrived = [[(0, x)] for x in packed]
    states = [None] * kv_heads
    earlier = None
    for distance in range(reach + 1):
        stages = [[(hop, sub_copies(x)) for hop, x in blocks] for blocks in arrived]
        if distance == 0:
            out_proj, packed = lax.optimization_barrier((out_proj, packed))
            projections = sub_copies(out_proj)
        onward = [[] for _ in packed]
        if distance < reach:
            opposite = 2 * (distance + 1) == n_ep
            for kv in range(kv_heads):
                if not opposite or kv % 2 == 0:
                    up[kv] = lax.ppermute(up[kv], "ep", cycle(n_ep))
                    onward[kv].append((distance + 1, up[kv]))
                if not opposite or kv % 2 == 1:
                    down[kv] = lax.ppermute(down[kv], "ep", cycle(n_ep, n_ep - 1))
                    onward[kv].append((n_ep - distance - 1, down[kv]))
        for kv in range(kv_heads):
            finish = (projections, earlier) if distance == reach else None
            states[kv] = attend(
                query_rows_here,
                kv,
                stages[kv],
                states[kv],
                cache_rows,
                kv_heads,
                n_hd,
                2 if dense else 1,
                finish,
            )
            if finish:
                earlier = states[kv][0]
                continue
            came = [x for _, x in onward[kv]]
            came, states[kv] = lax.optimization_barrier((came, states[kv]))
            onward[kv] = [(hop, x) for (hop, _), x in zip(onward[kv], came)]
            for hop, x in onward[kv]:
                if hop == distance + 1:
                    up[kv] = x
                else:
                    down[kv] = x
        if distance == 0:
            residual, states[0] = lax.optimization_barrier((residual, states[0]))
            residual_parts = hand_over(split_rows(residual, n_sub))
            gate_table = gates_by_expert(expert_ids, gates, rows) if dense else None
        arrived = onward
    if dense:
        gate_up, w_down, states[-1] = lax.optimization_barrier((gate_up, w_down, states[-1]))
        gate_up_parts = sub_copies(gate_up[0])
        w_down_parts = sub_copies(w_down[0])
    parts = states[-1]
    if n_hd == 2:
        kept, sent = parts[: len(parts) // 2], parts[len(parts) // 2 :]
        came = [lax.ppermute(x, "hd", cycle(n_hd)) for x in sent]
    else:
        kept = [None]
        came = [lax.psum_scatter(parts[0], "hd", scatter_dimension=0, tiled=True)]
    hidden, normed = [], []
    for index, (kept_chunk, came_chunk) in enumerate(zip(kept, came)):
        pair = normalise(
            kept_chunk,
            came_chunk,
            residual_parts,
            norm_gain,
            gate_table,
            index * came_chunk.shape[0],
        )
        hidden.append(pair[0])
        normed.append(pair[1])
    if not dense:
        own_columns = [
            jnp.concatenate(by_sub(sub_exchange(x, 1)), axis=0) for x in (hidden[0], normed[0])
        ]
        return sparse_experts(
            own_columns[0].astype(jnp.float32),
            own_columns[1],
            gate_up,
            w_down,
            expert_ids,
            gates,
            features,
        )
    mine, to_back, to_ahead = dense_experts(normed, gate_up_parts, w_down_parts)
    return stack_rows(hand_over(add_up(hidden, mine, to_back, to_ahead, n_sub)))


def solution(mesh):
    return jax.shard_map(
        shards,
        mesh=mesh,
        in_specs=(
            P(("grp", "ep"), "hd"),
            P(("grp", "ep", "sub"), None),
            P(("grp", "ep", "sub"), None),
            P(("grp", "ep", "sub")),
            P(("grp", "ep", "sub"), None),
            P(("grp", "ep", "sub"), None),
            P("hd", "sub"),
            P(("grp", "ep", "hd"), "sub"),
            P(),
            P(("ep", "hd"), None, "sub", None),
            P(("ep", "hd"), "sub", None),
            P(("grp", "ep", "hd"), None),
            P(("grp", "ep", "hd"), None),
        ),
        out_specs=P(("grp", "ep", "hd"), "sub"),
        check_vma=False,
    )
```

```python
import functools
import math

import jax
import jax.numpy as jnp
from jax import lax
from jax.experimental import pallas as pl
from jax.experimental.pallas import tpu as pltpu
from jax.sharding import PartitionSpec as P

QH = 32
KVH = 4
HD = 128
GROUPS_ROW = 4
NEG_FILL = -1e30
EPSILON = 1e-06
MASK_ROWS = 16
LANES = 128
MIB = 1024 * 1024
CONTRACT_LAST = (((1,), (1,)), ((), ()))


def block_sizes(block_rows, group_total, experts_group):
    group_slots = min(block_rows, 3 * GROUPS_ROW * block_rows // (2 * group_total))
    return (group_slots, 2 * group_slots // experts_group)


def cycle(size, step=1):
    return [(i, (i + step) % size) for i in range(size)]


def sub_copies(x):
    size = lax.axis_size("sub")
    return [x] + [lax.ppermute(x, "sub", cycle(size, step)) for step in range(1, size)]


def by_sub(copies):
    size = len(copies)
    me = lax.axis_index("sub")
    ordered = []
    for target in range(size):
        value = copies[0]
        for step in range(1, size):
            value = jnp.where((me - step) % size == target, copies[step], value)
        ordered.append(value)
    return ordered


def sub_exchange(x, axis):
    size = lax.axis_size("sub")
    me = lax.axis_index("sub")
    length = x.shape[axis] // size

    def part(index):
        return lax.dynamic_slice_in_dim(x, index * length, length, axis)

    came = [part(me)]
    for step in range(1, size):
        came.append(lax.ppermute(part((me + step) % size), "sub", cycle(size, step)))
    return came


def pack_keys(cache_keys, cache_values, new_keys, new_values, page_len, kv_heads, heads_here):
    cache_rows, new_rows = cache_keys.shape[0], new_keys.shape[0]
    group_width = QH // KVH
    rows = cache_rows + new_rows + MASK_ROWS

    def kernel(page_ref, ck_ref, cv_ref, nk_ref, nv_ref, *out_refs):
        first = lax.axis_index("hd") * heads_here // group_width
        lane = lax.broadcasted_iota(jnp.int32, (MASK_ROWS, 2 * HD), 1)
        bias = jnp.where(lane < page_ref[0], 0.0, NEG_FILL).astype(jnp.bfloat16)
        for kv, out_ref in enumerate(out_refs):
            columns = pl.ds(pl.multiple_of((first + kv) * HD, HD), HD)
            out_ref[:cache_rows, :HD] = ck_ref[:, columns]
            out_ref[:cache_rows, HD:] = cv_ref[:, columns]
            out_ref[cache_rows : cache_rows + new_rows, :HD] = nk_ref[:, columns]
            out_ref[cache_rows : cache_rows + new_rows, HD:] = nv_ref[:, columns]
            out_ref[cache_rows + new_rows :, :] = bias

    vmem = pl.BlockSpec(memory_space=pltpu.VMEM)
    return pl.pallas_call(
        kernel,
        out_shape=[jax.ShapeDtypeStruct((rows, 2 * HD), cache_keys.dtype)] * kv_heads,
        in_specs=[pl.BlockSpec(memory_space=pltpu.SMEM)] + [vmem] * 4,
        out_specs=[vmem] * kv_heads,
        name="pack_keys",
    )(page_len, cache_keys, cache_values, new_keys, new_values)


def small_kernel(kernel, out_shape, operands, name):
    vmem = pl.BlockSpec(memory_space=pltpu.VMEM)
    return pl.pallas_call(
        kernel,
        out_shape=out_shape,
        in_specs=[vmem] * len(operands),
        out_specs=[vmem] * len(out_shape),
        compiler_params=pltpu.CompilerParams(vmem_limit_bytes=8 * MIB),
        cost_estimate=pl.CostEstimate(flops=MIB, bytes_accessed=MIB, transcendentals=0),
        name=name,
    )(*operands)


def hand_over(parts):
    size = len(parts)
    return [parts[0]] + [
        lax.ppermute(part, "sub", cycle(size, step)) for step, part in enumerate(parts) if step
    ]


def choose_queries(queries):
    n_hd, n_sub, rows, columns = queries.shape

    def kernel(in_ref, out_ref, sems):
        sub = lax.axis_index("sub")
        hd = lax.axis_index("hd")
        copies = []
        for j in range(n_hd):
            place = (hd + j) % n_hd if n_hd == 2 else j
            copies.append(
                pltpu.make_async_copy(
                    in_ref.at[place, sub], out_ref.at[pl.ds(j * rows, rows), :], sems.at[j]
                )
            )
            copies[-1].start()
        for copy in copies:
            copy.wait()

    return pl.pallas_call(
        kernel,
        out_shape=jax.ShapeDtypeStruct((n_hd * rows, columns), queries.dtype),
        in_specs=[pl.BlockSpec(memory_space=pltpu.HBM)],
        out_specs=pl.BlockSpec(memory_space=pltpu.VMEM),
        scratch_shapes=[pltpu.SemaphoreType.DMA((n_hd,))],
        compiler_params=pltpu.CompilerParams(vmem_limit_bytes=8 * MIB),
        name="choose_queries",
    )(queries)


def split_rows(residual, n_sub):
    rows, columns = residual.shape[0] // n_sub, residual.shape[1]

    def kernel(in_ref, *out_refs):
        sub = lax.axis_index("sub")
        for step, out_ref in enumerate(out_refs):
            first = pl.multiple_of((sub + step) % n_sub * rows, rows)
            out_ref[...] = in_ref[pl.ds(first, rows), :]

    shape = jax.ShapeDtypeStruct((rows, columns), residual.dtype)
    return small_kernel(kernel, [shape] * n_sub, [residual], "split_rows")


def gates_by_expert(expert_ids, gates, rows):
    choices, block_rows = expert_ids.shape[1], expert_ids.shape[0]

    def kernel(ids_ref, gates_ref, out_ref):
        sub = lax.axis_index("sub")
        expert = lax.broadcasted_iota(jnp.int32, (LANES, block_rows), 0)
        weights = gates_ref[...].astype(jnp.float32)
        ids = ids_ref[...]
        table = jnp.zeros((LANES, block_rows), jnp.float32)
        for k in range(choices):
            table = table + jnp.where(ids[k : k + 1, :] == expert, weights[k : k + 1, :], 0.0)
        table = table.T
        chosen = table[:rows]
        for place in range(1, block_rows // rows):
            chosen = jnp.where(sub == place, table[place * rows : (place + 1) * rows], chosen)
        out_ref[...] = chosen.astype(jnp.bfloat16)

    shape = jax.ShapeDtypeStruct((rows, LANES), jnp.bfloat16)
    return small_kernel(kernel, [shape], [expert_ids.T, gates.T], "gates_by_expert")[0]


def normalise(kept, came, residual_parts, gain, gate_table, first):
    n_sub = len(residual_parts)
    rows, width = came.shape[0], residual_parts[0].shape[1]
    chunk = slice(first, first + rows)
    features = n_sub * width
    extra = 0 if gate_table is None else LANES

    def kernel(*refs):
        refs = list(refs)
        kept_ref = refs.pop(0) if kept is not None else None
        came_ref = refs.pop(0)
        part_refs = [refs.pop(0) for _ in residual_parts]
        gain_ref = refs.pop(0)
        if extra:
            gate_ref = refs.pop(0)
        hidden_ref, normed_ref = refs
        sub = lax.axis_index("sub")
        hidden, places, squares = [], [], 0.0
        for step, part_ref in enumerate(part_refs):
            here = slice(step * width, (step + 1) * width)
            projected = came_ref[:, here].astype(jnp.float32)
            if kept is not None:
                projected = kept_ref[:, here] + projected
            value = (part_ref[chunk, :].astype(jnp.float32) + projected).astype(jnp.bfloat16)
            hidden.append(value)
            place = pl.ds(pl.multiple_of((sub - step) % n_sub * width, width), width)
            places.append(place)
            hidden_ref[:, place] = value
            wide = value.astype(jnp.float32)
            squares = squares + jnp.sum(wide * wide, axis=1, keepdims=True)
        scale = lax.rsqrt(squares / features + EPSILON)
        for value, place in zip(hidden, places):
            normed = value.astype(jnp.float32) * scale * gain_ref[:, place].astype(jnp.float32)
            normed_ref[:, place] = normed.astype(jnp.bfloat16)
        if extra:
            normed_ref[:, features:] = gate_ref[chunk, :]

    operands = ([kept] if kept is not None else []) + [came] + list(residual_parts)
    operands.append(gain.reshape(1, features))
    if extra:
        operands.append(gate_table)
    out_shape = [
        jax.ShapeDtypeStruct((rows, features), jnp.bfloat16),
        jax.ShapeDtypeStruct((rows, features + extra), jnp.bfloat16),
    ]
    return small_kernel(kernel, out_shape, operands, "normalise")


def add_up(hidden, mine, to_back, to_ahead, n_sub):
    chunks = len(hidden)
    rows, features = hidden[0].shape
    width = features // n_sub

    def kernel(*refs):
        terms, out_refs = refs[: 4 * chunks], refs[4 * chunks :]
        sub = lax.axis_index("sub")
        for step, out_ref in enumerate(out_refs):
            place = pl.ds(pl.multiple_of((sub + step) % n_sub * width, width), width)
            for chunk in range(chunks):
                hidden_ref, mine_ref, back_ref, ahead_ref = terms[chunk::chunks]
                mixture = mine_ref[:, place] + back_ref[:, place].astype(jnp.float32)
                mixture = mixture + ahead_ref[:, place].astype(jnp.float32)
                total = hidden_ref[:, place].astype(jnp.float32) + mixture
                out_ref[chunk * rows : (chunk + 1) * rows, :] = total.astype(jnp.bfloat16)

    shape = jax.ShapeDtypeStruct((chunks * rows, width), jnp.bfloat16)
    operands = [*hidden, *mine, *to_back, *to_ahead]
    return small_kernel(kernel, [shape] * n_sub, operands, "add_up")


def stack_rows(parts):
    n_sub = len(parts)
    rows, width = parts[0].shape

    def kernel(*refs):
        sub = lax.axis_index("sub")
        for step, part_ref in enumerate(refs[:-1]):
            first = pl.multiple_of((sub - step) % n_sub * rows, rows)
            refs[-1][pl.ds(first, rows), :] = part_ref[...]

    shape = jax.ShapeDtypeStruct((n_sub * rows, width), parts[0].dtype)
    return small_kernel(kernel, [shape], parts, "stack_rows")[0]


def attend(queries, kv, stages, state, cache_rows, kv_heads, n_hd, chunks, finish=None):
    all_rows, columns = queries.shape
    rows, n_sub = all_rows // n_hd, len(stages[0][1])
    blocks = [block for _, stage_blocks in stages for block in stage_blocks]
    origins = [(hop, step) for hop, _ in stages for step in range(n_sub)]
    per_kv = columns // HD // kv_heads
    stack = 2 if per_kv % 2 == 0 else 1
    part = stack * all_rows
    new_rows = blocks[0].shape[0] - cache_rows - MASK_ROWS
    keys = cache_rows + new_rows
    factor = math.log2(math.e) / math.sqrt(HD)
    relative = n_hd == 2
    last = finish is not None
    weights, earlier = finish if last else ([], None)
    head_columns = per_kv * HD
    final = last and kv == kv_heads - 1
    kept_rows = rows if relative else 0
    chunk_rows = rows // chunks if relative else all_rows

    def kernel(*refs):
        q_ref, refs = refs[0], refs[1:]
        block_refs, refs = refs[: len(blocks)], refs[len(blocks) :]
        if state is not None:
            (m_in, acc_in), refs = refs[:2], refs[2:]
        weight_refs, refs = refs[: len(weights)], refs[len(weights) :]
        if earlier is not None:
            earlier_ref, refs = refs[0], refs[1:]
        if last:
            results = len(out_shape)
            result_refs, refs = refs[:results], refs[results:]
            head_ref, refs = refs[0], refs[1:]
        else:
            m_out, acc_out = refs
        sub = lax.axis_index("sub")
        ep = lax.axis_index("ep")
        hd = lax.axis_index("hd")
        places = [(hd + j) % n_hd if relative else j for j in range(n_hd)]
        biases = []
        for (hop, step), block in zip(origins, block_refs):
            cache_bias = block[keys : keys + 1, :cache_rows].astype(jnp.float32)
            if hop == 0:
                key_id = ((sub - step) % n_sub) * new_rows + lax.broadcasted_iota(
                    jnp.int32, (rows, new_rows), 1
                )
                row_id = lax.broadcasted_iota(jnp.int32, (rows, new_rows), 0)
                seen = [
                    jnp.where(
                        key_id <= row_id + (place * n_sub + sub) * rows, 0.0, NEG_FILL
                    )
                    for place in places
                ]
                new_bias = jnp.concatenate(seen * stack, axis=0)
                cache_bias = jnp.broadcast_to(cache_bias, (part, cache_rows))
            else:
                new_bias = jnp.full(
                    (1, new_rows), jnp.where(ep >= hop, 0.0, NEG_FILL), jnp.float32
                )
            biases.append(jnp.concatenate([cache_bias, new_bias], axis=1))
        ones = jnp.ones((keys, HD), jnp.bfloat16)
        key_parts = [block[:keys, :HD] for block in block_refs]
        value_parts = [
            jnp.concatenate([block[:keys, HD:], ones], axis=1) for block in block_refs
        ]
        for index in range(per_kv // stack):
            here = slice(index * part, (index + 1) * part)
            heads = range(kv * per_kv + index * stack, kv * per_kv + (index + 1) * stack)
            q = jnp.concatenate([q_ref[:, h * HD : (h + 1) * HD] for h in heads], axis=0)
            terms = [
                lax.dot_general(q, k, CONTRACT_LAST, preferred_element_type=jnp.float32) * factor
                + bias
                for k, bias in zip(key_parts, biases)
            ]
            top = jnp.max(functools.reduce(jnp.maximum, terms), axis=1, keepdims=True)
            top = jnp.broadcast_to(top, (part, LANES))
            if state is not None:
                top_in = m_in[here, :]
                top = jnp.maximum(top, top_in)
            wide_top = jnp.concatenate([top] * (keys // LANES), axis=1)
            acc = None
            for term, v in zip(terms, value_parts):
                exp_terms = jnp.exp2(term - wide_top).astype(jnp.bfloat16)
                product = jnp.dot(exp_terms, v, preferred_element_type=jnp.float32)
                acc = product if acc is None else acc + product
            if state is not None:
                scale = jnp.exp2(top_in - top)
                acc = acc + jnp.concatenate([scale, scale], axis=1) * acc_in[here, :]
            if last:
                out = (acc[:, :HD] / acc[:, HD:]).astype(jnp.bfloat16)
                for s in range(stack):
                    first = (index * stack + s) * HD
                    head_ref[:, first : first + HD] = out[s * all_rows : (s + 1) * all_rows]
            else:
                m_out[here, :] = top
                acc_out[here, :] = acc
        if last:
            source = head_ref[...]
            width = weight_refs[0].shape[1]
            these = slice(kv * head_columns, (kv + 1) * head_columns)
            for i, weight_ref in enumerate(weight_refs):
                here = slice(i * width, (i + 1) * width)
                product = jnp.dot(
                    source, weight_ref[these, :], preferred_element_type=jnp.float32
                )
                if earlier is not None:
                    product = product + earlier_ref[:, here]
                if final:
                    for j, result_ref in enumerate(result_refs):
                        share = product[j * chunk_rows : (j + 1) * chunk_rows]
                        result_ref[:, here] = share.astype(result_ref.dtype)
                else:
                    result_refs[0][:, here] = product

    vmem = pl.BlockSpec(memory_space=pltpu.VMEM)
    scratch = []
    if last:
        features = sum(w.shape[1] for w in weights)
        if final:
            out_shape = [
                jax.ShapeDtypeStruct((chunk_rows, features), kind)
                for kind, count in [
                    (jnp.float32, kept_rows // chunk_rows),
                    (jnp.bfloat16, (all_rows - kept_rows) // chunk_rows),
                ]
                for _ in range(count)
            ]
        else:
            out_shape = (jax.ShapeDtypeStruct((all_rows, features), jnp.float32),)
        scratch = [pltpu.VMEM((all_rows, head_columns), jnp.bfloat16)]
    else:
        out_shape = (
            jax.ShapeDtypeStruct((per_kv * all_rows, LANES), jnp.float32),
            jax.ShapeDtypeStruct((per_kv * all_rows, 2 * HD), jnp.float32),
        )
    operands = [queries] + list(blocks) + (list(state) if state is not None else [])
    operands += list(weights)
    if earlier is not None:
        operands.append(earlier)
    scores = all_rows * per_kv * keys * len(blocks)
    return pl.pallas_call(
        kernel,
        out_shape=out_shape,
        in_specs=[vmem] * len(operands),
        out_specs=tuple(vmem for _ in out_shape),
        scratch_shapes=scratch,
        compiler_params=pltpu.CompilerParams(vmem_limit_bytes=16 * MIB),
        cost_estimate=pl.CostEstimate(
            flops=6 * scores * HD, bytes_accessed=4 * MIB, transcendentals=scores
        ),
        name="attend",
    )(*operands)


def apply_expert(inputs, gate_up, w_down):
    features = w_down[0].shape[1]
    hidden = w_down[0].shape[0]
    rows = sum(x.shape[0] for x in inputs)

    def kernel(*refs):
        x_refs, refs = refs[: len(inputs)], refs[len(inputs) :]
        gu_refs, refs = refs[: len(gate_up)], refs[len(gate_up) :]
        down_refs, out_refs = refs[: len(w_down)], refs[len(w_down) :]
        mine = lax.axis_index("ep") * lax.axis_size("hd") + lax.axis_index("hd")
        joined = jnp.concatenate([x[...] for x in x_refs], axis=0)
        x = joined[:, :features]
        table = joined[:, features:].astype(jnp.float32)
        lane = lax.broadcasted_iota(jnp.int32, table.shape, 1)
        gate = jnp.sum(jnp.where(lane == mine, table, 0.0), axis=1, keepdims=True)
        total = None
        for gu, down in zip(gu_refs, down_refs):
            gate_part = lax.dot_general(
                x, gu[0], CONTRACT_LAST, preferred_element_type=jnp.float32
            )
            up_part = lax.dot_general(x, gu[1], CONTRACT_LAST, preferred_element_type=jnp.float32)
            activation = (gate_part / (1.0 + jnp.exp(-gate_part)) * up_part).astype(jnp.bfloat16)
            product = jnp.dot(activation, down[...], preferred_element_type=jnp.float32)
            total = product if total is None else total + product
        total = gate * total.astype(jnp.bfloat16).astype(jnp.float32)
        first = 0
        for out_ref in out_refs:
            out_ref[...] = total[first : first + out_ref.shape[0]]
            first += out_ref.shape[0]

    vmem = pl.BlockSpec(memory_space=pltpu.VMEM)
    operands = list(inputs) + list(gate_up) + list(w_down)
    return pl.pallas_call(
        kernel,
        out_shape=[jax.ShapeDtypeStruct((x.shape[0], features), jnp.float32) for x in inputs],
        in_specs=[vmem] * len(operands),
        out_specs=[vmem] * len(inputs),
        compiler_params=pltpu.CompilerParams(vmem_limit_bytes=16 * MIB),
        cost_estimate=pl.CostEstimate(
            flops=6 * rows * hidden * len(w_down) * features,
            bytes_accessed=6 * MIB,
            transcendentals=rows * hidden * len(w_down),
        ),
        name="apply_expert",
    )(*operands)


def chip_ring(n_ep, n_hd):
    if n_hd == 2:
        return [z * 2 for z in range(n_ep)] + [z * 2 + 1 for z in reversed(range(n_ep))]
    return list(range(n_ep * n_hd))


def add_share(came, share):
    def kernel(came_ref, share_ref, out_ref):
        total = came_ref[...].astype(jnp.float32) + share_ref[...]
        out_ref[...] = total.astype(jnp.bfloat16)

    shape = jax.ShapeDtypeStruct(share.shape, jnp.bfloat16)
    return small_kernel(kernel, [shape], [came, share], "add_share")[0]


def dense_experts(own, gate_up, w_down):
    axes = ("ep", "hd")
    walk = chip_ring(lax.axis_size("ep"), lax.axis_size("hd"))
    size = len(walk)
    ahead = [(walk[i], walk[(i + 1) % size]) for i in range(size)]
    back = [(b, a) for a, b in ahead]
    reach = size // 2
    behind, before, waiting = list(own), list(own), None
    outs = [None]
    for hop in range(1, reach + 1):
        behind[0] = lax.ppermute(behind[0], axes, ahead)
        before[1] = lax.ppermute(before[1], axes, back)
        if hop < reach:
            behind[1] = lax.ppermute(behind[1], axes, ahead)
            before[0] = lax.ppermute(before[0], axes, back)
        if waiting:
            out = apply_expert(waiting, gate_up, w_down)
            behind[0], out = lax.optimization_barrier((behind[0], out))
            outs.append(out)
        waiting = [behind[0], before[1]] + ([behind[1], before[0]] if hop < reach else [])
    outs.append(apply_expert(waiting, gate_up, w_down))
    to_back, to_ahead = [None, None], [None, None]
    for hop in range(reach, 0, -1):
        shares = outs[hop]
        for chunks, chunk, way, share in [
            (to_back, 0, back, 0),
            (to_ahead, 1, ahead, 1),
            (to_back, 1, back, 2),
            (to_ahead, 0, ahead, 3),
        ]:
            if share >= len(shares):
                continue
            if chunks[chunk] is None:
                sum_here = shares[share].astype(jnp.bfloat16)
            else:
                sum_here = add_share(chunks[chunk], shares[share])
            chunks[chunk] = lax.ppermute(sum_here, axes, way)
            if hop == min(2, reach) and share == 0:
                chunks[chunk], own = lax.optimization_barrier((chunks[chunk], own))
    return apply_expert(own, gate_up, w_down), to_back, to_ahead


def sparse_experts(widened, normed, gate_up, w_down, expert_ids, gates, features):
    half_width = normed.shape[1]
    pair_weights = gate_up[0].reshape(-1, features)
    hidden_units = w_down.shape[1]
    group_total = lax.axis_size("ep")
    group_experts = lax.axis_size("hd")
    all_experts = group_total * group_experts
    block_rows = expert_ids.shape[0]
    group_slots, expert_slots = block_sizes(block_rows, group_total, group_experts)
    chosen = (
        expert_ids[:, :, None] == jnp.arange(all_experts, dtype=jnp.int32)[None, None, :]
    ).astype(jnp.int32)
    named_count = jnp.sum(chosen, axis=1)
    earlier = jnp.cumsum(named_count, axis=0) - named_count
    slot_index = jnp.sum(chosen * earlier[:, None, :], axis=2)
    position = expert_ids * expert_slots + slot_index
    slot_columns = jnp.arange(all_experts * expert_slots, dtype=jnp.int32)
    gate_table = jnp.sum(
        jnp.where(
            position[:, :, None] == slot_columns[None, None, :],
            gates.astype(jnp.float32)[:, :, None],
            0.0,
        ),
        axis=1,
    ).astype(jnp.bfloat16)
    placed = (gate_table != 0).astype(jnp.bfloat16)
    outgoing = jnp.einsum("rq,rd->qd", placed, normed, preferred_element_type=jnp.float32).astype(
        jnp.bfloat16
    )
    outgoing = outgoing.reshape(all_experts, expert_slots, normed.shape[1])
    arrived = lax.all_to_all(outgoing, ("ep", "hd"), split_axis=0, concat_axis=0, tiled=True)
    lead_shape = arrived.shape[:-1]
    rows_in = arrived.reshape(-1, arrived.shape[-1])
    rows_in = lax.all_gather(rows_in, "sub", axis=1, tiled=True)
    projected_pair = jnp.einsum(
        "rd,fd->rf", rows_in, pair_weights, preferred_element_type=jnp.float32
    )
    activation = (
        jax.nn.silu(projected_pair[:, :hidden_units]) * projected_pair[:, hidden_units:]
    ).astype(jnp.bfloat16)
    partial_out = jnp.dot(activation, w_down[0], preferred_element_type=jnp.float32)
    expert_out = lax.psum_scatter(
        partial_out.astype(jnp.bfloat16), "sub", scatter_dimension=1, tiled=True
    )
    results = expert_out.reshape(lead_shape + (expert_out.shape[1],))
    returned = lax.all_to_all(results, ("ep", "hd"), split_axis=0, concat_axis=0, tiled=True)
    mixture = jnp.dot(
        gate_table,
        returned.reshape(all_experts * expert_slots, half_width),
        preferred_element_type=jnp.float32,
    )
    return (widened + mixture).astype(jnp.bfloat16)


def shards(
    queries,
    cache_keys,
    cache_values,
    page_len,
    new_keys,
    new_values,
    out_proj,
    residual,
    norm_gain,
    gate_up,
    w_down,
    expert_ids,
    gates,
):
    n_ep, n_hd, n_sub = lax.axis_size("ep"), lax.axis_size("hd"), lax.axis_size("sub")
    query_rows = queries.shape[0]
    heads_here = queries.shape[1] // HD
    kv_heads = max(1, heads_here // (QH // KVH))
    rows = query_rows // (n_hd * n_sub)
    features = norm_gain.shape[0]
    cache_rows = cache_keys.shape[0]
    all_experts = n_ep * n_hd * gate_up.shape[0]
    dense = (
        expert_ids.shape[1] == all_experts
        and gate_up.shape[0] == 1
        and n_ep * n_hd % 2 == 0
        and rows % 32 == 0
    )

    packed = pack_keys(
        cache_keys, cache_values, new_keys, new_values, page_len, kv_heads, heads_here
    )
    query_rows_here = choose_queries(queries.reshape(n_hd, n_sub, rows, heads_here * HD))
    reach = n_ep // 2
    up, down = list(packed), list(packed)
    arrived = [[(0, x)] for x in packed]
    states = [None] * kv_heads
    earlier = None
    for distance in range(reach + 1):
        stages = [[(hop, sub_copies(x)) for hop, x in blocks] for blocks in arrived]
        if distance == 0:
            out_proj, packed = lax.optimization_barrier((out_proj, packed))
            projections = sub_copies(out_proj)
        if distance == reach and dense:
            blocks = [x for kv_stages in stages for _, x in kv_stages]
            gate_up, w_down, blocks = lax.optimization_barrier((gate_up, w_down, blocks))
            stages = [
                [(hop, blocks.pop(0)) for hop, _ in kv_stages] for kv_stages in stages
            ]
            gate_up_parts = sub_copies(gate_up[0])
            w_down_parts = sub_copies(w_down[0])
        onward = [[] for _ in packed]
        if distance < reach:
            opposite = 2 * (distance + 1) == n_ep
            for kv in range(kv_heads):
                if not opposite or kv % 2 == 0:
                    up[kv] = lax.ppermute(up[kv], "ep", cycle(n_ep))
                    onward[kv].append((distance + 1, up[kv]))
                if not opposite or kv % 2 == 1:
                    down[kv] = lax.ppermute(down[kv], "ep", cycle(n_ep, n_ep - 1))
                    onward[kv].append((n_ep - distance - 1, down[kv]))
        for kv in range(kv_heads):
            finish = (projections, earlier) if distance == reach else None
            states[kv] = attend(
                query_rows_here,
                kv,
                stages[kv],
                states[kv],
                cache_rows,
                kv_heads,
                n_hd,
                2 if dense else 1,
                finish,
            )
            if finish:
                earlier = states[kv][0]
                continue
            came = [x for _, x in onward[kv]]
            came, states[kv] = lax.optimization_barrier((came, states[kv]))
            onward[kv] = [(hop, x) for (hop, _), x in zip(onward[kv], came)]
            for hop, x in onward[kv]:
                if hop == distance + 1:
                    up[kv] = x
                else:
                    down[kv] = x
        if distance == 0:
            residual, states[0] = lax.optimization_barrier((residual, states[0]))
            residual_parts = hand_over(split_rows(residual, n_sub))
            gate_table = gates_by_expert(expert_ids, gates, rows) if dense else None
        arrived = onward
    parts = states[-1]
    if n_hd == 2:
        kept, sent = parts[: len(parts) // 2], parts[len(parts) // 2 :]
        came = [lax.ppermute(x, "hd", cycle(n_hd)) for x in sent]
    else:
        kept = [None]
        came = [lax.psum_scatter(parts[0], "hd", scatter_dimension=0, tiled=True)]
    hidden, normed = [], []
    for index, (kept_chunk, came_chunk) in enumerate(zip(kept, came)):
        pair = normalise(
            kept_chunk,
            came_chunk,
            residual_parts,
            norm_gain,
            gate_table,
            index * came_chunk.shape[0],
        )
        hidden.append(pair[0])
        normed.append(pair[1])
    if not dense:
        own_columns = [
            jnp.concatenate(by_sub(sub_exchange(x, 1)), axis=0) for x in (hidden[0], normed[0])
        ]
        return sparse_experts(
            own_columns[0].astype(jnp.float32),
            own_columns[1],
            gate_up,
            w_down,
            expert_ids,
            gates,
            features,
        )
    mine, to_back, to_ahead = dense_experts(normed, gate_up_parts, w_down_parts)
    return stack_rows(hand_over(add_up(hidden, mine, to_back, to_ahead, n_sub)))


def solution(mesh):
    return jax.shard_map(
        shards,
        mesh=mesh,
        in_specs=(
            P(("grp", "ep"), "hd"),
            P(("grp", "ep", "sub"), None),
            P(("grp", "ep", "sub"), None),
            P(("grp", "ep", "sub")),
            P(("grp", "ep", "sub"), None),
            P(("grp", "ep", "sub"), None),
            P("hd", "sub"),
            P(("grp", "ep", "hd"), "sub"),
            P(),
            P(("ep", "hd"), None, "sub", None),
            P(("ep", "hd"), "sub", None),
            P(("grp", "ep", "hd"), None),
            P(("grp", "ep", "hd"), None),
        ),
        out_specs=P(("grp", "ep", "hd"), "sub"),
        check_vma=False,
    )
```

```python
import functools
import math

import jax
import jax.numpy as jnp
from jax import lax
from jax.experimental import pallas as pl
from jax.experimental.pallas import tpu as pltpu
from jax.sharding import PartitionSpec as P

QH = 32
KVH = 4
HD = 128
GROUPS_ROW = 4
NEG_FILL = -1e30
EPSILON = 1e-06
MASK_ROWS = 16
LANES = 128
MIB = 1024 * 1024
CONTRACT_LAST = (((1,), (1,)), ((), ()))


def block_sizes(block_rows, group_total, experts_group):
    group_slots = min(block_rows, 3 * GROUPS_ROW * block_rows // (2 * group_total))
    return (group_slots, 2 * group_slots // experts_group)


def cycle(size, step=1):
    return [(i, (i + step) % size) for i in range(size)]


def sub_copies(x):
    size = lax.axis_size("sub")
    return [x] + [lax.ppermute(x, "sub", cycle(size, step)) for step in range(1, size)]


def by_sub(copies):
    size = len(copies)
    me = lax.axis_index("sub")
    ordered = []
    for target in range(size):
        value = copies[0]
        for step in range(1, size):
            value = jnp.where((me - step) % size == target, copies[step], value)
        ordered.append(value)
    return ordered


def sub_exchange(x, axis):
    size = lax.axis_size("sub")
    me = lax.axis_index("sub")
    length = x.shape[axis] // size

    def part(index):
        return lax.dynamic_slice_in_dim(x, index * length, length, axis)

    came = [part(me)]
    for step in range(1, size):
        came.append(lax.ppermute(part((me + step) % size), "sub", cycle(size, step)))
    return came


def pack_keys(cache_keys, cache_values, new_keys, new_values, page_len, kv_heads, heads_here):
    cache_rows, new_rows = cache_keys.shape[0], new_keys.shape[0]
    group_width = QH // KVH
    rows = cache_rows + new_rows + MASK_ROWS

    def kernel(page_ref, ck_ref, cv_ref, nk_ref, nv_ref, *out_refs):
        first = lax.axis_index("hd") * heads_here // group_width
        lane = lax.broadcasted_iota(jnp.int32, (MASK_ROWS, 2 * HD), 1)
        bias = jnp.where(lane < page_ref[0], 0.0, NEG_FILL).astype(jnp.bfloat16)
        for kv, out_ref in enumerate(out_refs):
            columns = pl.ds(pl.multiple_of((first + kv) * HD, HD), HD)
            out_ref[:cache_rows, :HD] = ck_ref[:, columns]
            out_ref[:cache_rows, HD:] = cv_ref[:, columns]
            out_ref[cache_rows : cache_rows + new_rows, :HD] = nk_ref[:, columns]
            out_ref[cache_rows : cache_rows + new_rows, HD:] = nv_ref[:, columns]
            out_ref[cache_rows + new_rows :, :] = bias

    vmem = pl.BlockSpec(memory_space=pltpu.VMEM)
    return pl.pallas_call(
        kernel,
        out_shape=[jax.ShapeDtypeStruct((rows, 2 * HD), cache_keys.dtype)] * kv_heads,
        in_specs=[pl.BlockSpec(memory_space=pltpu.SMEM)] + [vmem] * 4,
        out_specs=[vmem] * kv_heads,
        name="pack_keys",
    )(page_len, cache_keys, cache_values, new_keys, new_values)


def small_kernel(kernel, out_shape, operands, name):
    vmem = pl.BlockSpec(memory_space=pltpu.VMEM)
    return pl.pallas_call(
        kernel,
        out_shape=out_shape,
        in_specs=[vmem] * len(operands),
        out_specs=[vmem] * len(out_shape),
        compiler_params=pltpu.CompilerParams(vmem_limit_bytes=8 * MIB),
        cost_estimate=pl.CostEstimate(flops=MIB, bytes_accessed=MIB, transcendentals=0),
        name=name,
    )(*operands)


def hand_over(parts):
    size = len(parts)
    return [parts[0]] + [
        lax.ppermute(part, "sub", cycle(size, step)) for step, part in enumerate(parts) if step
    ]


def choose_queries(queries):
    n_hd, n_sub, rows, columns = queries.shape

    def kernel(in_ref, out_ref, sems):
        sub = lax.axis_index("sub")
        hd = lax.axis_index("hd")
        copies = []
        for j in range(n_hd):
            place = (hd + j) % n_hd if n_hd == 2 else j
            copies.append(
                pltpu.make_async_copy(
                    in_ref.at[place, sub], out_ref.at[pl.ds(j * rows, rows), :], sems.at[j]
                )
            )
            copies[-1].start()
        for copy in copies:
            copy.wait()

    return pl.pallas_call(
        kernel,
        out_shape=jax.ShapeDtypeStruct((n_hd * rows, columns), queries.dtype),
        in_specs=[pl.BlockSpec(memory_space=pltpu.HBM)],
        out_specs=pl.BlockSpec(memory_space=pltpu.VMEM),
        scratch_shapes=[pltpu.SemaphoreType.DMA((n_hd,))],
        compiler_params=pltpu.CompilerParams(vmem_limit_bytes=8 * MIB),
        name="choose_queries",
    )(queries)


def split_rows(residual, n_sub):
    rows, columns = residual.shape[0] // n_sub, residual.shape[1]

    def kernel(in_ref, *out_refs):
        sub = lax.axis_index("sub")
        for step, out_ref in enumerate(out_refs):
            first = pl.multiple_of((sub + step) % n_sub * rows, rows)
            out_ref[...] = in_ref[pl.ds(first, rows), :]

    shape = jax.ShapeDtypeStruct((rows, columns), residual.dtype)
    return small_kernel(kernel, [shape] * n_sub, [residual], "split_rows")


def gates_by_expert(expert_ids, gates, rows):
    choices, block_rows = expert_ids.shape[1], expert_ids.shape[0]

    def kernel(ids_ref, gates_ref, out_ref):
        sub = lax.axis_index("sub")
        expert = lax.broadcasted_iota(jnp.int32, (LANES, block_rows), 0)
        weights = gates_ref[...].astype(jnp.float32)
        ids = ids_ref[...]
        table = jnp.zeros((LANES, block_rows), jnp.float32)
        for k in range(choices):
            table = table + jnp.where(ids[k : k + 1, :] == expert, weights[k : k + 1, :], 0.0)
        table = table.T
        chosen = table[:rows]
        for place in range(1, block_rows // rows):
            chosen = jnp.where(sub == place, table[place * rows : (place + 1) * rows], chosen)
        out_ref[...] = chosen.astype(jnp.bfloat16)

    shape = jax.ShapeDtypeStruct((rows, LANES), jnp.bfloat16)
    return small_kernel(kernel, [shape], [expert_ids.T, gates.T], "gates_by_expert")[0]


def normalise(kept, came, residual_parts, gain, gate_table, first):
    n_sub = len(residual_parts)
    rows, width = came.shape[0], residual_parts[0].shape[1]
    chunk = slice(first, first + rows)
    features = n_sub * width
    extra = 0 if gate_table is None else LANES

    def kernel(*refs):
        refs = list(refs)
        kept_ref = refs.pop(0) if kept is not None else None
        came_ref = refs.pop(0)
        part_refs = [refs.pop(0) for _ in residual_parts]
        gain_ref = refs.pop(0)
        if extra:
            gate_ref = refs.pop(0)
        hidden_ref, normed_ref = refs
        sub = lax.axis_index("sub")
        hidden, places, squares = [], [], 0.0
        for step, part_ref in enumerate(part_refs):
            here = slice(step * width, (step + 1) * width)
            projected = came_ref[:, here].astype(jnp.float32)
            if kept is not None:
                projected = kept_ref[:, here] + projected
            value = (part_ref[chunk, :].astype(jnp.float32) + projected).astype(jnp.bfloat16)
            hidden.append(value)
            place = pl.ds(pl.multiple_of((sub - step) % n_sub * width, width), width)
            places.append(place)
            hidden_ref[:, place] = value
            wide = value.astype(jnp.float32)
            squares = squares + jnp.sum(wide * wide, axis=1, keepdims=True)
        scale = lax.rsqrt(squares / features + EPSILON)
        for value, place in zip(hidden, places):
            normed = value.astype(jnp.float32) * scale * gain_ref[:, place].astype(jnp.float32)
            normed_ref[:, place] = normed.astype(jnp.bfloat16)
        if extra:
            normed_ref[:, features:] = gate_ref[chunk, :]

    operands = ([kept] if kept is not None else []) + [came] + list(residual_parts)
    operands.append(gain.reshape(1, features))
    if extra:
        operands.append(gate_table)
    out_shape = [
        jax.ShapeDtypeStruct((rows, features), jnp.bfloat16),
        jax.ShapeDtypeStruct((rows, features + extra), jnp.bfloat16),
    ]
    return small_kernel(kernel, out_shape, operands, "normalise")


def add_up(hidden, mine, to_back, to_ahead, n_sub):
    chunks = len(hidden)
    rows, features = hidden[0].shape
    width = features // n_sub

    def kernel(*refs):
        terms, out_refs = refs[: 4 * chunks], refs[4 * chunks :]
        sub = lax.axis_index("sub")
        for step, out_ref in enumerate(out_refs):
            place = pl.ds(pl.multiple_of((sub + step) % n_sub * width, width), width)
            for chunk in range(chunks):
                hidden_ref, mine_ref, back_ref, ahead_ref = terms[chunk::chunks]
                mixture = mine_ref[:, place] + back_ref[:, place].astype(jnp.float32)
                mixture = mixture + ahead_ref[:, place].astype(jnp.float32)
                total = hidden_ref[:, place].astype(jnp.float32) + mixture
                out_ref[chunk * rows : (chunk + 1) * rows, :] = total.astype(jnp.bfloat16)

    shape = jax.ShapeDtypeStruct((chunks * rows, width), jnp.bfloat16)
    operands = [*hidden, *mine, *to_back, *to_ahead]
    return small_kernel(kernel, [shape] * n_sub, operands, "add_up")


def stack_rows(parts):
    n_sub = len(parts)
    rows, width = parts[0].shape

    def kernel(*refs):
        sub = lax.axis_index("sub")
        for step, part_ref in enumerate(refs[:-1]):
            first = pl.multiple_of((sub - step) % n_sub * rows, rows)
            refs[-1][pl.ds(first, rows), :] = part_ref[...]

    shape = jax.ShapeDtypeStruct((n_sub * rows, width), parts[0].dtype)
    return small_kernel(kernel, [shape], parts, "stack_rows")[0]


def attend(queries, kv, stages, state, cache_rows, kv_heads, n_hd, chunks, finish=None):
    all_rows, columns = queries.shape
    rows, n_sub = all_rows // n_hd, len(stages[0][1])
    blocks = [block for _, stage_blocks in stages for block in stage_blocks]
    origins = [(hop, step) for hop, _ in stages for step in range(n_sub)]
    per_kv = columns // HD // kv_heads
    stack = 2 if per_kv % 2 == 0 else 1
    part = stack * all_rows
    new_rows = blocks[0].shape[0] - cache_rows - MASK_ROWS
    keys = cache_rows + new_rows
    factor = math.log2(math.e) / math.sqrt(HD)
    relative = n_hd == 2
    last = finish is not None
    weights, earlier = finish if last else ([], None)
    head_columns = per_kv * HD
    final = last and kv == kv_heads - 1
    kept_rows = rows if relative else 0
    chunk_rows = rows // chunks if relative else all_rows

    def kernel(*refs):
        q_ref, refs = refs[0], refs[1:]
        block_refs, refs = refs[: len(blocks)], refs[len(blocks) :]
        if state is not None:
            (m_in, acc_in), refs = refs[:2], refs[2:]
        weight_refs, refs = refs[: len(weights)], refs[len(weights) :]
        if earlier is not None:
            earlier_ref, refs = refs[0], refs[1:]
        if last:
            results = len(out_shape)
            result_refs, refs = refs[:results], refs[results:]
            head_ref, refs = refs[0], refs[1:]
        else:
            m_out, acc_out = refs
        sub = lax.axis_index("sub")
        ep = lax.axis_index("ep")
        hd = lax.axis_index("hd")
        places = [(hd + j) % n_hd if relative else j for j in range(n_hd)]
        biases = []
        for (hop, step), block in zip(origins, block_refs):
            cache_bias = block[keys : keys + 1, :cache_rows].astype(jnp.float32)
            if hop == 0:
                key_id = ((sub - step) % n_sub) * new_rows + lax.broadcasted_iota(
                    jnp.int32, (rows, new_rows), 1
                )
                row_id = lax.broadcasted_iota(jnp.int32, (rows, new_rows), 0)
                seen = [
                    jnp.where(
                        key_id <= row_id + (place * n_sub + sub) * rows, 0.0, NEG_FILL
                    )
                    for place in places
                ]
                new_bias = jnp.concatenate(seen * stack, axis=0)
                cache_bias = jnp.broadcast_to(cache_bias, (part, cache_rows))
            else:
                new_bias = jnp.full(
                    (1, new_rows), jnp.where(ep >= hop, 0.0, NEG_FILL), jnp.float32
                )
            biases.append(jnp.concatenate([cache_bias, new_bias], axis=1))
        ones = jnp.ones((keys, HD), jnp.bfloat16)
        key_parts = [block[:keys, :HD] for block in block_refs]
        value_parts = [
            jnp.concatenate([block[:keys, HD:], ones], axis=1) for block in block_refs
        ]
        for index in range(per_kv // stack):
            here = slice(index * part, (index + 1) * part)
            heads = range(kv * per_kv + index * stack, kv * per_kv + (index + 1) * stack)
            q = jnp.concatenate([q_ref[:, h * HD : (h + 1) * HD] for h in heads], axis=0)
            terms = [
                lax.dot_general(q, k, CONTRACT_LAST, preferred_element_type=jnp.float32) * factor
                + bias
                for k, bias in zip(key_parts, biases)
            ]
            top = jnp.max(functools.reduce(jnp.maximum, terms), axis=1, keepdims=True)
            top = jnp.broadcast_to(top, (part, LANES))
            if state is not None:
                top_in = m_in[here, :]
                top = jnp.maximum(top, top_in)
            wide_top = jnp.concatenate([top] * (keys // LANES), axis=1)
            acc = None
            for term, v in zip(terms, value_parts):
                exp_terms = jnp.exp2(term - wide_top).astype(jnp.bfloat16)
                product = jnp.dot(exp_terms, v, preferred_element_type=jnp.float32)
                acc = product if acc is None else acc + product
            if state is not None:
                scale = jnp.exp2(top_in - top)
                acc = acc + jnp.concatenate([scale, scale], axis=1) * acc_in[here, :]
            if last:
                out = (acc[:, :HD] / acc[:, HD:]).astype(jnp.bfloat16)
                for s in range(stack):
                    first = (index * stack + s) * HD
                    head_ref[:, first : first + HD] = out[s * all_rows : (s + 1) * all_rows]
            else:
                m_out[here, :] = top
                acc_out[here, :] = acc
        if last:
            source = head_ref[...]
            width = weight_refs[0].shape[1]
            these = slice(kv * head_columns, (kv + 1) * head_columns)
            for i, weight_ref in enumerate(weight_refs):
                here = slice(i * width, (i + 1) * width)
                product = jnp.dot(
                    source, weight_ref[these, :], preferred_element_type=jnp.float32
                )
                if earlier is not None:
                    product = product + earlier_ref[:, here]
                if final:
                    for j, result_ref in enumerate(result_refs):
                        share = product[j * chunk_rows : (j + 1) * chunk_rows]
                        result_ref[:, here] = share.astype(result_ref.dtype)
                else:
                    result_refs[0][:, here] = product

    vmem = pl.BlockSpec(memory_space=pltpu.VMEM)
    scratch = []
    if last:
        features = sum(w.shape[1] for w in weights)
        if final:
            out_shape = [
                jax.ShapeDtypeStruct((chunk_rows, features), kind)
                for kind, count in [
                    (jnp.float32, kept_rows // chunk_rows),
                    (jnp.bfloat16, (all_rows - kept_rows) // chunk_rows),
                ]
                for _ in range(count)
            ]
        else:
            out_shape = (jax.ShapeDtypeStruct((all_rows, features), jnp.float32),)
        scratch = [pltpu.VMEM((all_rows, head_columns), jnp.bfloat16)]
    else:
        out_shape = (
            jax.ShapeDtypeStruct((per_kv * all_rows, LANES), jnp.float32),
            jax.ShapeDtypeStruct((per_kv * all_rows, 2 * HD), jnp.float32),
        )
    operands = [queries] + list(blocks) + (list(state) if state is not None else [])
    operands += list(weights)
    if earlier is not None:
        operands.append(earlier)
    scores = all_rows * per_kv * keys * len(blocks)
    return pl.pallas_call(
        kernel,
        out_shape=out_shape,
        in_specs=[vmem] * len(operands),
        out_specs=tuple(vmem for _ in out_shape),
        scratch_shapes=scratch,
        compiler_params=pltpu.CompilerParams(vmem_limit_bytes=16 * MIB),
        cost_estimate=pl.CostEstimate(
            flops=6 * scores * HD, bytes_accessed=4 * MIB, transcendentals=scores
        ),
        name="attend",
    )(*operands)


def apply_expert(inputs, gate_up, w_down):
    features = w_down[0].shape[1]
    hidden = w_down[0].shape[0]
    rows = sum(x.shape[0] for x in inputs)

    def kernel(*refs):
        x_refs, refs = refs[: len(inputs)], refs[len(inputs) :]
        gu_refs, refs = refs[: len(gate_up)], refs[len(gate_up) :]
        down_refs, out_refs = refs[: len(w_down)], refs[len(w_down) :]
        mine = lax.axis_index("ep") * lax.axis_size("hd") + lax.axis_index("hd")
        joined = jnp.concatenate([x[...] for x in x_refs], axis=0)
        x = joined[:, :features]
        table = joined[:, features:].astype(jnp.float32)
        lane = lax.broadcasted_iota(jnp.int32, table.shape, 1)
        gate = jnp.sum(jnp.where(lane == mine, table, 0.0), axis=1, keepdims=True)
        total = None
        for gu, down in zip(gu_refs, down_refs):
            gate_part = lax.dot_general(
                x, gu[0], CONTRACT_LAST, preferred_element_type=jnp.float32
            )
            up_part = lax.dot_general(x, gu[1], CONTRACT_LAST, preferred_element_type=jnp.float32)
            activation = (gate_part / (1.0 + jnp.exp(-gate_part)) * up_part).astype(jnp.bfloat16)
            product = jnp.dot(activation, down[...], preferred_element_type=jnp.float32)
            total = product if total is None else total + product
        total = gate * total.astype(jnp.bfloat16).astype(jnp.float32)
        first = 0
        for out_ref in out_refs:
            out_ref[...] = total[first : first + out_ref.shape[0]]
            first += out_ref.shape[0]

    vmem = pl.BlockSpec(memory_space=pltpu.VMEM)
    operands = list(inputs) + list(gate_up) + list(w_down)
    return pl.pallas_call(
        kernel,
        out_shape=[jax.ShapeDtypeStruct((x.shape[0], features), jnp.float32) for x in inputs],
        in_specs=[vmem] * len(operands),
        out_specs=[vmem] * len(inputs),
        compiler_params=pltpu.CompilerParams(vmem_limit_bytes=16 * MIB),
        cost_estimate=pl.CostEstimate(
            flops=6 * rows * hidden * len(w_down) * features,
            bytes_accessed=6 * MIB,
            transcendentals=rows * hidden * len(w_down),
        ),
        name="apply_expert",
    )(*operands)


def chip_ring(n_ep, n_hd):
    if n_hd == 2:
        return [z * 2 for z in range(n_ep)] + [z * 2 + 1 for z in reversed(range(n_ep))]
    return list(range(n_ep * n_hd))


def add_share(came, share):
    def kernel(came_ref, share_ref, out_ref):
        total = came_ref[...].astype(jnp.float32) + share_ref[...]
        out_ref[...] = total.astype(jnp.bfloat16)

    shape = jax.ShapeDtypeStruct(share.shape, jnp.bfloat16)
    return small_kernel(kernel, [shape], [came, share], "add_share")[0]


def dense_experts(own, gate_up, w_down):
    axes = ("ep", "hd", "sub")
    walk = chip_ring(lax.axis_size("ep"), lax.axis_size("hd"))
    size, n_sub = len(walk), lax.axis_size("sub")
    ahead = [
        (walk[i] * n_sub + sub, walk[(i + 1) % size] * n_sub + (sub + 1) % n_sub)
        for i in range(size)
        for sub in range(n_sub)
    ]
    back = [(b, a) for a, b in ahead]
    reach = size // 2
    behind, before, waiting = list(own), list(own), None
    outs = [None]
    for hop in range(1, reach + 1):
        behind[0] = lax.ppermute(behind[0], axes, ahead)
        before[1] = lax.ppermute(before[1], axes, back)
        if hop < reach:
            behind[1] = lax.ppermute(behind[1], axes, ahead)
            before[0] = lax.ppermute(before[0], axes, back)
        if waiting:
            out = apply_expert(waiting, gate_up, w_down)
            late = int(hop < reach)
            behind[late], out = lax.optimization_barrier((behind[late], out))
            outs.append(out)
        waiting = [behind[0], before[1]] + ([behind[1], before[0]] if hop < reach else [])
    outs.append(apply_expert(waiting, gate_up, w_down))
    to_back, to_ahead = [None, None], [None, None]
    for hop in range(reach, 0, -1):
        shares = outs[hop]
        for chunks, chunk, way, share in [
            (to_back, 0, back, 0),
            (to_ahead, 1, ahead, 1),
            (to_back, 1, back, 2),
            (to_ahead, 0, ahead, 3),
        ]:
            if share >= len(shares):
                continue
            if chunks[chunk] is None:
                sum_here = shares[share].astype(jnp.bfloat16)
            else:
                sum_here = add_share(chunks[chunk], shares[share])
            chunks[chunk] = lax.ppermute(sum_here, axes, way)
            if hop == min(2, reach) and share == 0:
                chunks[chunk], own = lax.optimization_barrier((chunks[chunk], own))
    return apply_expert(own, gate_up, w_down), to_back, to_ahead


def sparse_experts(widened, normed, gate_up, w_down, expert_ids, gates, features):
    half_width = normed.shape[1]
    pair_weights = gate_up[0].reshape(-1, features)
    hidden_units = w_down.shape[1]
    group_total = lax.axis_size("ep")
    group_experts = lax.axis_size("hd")
    all_experts = group_total * group_experts
    block_rows = expert_ids.shape[0]
    group_slots, expert_slots = block_sizes(block_rows, group_total, group_experts)
    chosen = (
        expert_ids[:, :, None] == jnp.arange(all_experts, dtype=jnp.int32)[None, None, :]
    ).astype(jnp.int32)
    named_count = jnp.sum(chosen, axis=1)
    earlier = jnp.cumsum(named_count, axis=0) - named_count
    slot_index = jnp.sum(chosen * earlier[:, None, :], axis=2)
    position = expert_ids * expert_slots + slot_index
    slot_columns = jnp.arange(all_experts * expert_slots, dtype=jnp.int32)
    gate_table = jnp.sum(
        jnp.where(
            position[:, :, None] == slot_columns[None, None, :],
            gates.astype(jnp.float32)[:, :, None],
            0.0,
        ),
        axis=1,
    ).astype(jnp.bfloat16)
    placed = (gate_table != 0).astype(jnp.bfloat16)
    outgoing = jnp.einsum("rq,rd->qd", placed, normed, preferred_element_type=jnp.float32).astype(
        jnp.bfloat16
    )
    outgoing = outgoing.reshape(all_experts, expert_slots, normed.shape[1])
    arrived = lax.all_to_all(outgoing, ("ep", "hd"), split_axis=0, concat_axis=0, tiled=True)
    lead_shape = arrived.shape[:-1]
    rows_in = arrived.reshape(-1, arrived.shape[-1])
    rows_in = lax.all_gather(rows_in, "sub", axis=1, tiled=True)
    projected_pair = jnp.einsum(
        "rd,fd->rf", rows_in, pair_weights, preferred_element_type=jnp.float32
    )
    activation = (
        jax.nn.silu(projected_pair[:, :hidden_units]) * projected_pair[:, hidden_units:]
    ).astype(jnp.bfloat16)
    partial_out = jnp.dot(activation, w_down[0], preferred_element_type=jnp.float32)
    expert_out = lax.psum_scatter(
        partial_out.astype(jnp.bfloat16), "sub", scatter_dimension=1, tiled=True
    )
    results = expert_out.reshape(lead_shape + (expert_out.shape[1],))
    returned = lax.all_to_all(results, ("ep", "hd"), split_axis=0, concat_axis=0, tiled=True)
    mixture = jnp.dot(
        gate_table,
        returned.reshape(all_experts * expert_slots, half_width),
        preferred_element_type=jnp.float32,
    )
    return (widened + mixture).astype(jnp.bfloat16)


def shards(
    queries,
    cache_keys,
    cache_values,
    page_len,
    new_keys,
    new_values,
    out_proj,
    residual,
    norm_gain,
    gate_up,
    w_down,
    expert_ids,
    gates,
):
    n_ep, n_hd, n_sub = lax.axis_size("ep"), lax.axis_size("hd"), lax.axis_size("sub")
    query_rows = queries.shape[0]
    heads_here = queries.shape[1] // HD
    kv_heads = max(1, heads_here // (QH // KVH))
    rows = query_rows // (n_hd * n_sub)
    features = norm_gain.shape[0]
    cache_rows = cache_keys.shape[0]
    all_experts = n_ep * n_hd * gate_up.shape[0]
    dense = (
        expert_ids.shape[1] == all_experts
        and gate_up.shape[0] == 1
        and n_ep * n_hd % 2 == 0
        and rows % 32 == 0
    )

    packed = pack_keys(
        cache_keys, cache_values, new_keys, new_values, page_len, kv_heads, heads_here
    )
    query_rows_here = choose_queries(queries.reshape(n_hd, n_sub, rows, heads_here * HD))
    reach = n_ep // 2
    up, down = list(packed), list(packed)
    arrived = [[(0, x)] for x in packed]
    states = [None] * kv_heads
    earlier = None
    for distance in range(reach + 1):
        stages = [[(hop, sub_copies(x)) for hop, x in blocks] for blocks in arrived]
        if distance == 0:
            out_proj, packed = lax.optimization_barrier((out_proj, packed))
            projections = sub_copies(out_proj)
        if distance == reach and dense:
            blocks = [x for kv_stages in stages for _, x in kv_stages]
            gate_up, w_down, blocks = lax.optimization_barrier((gate_up, w_down, blocks))
            stages = [
                [(hop, blocks.pop(0)) for hop, _ in kv_stages] for kv_stages in stages
            ]
            gate_up_parts = sub_copies(gate_up[0])
            w_down_parts = sub_copies(w_down[0])
        onward = [[] for _ in packed]
        if distance < reach:
            opposite = 2 * (distance + 1) == n_ep
            for kv in range(kv_heads):
                if not opposite or kv % 2 == 0:
                    up[kv] = lax.ppermute(up[kv], "ep", cycle(n_ep))
                    onward[kv].append((distance + 1, up[kv]))
                if not opposite or kv % 2 == 1:
                    down[kv] = lax.ppermute(down[kv], "ep", cycle(n_ep, n_ep - 1))
                    onward[kv].append((n_ep - distance - 1, down[kv]))
        for kv in range(kv_heads):
            finish = (projections, earlier) if distance == reach else None
            states[kv] = attend(
                query_rows_here,
                kv,
                stages[kv],
                states[kv],
                cache_rows,
                kv_heads,
                n_hd,
                2 if dense else 1,
                finish,
            )
            if finish:
                earlier = states[kv][0]
                continue
            came = [x for _, x in onward[kv]]
            came, states[kv] = lax.optimization_barrier((came, states[kv]))
            onward[kv] = [(hop, x) for (hop, _), x in zip(onward[kv], came)]
            for hop, x in onward[kv]:
                if hop == distance + 1:
                    up[kv] = x
                else:
                    down[kv] = x
        if distance == 0:
            residual, states[0] = lax.optimization_barrier((residual, states[0]))
            residual_parts = hand_over(split_rows(residual, n_sub))
            gate_table = gates_by_expert(expert_ids, gates, rows) if dense else None
        arrived = onward
    parts = states[-1]
    if n_hd == 2:
        kept, sent = parts[: len(parts) // 2], parts[len(parts) // 2 :]
        came = [lax.ppermute(x, "hd", cycle(n_hd)) for x in sent]
    else:
        kept = [None]
        came = [lax.psum_scatter(parts[0], "hd", scatter_dimension=0, tiled=True)]
    hidden, normed = [], []
    for index, (kept_chunk, came_chunk) in enumerate(zip(kept, came)):
        pair = normalise(
            kept_chunk,
            came_chunk,
            residual_parts,
            norm_gain,
            gate_table,
            index * came_chunk.shape[0],
        )
        hidden.append(pair[0])
        normed.append(pair[1])
    if not dense:
        own_columns = [
            jnp.concatenate(by_sub(sub_exchange(x, 1)), axis=0) for x in (hidden[0], normed[0])
        ]
        return sparse_experts(
            own_columns[0].astype(jnp.float32),
            own_columns[1],
            gate_up,
            w_down,
            expert_ids,
            gates,
            features,
        )
    mine, to_back, to_ahead = dense_experts(normed, gate_up_parts, w_down_parts)
    return stack_rows(hand_over(add_up(hidden, mine, to_back, to_ahead, n_sub)))


def solution(mesh):
    return jax.shard_map(
        shards,
        mesh=mesh,
        in_specs=(
            P(("grp", "ep"), "hd"),
            P(("grp", "ep", "sub"), None),
            P(("grp", "ep", "sub"), None),
            P(("grp", "ep", "sub")),
            P(("grp", "ep", "sub"), None),
            P(("grp", "ep", "sub"), None),
            P("hd", "sub"),
            P(("grp", "ep", "hd"), "sub"),
            P(),
            P(("ep", "hd"), None, "sub", None),
            P(("ep", "hd"), "sub", None),
            P(("grp", "ep", "hd"), None),
            P(("grp", "ep", "hd"), None),
        ),
        out_specs=P(("grp", "ep", "hd"), "sub"),
        check_vma=False,
    )
```

```python
import functools
import math

import jax
import jax.numpy as jnp
from jax import lax
from jax.experimental import pallas as pl
from jax.experimental.pallas import tpu as pltpu
from jax.sharding import PartitionSpec as P

QH = 32
KVH = 4
HD = 128
GROUPS_ROW = 4
NEG_FILL = -1e30
EPSILON = 1e-06
MASK_ROWS = 16
LANES = 128
MIB = 1024 * 1024
CONTRACT_LAST = (((1,), (1,)), ((), ()))


def block_sizes(block_rows, group_total, experts_group):
    group_slots = min(block_rows, 3 * GROUPS_ROW * block_rows // (2 * group_total))
    return (group_slots, 2 * group_slots // experts_group)


def cycle(size, step=1):
    return [(i, (i + step) % size) for i in range(size)]


def sub_copies(x):
    size = lax.axis_size("sub")
    return [x] + [lax.ppermute(x, "sub", cycle(size, step)) for step in range(1, size)]


def by_sub(copies):
    size = len(copies)
    me = lax.axis_index("sub")
    ordered = []
    for target in range(size):
        value = copies[0]
        for step in range(1, size):
            value = jnp.where((me - step) % size == target, copies[step], value)
        ordered.append(value)
    return ordered


def sub_exchange(x, axis):
    size = lax.axis_size("sub")
    me = lax.axis_index("sub")
    length = x.shape[axis] // size

    def part(index):
        return lax.dynamic_slice_in_dim(x, index * length, length, axis)

    came = [part(me)]
    for step in range(1, size):
        came.append(lax.ppermute(part((me + step) % size), "sub", cycle(size, step)))
    return came


def pack_keys(cache_keys, cache_values, new_keys, new_values, page_len, routing, kv_heads, heads_here):
    cache_rows, new_rows = cache_keys.shape[0], new_keys.shape[0]
    group_width = QH // KVH
    rows = cache_rows + new_rows + MASK_ROWS

    def kernel(page_ref, ck_ref, cv_ref, nk_ref, nv_ref, *refs):
        routing_refs, out_refs = refs[: len(routing)], refs[len(routing) :]
        first = lax.axis_index("hd") * heads_here // group_width
        lane = lax.broadcasted_iota(jnp.int32, (MASK_ROWS, 2 * HD), 1)
        bias = jnp.where(lane < page_ref[0], 0.0, NEG_FILL).astype(jnp.bfloat16)
        for kv, out_ref in enumerate(out_refs):
            columns = pl.ds(pl.multiple_of((first + kv) * HD, HD), HD)
            out_ref[:cache_rows, :HD] = ck_ref[:, columns]
            out_ref[:cache_rows, HD:] = cv_ref[:, columns]
            out_ref[cache_rows : cache_rows + new_rows, :HD] = nk_ref[:, columns]
            out_ref[cache_rows : cache_rows + new_rows, HD:] = nv_ref[:, columns]
            out_ref[cache_rows + new_rows :, :] = bias
        if routing:
            ids = routing_refs[0][...]
            gates = routing_refs[1][...].astype(jnp.float32)
            expert = lax.broadcasted_iota(jnp.int32, (MASK_ROWS, ids.shape[1]), 0)
            table = jnp.zeros(expert.shape, jnp.float32)
            for k in range(ids.shape[0]):
                table = table + jnp.where(ids[k : k + 1, :] == expert, gates[k : k + 1, :], 0.0)
            out_refs[0][cache_rows + new_rows :, HD:] = table.astype(jnp.bfloat16)

    vmem = pl.BlockSpec(memory_space=pltpu.VMEM)
    return pl.pallas_call(
        kernel,
        out_shape=[jax.ShapeDtypeStruct((rows, 2 * HD), cache_keys.dtype)] * kv_heads,
        in_specs=[pl.BlockSpec(memory_space=pltpu.SMEM)] + [vmem] * (4 + len(routing)),
        out_specs=[vmem] * kv_heads,
        name="pack_keys",
    )(page_len, cache_keys, cache_values, new_keys, new_values, *routing)


def small_kernel(kernel, out_shape, operands, name):
    vmem = pl.BlockSpec(memory_space=pltpu.VMEM)
    return pl.pallas_call(
        kernel,
        out_shape=out_shape,
        in_specs=[vmem] * len(operands),
        out_specs=[vmem] * len(out_shape),
        compiler_params=pltpu.CompilerParams(vmem_limit_bytes=8 * MIB),
        cost_estimate=pl.CostEstimate(flops=MIB, bytes_accessed=MIB, transcendentals=0),
        name=name,
    )(*operands)


def hand_over(parts):
    size = len(parts)
    return [parts[0]] + [
        lax.ppermute(part, "sub", cycle(size, step)) for step, part in enumerate(parts) if step
    ]


def choose_queries(queries):
    n_hd, n_sub, rows, columns = queries.shape

    def kernel(in_ref, out_ref, sems):
        sub = lax.axis_index("sub")
        hd = lax.axis_index("hd")
        copies = []
        for j in range(n_hd):
            place = (hd + j) % n_hd if n_hd == 2 else j
            copies.append(
                pltpu.make_async_copy(
                    in_ref.at[place, sub], out_ref.at[pl.ds(j * rows, rows), :], sems.at[j]
                )
            )
            copies[-1].start()
        for copy in copies:
            copy.wait()

    return pl.pallas_call(
        kernel,
        out_shape=jax.ShapeDtypeStruct((n_hd * rows, columns), queries.dtype),
        in_specs=[pl.BlockSpec(memory_space=pltpu.HBM)],
        out_specs=pl.BlockSpec(memory_space=pltpu.VMEM),
        scratch_shapes=[pltpu.SemaphoreType.DMA((n_hd,))],
        compiler_params=pltpu.CompilerParams(vmem_limit_bytes=8 * MIB),
        name="choose_queries",
    )(queries)


def split_rows(residual, n_sub):
    rows, columns = residual.shape[0] // n_sub, residual.shape[1]

    def kernel(in_ref, *out_refs):
        sub = lax.axis_index("sub")
        for step, out_ref in enumerate(out_refs):
            first = pl.multiple_of((sub + step) % n_sub * rows, rows)
            out_ref[...] = in_ref[pl.ds(first, rows), :]

    shape = jax.ShapeDtypeStruct((rows, columns), residual.dtype)
    return small_kernel(kernel, [shape] * n_sub, [residual], "split_rows")


def walk_place(ep, hd, n_ep, n_hd):
    if n_hd == 2:
        return jnp.where(hd == 0, ep, 2 * n_ep - 1 - ep)
    return ep * n_hd + hd


def gates_by_chip(own, came, n_ep, n_hd):
    block_rows = own.shape[1]

    def kernel(own_ref, came_ref, out_ref):
        ep, hd = lax.axis_index("ep"), lax.axis_index("hd")
        mine = ep * n_hd + hd
        expert = lax.broadcasted_iota(jnp.int32, (MASK_ROWS, block_rows), 0)
        place = lax.broadcasted_iota(jnp.int32, (LANES, block_rows), 0)
        table = jnp.zeros((LANES, block_rows), jnp.float32)
        for ref, other in ((own_ref, hd), (came_ref, 1 - hd)):
            for hop in range(n_ep):
                tile = ref[hop * MASK_ROWS : (hop + 1) * MASK_ROWS, :].astype(jnp.float32)
                row = jnp.sum(jnp.where(expert == mine, tile, 0.0), axis=0, keepdims=True)
                chip = walk_place((ep - hop) % n_ep, other, n_ep, n_hd)
                table = jnp.where(place == chip, row, table)
        out_ref[...] = table.T

    shape = jax.ShapeDtypeStruct((block_rows, LANES), jnp.float32)
    return small_kernel(kernel, [shape], [own, came], "gates_by_chip")[0]


def normalise(kept, came, residual_parts, gain, first):
    n_sub = len(residual_parts)
    rows, width = came.shape[0], residual_parts[0].shape[1]
    chunk = slice(first, first + rows)
    features = n_sub * width

    def kernel(*refs):
        refs = list(refs)
        kept_ref = refs.pop(0) if kept is not None else None
        came_ref = refs.pop(0)
        part_refs = [refs.pop(0) for _ in residual_parts]
        gain_ref = refs.pop(0)
        hidden_ref, normed_ref = refs
        sub = lax.axis_index("sub")
        hidden, places, squares = [], [], 0.0
        for step, part_ref in enumerate(part_refs):
            here = slice(step * width, (step + 1) * width)
            projected = came_ref[:, here].astype(jnp.float32)
            if kept is not None:
                projected = kept_ref[:, here] + projected
            value = (part_ref[chunk, :].astype(jnp.float32) + projected).astype(jnp.bfloat16)
            hidden.append(value)
            place = pl.ds(pl.multiple_of((sub - step) % n_sub * width, width), width)
            places.append(place)
            hidden_ref[:, place] = value
            wide = value.astype(jnp.float32)
            squares = squares + jnp.sum(wide * wide, axis=1, keepdims=True)
        scale = lax.rsqrt(squares / features + EPSILON)
        for value, place in zip(hidden, places):
            normed = value.astype(jnp.float32) * scale * gain_ref[:, place].astype(jnp.float32)
            normed_ref[:, place] = normed.astype(jnp.bfloat16)

    operands = ([kept] if kept is not None else []) + [came] + list(residual_parts)
    operands.append(gain.reshape(1, features))
    out_shape = [jax.ShapeDtypeStruct((rows, features), jnp.bfloat16)] * 2
    return small_kernel(kernel, out_shape, operands, "normalise")


def add_up(hidden, mine, to_back, to_ahead, n_sub):
    chunks = len(hidden)
    rows, features = hidden[0].shape
    width = features // n_sub

    def kernel(*refs):
        terms, out_refs = refs[: 4 * chunks], refs[4 * chunks :]
        sub = lax.axis_index("sub")
        for step, out_ref in enumerate(out_refs):
            place = pl.ds(pl.multiple_of((sub + step) % n_sub * width, width), width)
            for chunk in range(chunks):
                hidden_ref, mine_ref, back_ref, ahead_ref = terms[chunk::chunks]
                mixture = mine_ref[:, place] + back_ref[:, place].astype(jnp.float32)
                mixture = mixture + ahead_ref[:, place].astype(jnp.float32)
                total = hidden_ref[:, place].astype(jnp.float32) + mixture
                out_ref[chunk * rows : (chunk + 1) * rows, :] = total.astype(jnp.bfloat16)

    shape = jax.ShapeDtypeStruct((chunks * rows, width), jnp.bfloat16)
    operands = [*hidden, *mine, *to_back, *to_ahead]
    return small_kernel(kernel, [shape] * n_sub, operands, "add_up")


def stack_rows(parts):
    n_sub = len(parts)
    rows, width = parts[0].shape

    def kernel(*refs):
        sub = lax.axis_index("sub")
        for step, part_ref in enumerate(refs[:-1]):
            first = pl.multiple_of((sub - step) % n_sub * rows, rows)
            refs[-1][pl.ds(first, rows), :] = part_ref[...]

    shape = jax.ShapeDtypeStruct((n_sub * rows, width), parts[0].dtype)
    return small_kernel(kernel, [shape], parts, "stack_rows")[0]


def attend(queries, kv, stages, state, cache_rows, kv_heads, n_hd, chunks, finish=None):
    all_rows, columns = queries.shape
    rows, n_sub = all_rows // n_hd, len(stages[0][1])
    blocks = [block for _, stage_blocks in stages for block in stage_blocks]
    origins = [(hop, step) for hop, _ in stages for step in range(n_sub)]
    per_kv = columns // HD // kv_heads
    stack = 2 if per_kv % 2 == 0 else 1
    part = stack * all_rows
    new_rows = blocks[0].shape[0] - cache_rows - MASK_ROWS
    keys = cache_rows + new_rows
    factor = math.log2(math.e) / math.sqrt(HD)
    relative = n_hd == 2
    last = finish is not None
    weights, earlier = finish if last else ([], None)
    head_columns = per_kv * HD
    final = last and kv == kv_heads - 1
    kept_rows = rows if relative else 0
    chunk_rows = rows // chunks if relative else all_rows

    def kernel(*refs):
        q_ref, refs = refs[0], refs[1:]
        block_refs, refs = refs[: len(blocks)], refs[len(blocks) :]
        if state is not None:
            (m_in, acc_in), refs = refs[:2], refs[2:]
        weight_refs, refs = refs[: len(weights)], refs[len(weights) :]
        if earlier is not None:
            earlier_ref, refs = refs[0], refs[1:]
        if last:
            results = len(out_shape)
            result_refs, refs = refs[:results], refs[results:]
            head_ref, refs = refs[0], refs[1:]
        else:
            m_out, acc_out = refs
        sub = lax.axis_index("sub")
        ep = lax.axis_index("ep")
        hd = lax.axis_index("hd")
        places = [(hd + j) % n_hd if relative else j for j in range(n_hd)]
        biases = []
        for (hop, step), block in zip(origins, block_refs):
            cache_bias = block[keys : keys + 1, :cache_rows].astype(jnp.float32)
            if hop == 0:
                key_id = ((sub - step) % n_sub) * new_rows + lax.broadcasted_iota(
                    jnp.int32, (rows, new_rows), 1
                )
                row_id = lax.broadcasted_iota(jnp.int32, (rows, new_rows), 0)
                seen = [
                    jnp.where(
                        key_id <= row_id + (place * n_sub + sub) * rows, 0.0, NEG_FILL
                    )
                    for place in places
                ]
                new_bias = jnp.concatenate(seen * stack, axis=0)
                cache_bias = jnp.broadcast_to(cache_bias, (part, cache_rows))
            else:
                new_bias = jnp.full(
                    (1, new_rows), jnp.where(ep >= hop, 0.0, NEG_FILL), jnp.float32
                )
            biases.append(jnp.concatenate([cache_bias, new_bias], axis=1))
        ones = jnp.ones((keys, HD), jnp.bfloat16)
        key_parts = [block[:keys, :HD] for block in block_refs]
        value_parts = [
            jnp.concatenate([block[:keys, HD:], ones], axis=1) for block in block_refs
        ]
        for index in range(per_kv // stack):
            here = slice(index * part, (index + 1) * part)
            heads = range(kv * per_kv + index * stack, kv * per_kv + (index + 1) * stack)
            q = jnp.concatenate([q_ref[:, h * HD : (h + 1) * HD] for h in heads], axis=0)
            terms = [
                lax.dot_general(q, k, CONTRACT_LAST, preferred_element_type=jnp.float32) * factor
                + bias
                for k, bias in zip(key_parts, biases)
            ]
            top = jnp.max(functools.reduce(jnp.maximum, terms), axis=1, keepdims=True)
            top = jnp.broadcast_to(top, (part, LANES))
            if state is not None:
                top_in = m_in[here, :]
                top = jnp.maximum(top, top_in)
            wide_top = jnp.concatenate([top] * (keys // LANES), axis=1)
            acc = None
            for term, v in zip(terms, value_parts):
                exp_terms = jnp.exp2(term - wide_top).astype(jnp.bfloat16)
                product = jnp.dot(exp_terms, v, preferred_element_type=jnp.float32)
                acc = product if acc is None else acc + product
            if state is not None:
                scale = jnp.exp2(top_in - top)
                acc = acc + jnp.concatenate([scale, scale], axis=1) * acc_in[here, :]
            if last:
                out = (acc[:, :HD] / acc[:, HD:]).astype(jnp.bfloat16)
                for s in range(stack):
                    first = (index * stack + s) * HD
                    head_ref[:, first : first + HD] = out[s * all_rows : (s + 1) * all_rows]
            else:
                m_out[here, :] = top
                acc_out[here, :] = acc
        if last:
            source = head_ref[...]
            width = weight_refs[0].shape[1]
            these = slice(kv * head_columns, (kv + 1) * head_columns)
            for i, weight_ref in enumerate(weight_refs):
                here = slice(i * width, (i + 1) * width)
                product = jnp.dot(
                    source, weight_ref[these, :], preferred_element_type=jnp.float32
                )
                if earlier is not None:
                    product = product + earlier_ref[:, here]
                if final:
                    for j, result_ref in enumerate(result_refs):
                        share = product[j * chunk_rows : (j + 1) * chunk_rows]
                        result_ref[:, here] = share.astype(result_ref.dtype)
                else:
                    result_refs[0][:, here] = product

    vmem = pl.BlockSpec(memory_space=pltpu.VMEM)
    scratch = []
    if last:
        features = sum(w.shape[1] for w in weights)
        if final:
            out_shape = [
                jax.ShapeDtypeStruct((chunk_rows, features), kind)
                for kind, count in [
                    (jnp.float32, kept_rows // chunk_rows),
                    (jnp.bfloat16, (all_rows - kept_rows) // chunk_rows),
                ]
                for _ in range(count)
            ]
        else:
            out_shape = (jax.ShapeDtypeStruct((all_rows, features), jnp.float32),)
        scratch = [pltpu.VMEM((all_rows, head_columns), jnp.bfloat16)]
    else:
        out_shape = (
            jax.ShapeDtypeStruct((per_kv * all_rows, LANES), jnp.float32),
            jax.ShapeDtypeStruct((per_kv * all_rows, 2 * HD), jnp.float32),
        )
    operands = [queries] + list(blocks) + (list(state) if state is not None else [])
    operands += list(weights)
    if earlier is not None:
        operands.append(earlier)
    scores = all_rows * per_kv * keys * len(blocks)
    return pl.pallas_call(
        kernel,
        out_shape=out_shape,
        in_specs=[vmem] * len(operands),
        out_specs=tuple(vmem for _ in out_shape),
        scratch_shapes=scratch,
        compiler_params=pltpu.CompilerParams(vmem_limit_bytes=16 * MIB),
        cost_estimate=pl.CostEstimate(
            flops=6 * scores * HD, bytes_accessed=4 * MIB, transcendentals=scores
        ),
        name="attend",
    )(*operands)


def apply_expert(inputs, origins, gate_table, gate_up, w_down):
    features = w_down[0].shape[1]
    hidden = w_down[0].shape[0]
    rows = sum(x.shape[0] for x in inputs)
    n_ep, n_hd, n_sub = lax.axis_size("ep"), lax.axis_size("hd"), lax.axis_size("sub")
    chunks = gate_table.shape[0] // n_sub // inputs[0].shape[0]

    def kernel(*refs):
        x_refs, refs = refs[: len(inputs)], refs[len(inputs) :]
        gate_ref, refs = refs[0], refs[1:]
        gu_refs, refs = refs[: len(gate_up)], refs[len(gate_up) :]
        down_refs, out_refs = refs[: len(w_down)], refs[len(w_down) :]
        x = jnp.concatenate([x[...] for x in x_refs], axis=0)
        here = walk_place(lax.axis_index("ep"), lax.axis_index("hd"), n_ep, n_hd)
        columns = []
        for (steps, chunk), x_ref in zip(origins, x_refs):
            count = x_ref.shape[0]
            sub = (lax.axis_index("sub") + steps) % n_sub
            first = pl.multiple_of((sub * chunks + chunk) * count, count)
            table = gate_ref[pl.ds(first, count), :]
            lane = lax.broadcasted_iota(jnp.int32, table.shape, 1)
            chip = (here + steps) % (n_ep * n_hd)
            columns.append(jnp.sum(jnp.where(lane == chip, table, 0.0), axis=1, keepdims=True))
        gate = jnp.concatenate(columns, axis=0)
        total = None
        for gu, down in zip(gu_refs, down_refs):
            gate_part = lax.dot_general(
                x, gu[0], CONTRACT_LAST, preferred_element_type=jnp.float32
            )
            up_part = lax.dot_general(x, gu[1], CONTRACT_LAST, preferred_element_type=jnp.float32)
            activation = (gate_part / (1.0 + jnp.exp(-gate_part)) * up_part).astype(jnp.bfloat16)
            product = jnp.dot(activation, down[...], preferred_element_type=jnp.float32)
            total = product if total is None else total + product
        total = gate * total.astype(jnp.bfloat16).astype(jnp.float32)
        first = 0
        for out_ref in out_refs:
            out_ref[...] = total[first : first + out_ref.shape[0]]
            first += out_ref.shape[0]

    vmem = pl.BlockSpec(memory_space=pltpu.VMEM)
    operands = list(inputs) + [gate_table] + list(gate_up) + list(w_down)
    return pl.pallas_call(
        kernel,
        out_shape=[jax.ShapeDtypeStruct((x.shape[0], features), jnp.float32) for x in inputs],
        in_specs=[vmem] * len(operands),
        out_specs=[vmem] * len(inputs),
        compiler_params=pltpu.CompilerParams(vmem_limit_bytes=16 * MIB),
        cost_estimate=pl.CostEstimate(
            flops=6 * rows * hidden * len(w_down) * features,
            bytes_accessed=6 * MIB,
            transcendentals=rows * hidden * len(w_down),
        ),
        name="apply_expert",
    )(*operands)


def chip_ring(n_ep, n_hd):
    if n_hd == 2:
        return [z * 2 for z in range(n_ep)] + [z * 2 + 1 for z in reversed(range(n_ep))]
    return list(range(n_ep * n_hd))


def add_share(came, share):
    def kernel(came_ref, share_ref, out_ref):
        total = came_ref[...].astype(jnp.float32) + share_ref[...]
        out_ref[...] = total.astype(jnp.bfloat16)

    shape = jax.ShapeDtypeStruct(share.shape, jnp.bfloat16)
    return small_kernel(kernel, [shape], [came, share], "add_share")[0]


def dense_experts(own, gate_table, gate_up, w_down):
    axes = ("ep", "hd", "sub")
    walk = chip_ring(lax.axis_size("ep"), lax.axis_size("hd"))
    size, n_sub = len(walk), lax.axis_size("sub")
    ahead = [
        (walk[i] * n_sub + sub, walk[(i + 1) % size] * n_sub + (sub + 1) % n_sub)
        for i in range(size)
        for sub in range(n_sub)
    ]
    back = [(b, a) for a, b in ahead]
    reach = size // 2
    behind, before, waiting = list(own), list(own), None
    outs = [None]
    for hop in range(1, reach + 1):
        behind[0] = lax.ppermute(behind[0], axes, ahead)
        before[1] = lax.ppermute(before[1], axes, back)
        if hop < reach:
            behind[1] = lax.ppermute(behind[1], axes, ahead)
            before[0] = lax.ppermute(before[0], axes, back)
        if waiting:
            out = apply_expert(waiting, origins, gate_table, gate_up, w_down)
            late = int(hop < reach)
            behind[late], out = lax.optimization_barrier((behind[late], out))
            outs.append(out)
        waiting = [behind[0], before[1]] + ([behind[1], before[0]] if hop < reach else [])
        origins = [(-hop, 0), (hop, 1), (-hop, 1), (hop, 0)][: len(waiting)]
    outs.append(apply_expert(waiting, origins, gate_table, gate_up, w_down))
    to_back, to_ahead = [None, None], [None, None]
    for hop in range(reach, 0, -1):
        shares = outs[hop]
        for chunks, chunk, way, share in [
            (to_back, 0, back, 0),
            (to_ahead, 1, ahead, 1),
            (to_back, 1, back, 2),
            (to_ahead, 0, ahead, 3),
        ]:
            if share >= len(shares):
                continue
            if chunks[chunk] is None:
                sum_here = shares[share].astype(jnp.bfloat16)
            else:
                sum_here = add_share(chunks[chunk], shares[share])
            chunks[chunk] = lax.ppermute(sum_here, axes, way)
            if hop == min(2, reach) and share == 0:
                chunks[chunk], own = lax.optimization_barrier((chunks[chunk], own))
    mine = apply_expert(own, [(0, 0), (0, 1)], gate_table, gate_up, w_down)
    return mine, to_back, to_ahead


def sparse_experts(widened, normed, gate_up, w_down, expert_ids, gates, features):
    half_width = normed.shape[1]
    pair_weights = gate_up[0].reshape(-1, features)
    hidden_units = w_down.shape[1]
    group_total = lax.axis_size("ep")
    group_experts = lax.axis_size("hd")
    all_experts = group_total * group_experts
    block_rows = expert_ids.shape[0]
    group_slots, expert_slots = block_sizes(block_rows, group_total, group_experts)
    chosen = (
        expert_ids[:, :, None] == jnp.arange(all_experts, dtype=jnp.int32)[None, None, :]
    ).astype(jnp.int32)
    named_count = jnp.sum(chosen, axis=1)
    earlier = jnp.cumsum(named_count, axis=0) - named_count
    slot_index = jnp.sum(chosen * earlier[:, None, :], axis=2)
    position = expert_ids * expert_slots + slot_index
    slot_columns = jnp.arange(all_experts * expert_slots, dtype=jnp.int32)
    gate_table = jnp.sum(
        jnp.where(
            position[:, :, None] == slot_columns[None, None, :],
            gates.astype(jnp.float32)[:, :, None],
            0.0,
        ),
        axis=1,
    ).astype(jnp.bfloat16)
    placed = (gate_table != 0).astype(jnp.bfloat16)
    outgoing = jnp.einsum("rq,rd->qd", placed, normed, preferred_element_type=jnp.float32).astype(
        jnp.bfloat16
    )
    outgoing = outgoing.reshape(all_experts, expert_slots, normed.shape[1])
    arrived = lax.all_to_all(outgoing, ("ep", "hd"), split_axis=0, concat_axis=0, tiled=True)
    lead_shape = arrived.shape[:-1]
    rows_in = arrived.reshape(-1, arrived.shape[-1])
    rows_in = lax.all_gather(rows_in, "sub", axis=1, tiled=True)
    projected_pair = jnp.einsum(
        "rd,fd->rf", rows_in, pair_weights, preferred_element_type=jnp.float32
    )
    activation = (
        jax.nn.silu(projected_pair[:, :hidden_units]) * projected_pair[:, hidden_units:]
    ).astype(jnp.bfloat16)
    partial_out = jnp.dot(activation, w_down[0], preferred_element_type=jnp.float32)
    expert_out = lax.psum_scatter(
        partial_out.astype(jnp.bfloat16), "sub", scatter_dimension=1, tiled=True
    )
    results = expert_out.reshape(lead_shape + (expert_out.shape[1],))
    returned = lax.all_to_all(results, ("ep", "hd"), split_axis=0, concat_axis=0, tiled=True)
    mixture = jnp.dot(
        gate_table,
        returned.reshape(all_experts * expert_slots, half_width),
        preferred_element_type=jnp.float32,
    )
    return (widened + mixture).astype(jnp.bfloat16)


def shards(
    queries,
    cache_keys,
    cache_values,
    page_len,
    new_keys,
    new_values,
    out_proj,
    residual,
    norm_gain,
    gate_up,
    w_down,
    expert_ids,
    gates,
):
    n_ep, n_hd, n_sub = lax.axis_size("ep"), lax.axis_size("hd"), lax.axis_size("sub")
    query_rows = queries.shape[0]
    heads_here = queries.shape[1] // HD
    kv_heads = max(1, heads_here // (QH // KVH))
    rows = query_rows // (n_hd * n_sub)
    features = norm_gain.shape[0]
    cache_rows = cache_keys.shape[0]
    all_experts = n_ep * n_hd * gate_up.shape[0]
    dense = (
        expert_ids.shape[1] == all_experts
        and gate_up.shape[0] == 1
        and n_hd == 2
        and rows % 32 == 0
        and all_experts <= MASK_ROWS
        and expert_ids.shape[0] == LANES
    )

    packed = pack_keys(
        cache_keys,
        cache_values,
        new_keys,
        new_values,
        page_len,
        [expert_ids.T, gates.T] if dense else [],
        kv_heads,
        heads_here,
    )
    query_rows_here = choose_queries(queries.reshape(n_hd, n_sub, rows, heads_here * HD))
    reach = n_ep // 2
    up, down = list(packed), list(packed)
    arrived = [[(0, x)] for x in packed]
    tables = {}
    states = [None] * kv_heads
    earlier = None
    for distance in range(reach + 1):
        stages = [[(hop, sub_copies(x)) for hop, x in blocks] for blocks in arrived]
        if distance == 0:
            out_proj, packed = lax.optimization_barrier((out_proj, packed))
            projections = sub_copies(out_proj)
        if distance == reach and dense:
            blocks = [x for kv_stages in stages for _, x in kv_stages]
            gate_up, w_down, blocks = lax.optimization_barrier((gate_up, w_down, blocks))
            stages = [
                [(hop, blocks.pop(0)) for hop, _ in kv_stages] for kv_stages in stages
            ]
            gate_up_parts = sub_copies(gate_up[0])
            w_down_parts = sub_copies(w_down[0])
        for hop, x in arrived[0]:
            tables[hop] = x[-MASK_ROWS:, HD:]
        onward = [[] for _ in packed]
        if distance < reach:
            opposite = 2 * (distance + 1) == n_ep
            for kv in range(kv_heads):
                if not opposite or kv % 2 == 0:
                    up[kv] = lax.ppermute(up[kv], "ep", cycle(n_ep))
                    onward[kv].append((distance + 1, up[kv]))
                if not opposite or kv % 2 == 1:
                    down[kv] = lax.ppermute(down[kv], "ep", cycle(n_ep, n_ep - 1))
                    onward[kv].append((n_ep - distance - 1, down[kv]))
        for kv in range(kv_heads):
            finish = (projections, earlier) if distance == reach else None
            states[kv] = attend(
                query_rows_here,
                kv,
                stages[kv],
                states[kv],
                cache_rows,
                kv_heads,
                n_hd,
                2 if dense else 1,
                finish,
            )
            if finish:
                earlier = states[kv][0]
                continue
            came = [x for _, x in onward[kv]]
            came, states[kv] = lax.optimization_barrier((came, states[kv]))
            onward[kv] = [(hop, x) for (hop, _), x in zip(onward[kv], came)]
            for hop, x in onward[kv]:
                if hop == distance + 1:
                    up[kv] = x
                else:
                    down[kv] = x
        if distance == 0:
            residual, states[0] = lax.optimization_barrier((residual, states[0]))
            residual_parts = hand_over(split_rows(residual, n_sub))
        arrived = onward
    parts = states[-1]
    if n_hd == 2:
        kept, sent = parts[: len(parts) // 2], parts[len(parts) // 2 :]
        came = [lax.ppermute(x, "hd", cycle(n_hd)) for x in sent]
        if dense:
            own_tables = jnp.concatenate([tables[hop] for hop in range(n_ep)], axis=0)
            other_tables = lax.ppermute(own_tables, "hd", cycle(n_hd))
            gate_table = gates_by_chip(own_tables, other_tables, n_ep, n_hd)
            came[0], gate_table = lax.optimization_barrier((came[0], gate_table))
    else:
        kept = [None]
        came = [lax.psum_scatter(parts[0], "hd", scatter_dimension=0, tiled=True)]
    hidden, normed = [], []
    for index, (kept_chunk, came_chunk) in enumerate(zip(kept, came)):
        pair = normalise(
            kept_chunk,
            came_chunk,
            residual_parts,
            norm_gain,
            index * came_chunk.shape[0],
        )
        hidden.append(pair[0])
        normed.append(pair[1])
    if not dense:
        own_columns = [
            jnp.concatenate(by_sub(sub_exchange(x, 1)), axis=0) for x in (hidden[0], normed[0])
        ]
        return sparse_experts(
            own_columns[0].astype(jnp.float32),
            own_columns[1],
            gate_up,
            w_down,
            expert_ids,
            gates,
            features,
        )
    mine, to_back, to_ahead = dense_experts(normed, gate_table, gate_up_parts, w_down_parts)
    return stack_rows(hand_over(add_up(hidden, mine, to_back, to_ahead, n_sub)))


def solution(mesh):
    return jax.shard_map(
        shards,
        mesh=mesh,
        in_specs=(
            P(("grp", "ep"), "hd"),
            P(("grp", "ep", "sub"), None),
            P(("grp", "ep", "sub"), None),
            P(("grp", "ep", "sub")),
            P(("grp", "ep", "sub"), None),
            P(("grp", "ep", "sub"), None),
            P("hd", "sub"),
            P(("grp", "ep", "hd"), "sub"),
            P(),
            P(("ep", "hd"), None, "sub", None),
            P(("ep", "hd"), "sub", None),
            P(("grp", "ep", "hd"), None),
            P(("grp", "ep", "hd"), None),
        ),
        out_specs=P(("grp", "ep", "hd"), "sub"),
        check_vma=False,
    )
```

```python
import functools
import math

import jax
import jax.numpy as jnp
from jax import lax
from jax.experimental import pallas as pl
from jax.experimental.pallas import tpu as pltpu
from jax.sharding import PartitionSpec as P

QH = 32
KVH = 4
HD = 128
GROUPS_ROW = 4
NEG_FILL = -1e30
EPSILON = 1e-06
MASK_ROWS = 16
TABLE_ROWS = 8
LANES = 128
MIB = 1024 * 1024
CONTRACT_LAST = (((1,), (1,)), ((), ()))


def block_sizes(block_rows, group_total, experts_group):
    group_slots = min(block_rows, 3 * GROUPS_ROW * block_rows // (2 * group_total))
    return (group_slots, 2 * group_slots // experts_group)


def cycle(size, step=1):
    return [(i, (i + step) % size) for i in range(size)]


def sub_copies(x):
    size = lax.axis_size("sub")
    return [x] + [lax.ppermute(x, "sub", cycle(size, step)) for step in range(1, size)]


def by_sub(copies):
    size = len(copies)
    me = lax.axis_index("sub")
    ordered = []
    for target in range(size):
        value = copies[0]
        for step in range(1, size):
            value = jnp.where((me - step) % size == target, copies[step], value)
        ordered.append(value)
    return ordered


def sub_exchange(x, axis):
    size = lax.axis_size("sub")
    me = lax.axis_index("sub")
    length = x.shape[axis] // size

    def part(index):
        return lax.dynamic_slice_in_dim(x, index * length, length, axis)

    came = [part(me)]
    for step in range(1, size):
        came.append(lax.ppermute(part((me + step) % size), "sub", cycle(size, step)))
    return came


def pack_keys(cache_keys, cache_values, new_keys, new_values, page_len, routing, kv_heads, heads_here):
    cache_rows, new_rows = cache_keys.shape[0], new_keys.shape[0]
    group_width = QH // KVH
    rows = cache_rows + new_rows + MASK_ROWS

    def kernel(page_ref, ck_ref, cv_ref, nk_ref, nv_ref, *refs):
        routing_refs, out_refs = refs[: len(routing)], refs[len(routing) :]
        first = lax.axis_index("hd") * heads_here // group_width
        lane = lax.broadcasted_iota(jnp.int32, (MASK_ROWS, 2 * HD), 1)
        bias = jnp.where(lane < page_ref[0], 0.0, NEG_FILL).astype(jnp.bfloat16)
        for kv, out_ref in enumerate(out_refs):
            columns = pl.ds(pl.multiple_of((first + kv) * HD, HD), HD)
            out_ref[:cache_rows, :HD] = ck_ref[:, columns]
            out_ref[:cache_rows, HD:] = cv_ref[:, columns]
            out_ref[cache_rows : cache_rows + new_rows, :HD] = nk_ref[:, columns]
            out_ref[cache_rows : cache_rows + new_rows, HD:] = nv_ref[:, columns]
            out_ref[cache_rows + new_rows :, :] = bias
        if routing:
            ids = routing_refs[0][...]
            gates = routing_refs[1][...].astype(jnp.float32)
            expert = lax.broadcasted_iota(jnp.int32, (MASK_ROWS, ids.shape[1]), 0)
            table = jnp.zeros(expert.shape, jnp.float32)
            for k in range(ids.shape[0]):
                table = table + jnp.where(ids[k : k + 1, :] == expert, gates[k : k + 1, :], 0.0)
            out_refs[0][cache_rows + new_rows :, HD:] = table.astype(jnp.bfloat16)

    vmem = pl.BlockSpec(memory_space=pltpu.VMEM)
    return pl.pallas_call(
        kernel,
        out_shape=[jax.ShapeDtypeStruct((rows, 2 * HD), cache_keys.dtype)] * kv_heads,
        in_specs=[pl.BlockSpec(memory_space=pltpu.SMEM)] + [vmem] * (4 + len(routing)),
        out_specs=[vmem] * kv_heads,
        name="pack_keys",
    )(page_len, cache_keys, cache_values, new_keys, new_values, *routing)


def small_kernel(kernel, out_shape, operands, name):
    vmem = pl.BlockSpec(memory_space=pltpu.VMEM)
    return pl.pallas_call(
        kernel,
        out_shape=out_shape,
        in_specs=[vmem] * len(operands),
        out_specs=[vmem] * len(out_shape),
        compiler_params=pltpu.CompilerParams(vmem_limit_bytes=8 * MIB),
        cost_estimate=pl.CostEstimate(flops=MIB, bytes_accessed=MIB, transcendentals=0),
        name=name,
    )(*operands)


def hand_over(parts):
    size = len(parts)
    return [parts[0]] + [
        lax.ppermute(part, "sub", cycle(size, step)) for step, part in enumerate(parts) if step
    ]


def choose_queries(queries):
    n_hd, n_sub, rows, columns = queries.shape

    def kernel(in_ref, out_ref, sems):
        sub = lax.axis_index("sub")
        hd = lax.axis_index("hd")
        copies = []
        for j in range(n_hd):
            place = (hd + j) % n_hd if n_hd == 2 else j
            copies.append(
                pltpu.make_async_copy(
                    in_ref.at[place, sub], out_ref.at[pl.ds(j * rows, rows), :], sems.at[j]
                )
            )
            copies[-1].start()
        for copy in copies:
            copy.wait()

    return pl.pallas_call(
        kernel,
        out_shape=jax.ShapeDtypeStruct((n_hd * rows, columns), queries.dtype),
        in_specs=[pl.BlockSpec(memory_space=pltpu.HBM)],
        out_specs=pl.BlockSpec(memory_space=pltpu.VMEM),
        scratch_shapes=[pltpu.SemaphoreType.DMA((n_hd,))],
        compiler_params=pltpu.CompilerParams(vmem_limit_bytes=8 * MIB),
        name="choose_queries",
    )(queries)


def split_rows(residual, n_sub):
    rows, columns = residual.shape[0] // n_sub, residual.shape[1]

    def kernel(in_ref, *out_refs):
        sub = lax.axis_index("sub")
        for step, out_ref in enumerate(out_refs):
            first = pl.multiple_of((sub + step) % n_sub * rows, rows)
            out_ref[...] = in_ref[pl.ds(first, rows), :]

    shape = jax.ShapeDtypeStruct((rows, columns), residual.dtype)
    return small_kernel(kernel, [shape] * n_sub, [residual], "split_rows")


def walk_place(ep, hd, n_ep, n_hd):
    if n_hd == 2:
        return jnp.where(hd == 0, ep, 2 * n_ep - 1 - ep)
    return ep * n_hd + hd


def gates_by_chip(own, came, n_ep, n_hd):
    block_rows = own.shape[1]
    places = slice(came.shape[1] - block_rows, came.shape[1])

    def kernel(own_ref, came_ref, out_ref):
        ep, hd = lax.axis_index("ep"), lax.axis_index("hd")
        mine = ep * n_hd + hd
        expert = lax.broadcasted_iota(jnp.int32, (TABLE_ROWS, block_rows), 0)
        place = lax.broadcasted_iota(jnp.int32, (LANES, block_rows), 0)
        table = jnp.zeros((LANES, block_rows), jnp.float32)
        tables = [(own_ref[...], hd), (came_ref[: n_ep * TABLE_ROWS, places], 1 - hd)]
        for joint, other in tables:
            joint = joint.astype(jnp.float32)
            for hop in range(n_ep):
                tile = joint[hop * TABLE_ROWS : (hop + 1) * TABLE_ROWS, :]
                row = jnp.sum(jnp.where(expert == mine, tile, 0.0), axis=0, keepdims=True)
                chip = walk_place((ep - hop) % n_ep, other, n_ep, n_hd)
                table = jnp.where(place == chip, row, table)
        out_ref[...] = table.T

    shape = jax.ShapeDtypeStruct((block_rows, LANES), jnp.float32)
    return small_kernel(kernel, [shape], [own, came], "gates_by_chip")[0]


def normalise(kept, came, residual_parts, gain, first):
    n_sub = len(residual_parts)
    rows, width = came.shape[0], residual_parts[0].shape[1]
    chunk = slice(first, first + rows)
    features = n_sub * width

    def kernel(*refs):
        refs = list(refs)
        kept_ref = refs.pop(0) if kept is not None else None
        came_ref = refs.pop(0)
        part_refs = [refs.pop(0) for _ in residual_parts]
        gain_ref = refs.pop(0)
        hidden_ref, normed_ref = refs
        sub = lax.axis_index("sub")
        hidden, places, squares = [], [], 0.0
        for step, part_ref in enumerate(part_refs):
            here = slice(step * width, (step + 1) * width)
            projected = came_ref[:, here].astype(jnp.float32)
            if kept is not None:
                projected = kept_ref[:, here] + projected
            value = (part_ref[chunk, :].astype(jnp.float32) + projected).astype(jnp.bfloat16)
            hidden.append(value)
            place = pl.ds(pl.multiple_of((sub - step) % n_sub * width, width), width)
            places.append(place)
            hidden_ref[:, place] = value
            wide = value.astype(jnp.float32)
            squares = squares + jnp.sum(wide * wide, axis=1, keepdims=True)
        scale = lax.rsqrt(squares / features + EPSILON)
        for value, place in zip(hidden, places):
            normed = value.astype(jnp.float32) * scale * gain_ref[:, place].astype(jnp.float32)
            normed_ref[:, place] = normed.astype(jnp.bfloat16)

    operands = ([kept] if kept is not None else []) + [came] + list(residual_parts)
    operands.append(gain.reshape(1, features))
    out_shape = [jax.ShapeDtypeStruct((rows, features), jnp.bfloat16)] * 2
    return small_kernel(kernel, out_shape, operands, "normalise")


def add_up(hidden, mine, to_back, to_ahead, n_sub):
    chunks = len(hidden)
    rows, features = hidden[0].shape
    width = features // n_sub

    def kernel(*refs):
        terms, out_refs = refs[: 4 * chunks], refs[4 * chunks :]
        sub = lax.axis_index("sub")
        for step, out_ref in enumerate(out_refs):
            place = pl.ds(pl.multiple_of((sub + step) % n_sub * width, width), width)
            for chunk in range(chunks):
                hidden_ref, mine_ref, back_ref, ahead_ref = terms[chunk::chunks]
                mixture = mine_ref[:, place] + back_ref[:, place].astype(jnp.float32)
                mixture = mixture + ahead_ref[:, place].astype(jnp.float32)
                total = hidden_ref[:, place].astype(jnp.float32) + mixture
                out_ref[chunk * rows : (chunk + 1) * rows, :] = total.astype(jnp.bfloat16)

    shape = jax.ShapeDtypeStruct((chunks * rows, width), jnp.bfloat16)
    operands = [*hidden, *mine, *to_back, *to_ahead]
    return small_kernel(kernel, [shape] * n_sub, operands, "add_up")


def stack_rows(parts):
    n_sub = len(parts)
    rows, width = parts[0].shape

    def kernel(*refs):
        sub = lax.axis_index("sub")
        for step, part_ref in enumerate(refs[:-1]):
            first = pl.multiple_of((sub - step) % n_sub * rows, rows)
            refs[-1][pl.ds(first, rows), :] = part_ref[...]

    shape = jax.ShapeDtypeStruct((n_sub * rows, width), parts[0].dtype)
    return small_kernel(kernel, [shape], parts, "stack_rows")[0]


def attend(queries, kv, stages, state, cache_rows, kv_heads, n_hd, chunks, finish=None):
    all_rows, columns = queries.shape
    rows, n_sub = all_rows // n_hd, len(stages[0][1])
    blocks = [block for _, stage_blocks in stages for block in stage_blocks]
    origins = [(hop, step) for hop, _ in stages for step in range(n_sub)]
    per_kv = columns // HD // kv_heads
    stack = 2 if per_kv % 2 == 0 else 1
    part = stack * all_rows
    new_rows = blocks[0].shape[0] - cache_rows - MASK_ROWS
    keys = cache_rows + new_rows
    factor = math.log2(math.e) / math.sqrt(HD)
    relative = n_hd == 2
    last = finish is not None
    weights, earlier, tables = finish if last else ([], None, [])
    head_columns = per_kv * HD
    final = last and kv == kv_heads - 1
    kept_rows = rows if relative else 0
    chunk_rows = rows // chunks if relative else all_rows

    def kernel(*refs):
        q_ref, refs = refs[0], refs[1:]
        block_refs, refs = refs[: len(blocks)], refs[len(blocks) :]
        if state is not None:
            (m_in, acc_in), refs = refs[:2], refs[2:]
        weight_refs, refs = refs[: len(weights)], refs[len(weights) :]
        table_refs, refs = refs[: len(tables)], refs[len(tables) :]
        if earlier is not None:
            earlier_ref, refs = refs[0], refs[1:]
        if last:
            results = len(out_shape)
            result_refs, refs = refs[:results], refs[results:]
            head_ref, refs = refs[0], refs[1:]
            copies = []
            if tables:
                result_refs, own_table_ref = result_refs[:-1], result_refs[-1]
                held_ref, sems = refs
                for i, table_ref in enumerate(table_refs):
                    copies.append(
                        pltpu.make_async_copy(
                            table_ref.at[pl.ds(keys, MASK_ROWS), pl.ds(HD, HD)],
                            held_ref.at[pl.ds(i * MASK_ROWS, MASK_ROWS), :],
                            sems.at[i],
                        )
                    )
                    copies[-1].start()
        else:
            m_out, acc_out = refs
        sub = lax.axis_index("sub")
        ep = lax.axis_index("ep")
        hd = lax.axis_index("hd")
        places = [(hd + j) % n_hd if relative else j for j in range(n_hd)]
        biases = []
        for (hop, step), block in zip(origins, block_refs):
            cache_bias = block[keys : keys + 1, :cache_rows].astype(jnp.float32)
            if hop == 0:
                key_id = ((sub - step) % n_sub) * new_rows + lax.broadcasted_iota(
                    jnp.int32, (rows, new_rows), 1
                )
                row_id = lax.broadcasted_iota(jnp.int32, (rows, new_rows), 0)
                seen = [
                    jnp.where(
                        key_id <= row_id + (place * n_sub + sub) * rows, 0.0, NEG_FILL
                    )
                    for place in places
                ]
                new_bias = jnp.concatenate(seen * stack, axis=0)
                cache_bias = jnp.broadcast_to(cache_bias, (part, cache_rows))
            else:
                new_bias = jnp.full(
                    (1, new_rows), jnp.where(ep >= hop, 0.0, NEG_FILL), jnp.float32
                )
            biases.append(jnp.concatenate([cache_bias, new_bias], axis=1))
        ones = jnp.ones((keys, HD), jnp.bfloat16)
        key_parts = [block[:keys, :HD] for block in block_refs]
        value_parts = [
            jnp.concatenate([block[:keys, HD:], ones], axis=1) for block in block_refs
        ]
        for index in range(per_kv // stack):
            here = slice(index * part, (index + 1) * part)
            heads = range(kv * per_kv + index * stack, kv * per_kv + (index + 1) * stack)
            q = jnp.concatenate([q_ref[:, h * HD : (h + 1) * HD] for h in heads], axis=0)
            terms = [
                lax.dot_general(q, k, CONTRACT_LAST, preferred_element_type=jnp.float32) * factor
                + bias
                for k, bias in zip(key_parts, biases)
            ]
            top = jnp.max(functools.reduce(jnp.maximum, terms), axis=1, keepdims=True)
            top = jnp.broadcast_to(top, (part, LANES))
            if state is not None:
                top_in = m_in[here, :]
                top = jnp.maximum(top, top_in)
            wide_top = jnp.concatenate([top] * (keys // LANES), axis=1)
            acc = None
            for term, v in zip(terms, value_parts):
                exp_terms = jnp.exp2(term - wide_top).astype(jnp.bfloat16)
                product = jnp.dot(exp_terms, v, preferred_element_type=jnp.float32)
                acc = product if acc is None else acc + product
            if state is not None:
                scale = jnp.exp2(top_in - top)
                acc = acc + jnp.concatenate([scale, scale], axis=1) * acc_in[here, :]
            if last:
                out = (acc[:, :HD] / acc[:, HD:]).astype(jnp.bfloat16)
                for s in range(stack):
                    first = (index * stack + s) * HD
                    head_ref[:, first : first + HD] = out[s * all_rows : (s + 1) * all_rows]
            else:
                m_out[here, :] = top
                acc_out[here, :] = acc
        if last:
            source = head_ref[...]
            width = weight_refs[0].shape[1]
            these = slice(kv * head_columns, (kv + 1) * head_columns)
            for i, weight_ref in enumerate(weight_refs):
                here = slice(i * width, (i + 1) * width)
                product = jnp.dot(
                    source, weight_ref[these, :], preferred_element_type=jnp.float32
                )
                if earlier is not None:
                    product = product + earlier_ref[:, here]
                if final:
                    for j, result_ref in enumerate(result_refs):
                        share = product[j * chunk_rows : (j + 1) * chunk_rows]
                        result_ref[:, here] = share.astype(result_ref.dtype)
                else:
                    result_refs[0][:, here] = product
            if tables:
                for copy in copies:
                    copy.wait()
                joint = jnp.concatenate(
                    [
                        held_ref[i * MASK_ROWS : (i + 1) * MASK_ROWS, :].astype(jnp.float32)[
                            :TABLE_ROWS
                        ]
                        for i in range(len(tables))
                    ],
                    axis=0,
                ).astype(jnp.bfloat16)
                own_table_ref[...] = joint
                result_refs[len(result_refs) // 2][: joint.shape[0], features:] = joint

    vmem = pl.BlockSpec(memory_space=pltpu.VMEM)
    scratch = []
    if last:
        features = sum(w.shape[1] for w in weights)
        if final:
            out_shape = [
                jax.ShapeDtypeStruct((chunk_rows, features), kind)
                for kind, count in [
                    (jnp.float32, kept_rows // chunk_rows),
                    (jnp.bfloat16, (all_rows - kept_rows) // chunk_rows),
                ]
                for _ in range(count)
            ]
        else:
            out_shape = (jax.ShapeDtypeStruct((all_rows, features), jnp.float32),)
        scratch = [pltpu.VMEM((all_rows, head_columns), jnp.bfloat16)]
        if tables:
            joint = (len(tables) * TABLE_ROWS, LANES)
            first = len(out_shape) // 2
            out_shape[first] = jax.ShapeDtypeStruct((chunk_rows, features + LANES), jnp.bfloat16)
            out_shape.append(jax.ShapeDtypeStruct(joint, jnp.bfloat16))
            scratch += [
                pltpu.VMEM((len(tables) * MASK_ROWS, LANES), jnp.bfloat16),
                pltpu.SemaphoreType.DMA((len(tables),)),
            ]
    else:
        out_shape = (
            jax.ShapeDtypeStruct((per_kv * all_rows, LANES), jnp.float32),
            jax.ShapeDtypeStruct((per_kv * all_rows, 2 * HD), jnp.float32),
        )
    operands = [queries] + list(blocks) + (list(state) if state is not None else [])
    operands += list(weights)
    in_specs = [vmem] * len(operands) + [pl.BlockSpec(memory_space=pl.ANY)] * len(tables)
    operands += list(tables)
    if earlier is not None:
        operands.append(earlier)
        in_specs.append(vmem)
    scores = all_rows * per_kv * keys * len(blocks)
    return pl.pallas_call(
        kernel,
        out_shape=out_shape,
        in_specs=in_specs,
        out_specs=tuple(vmem for _ in out_shape),
        scratch_shapes=scratch,
        compiler_params=pltpu.CompilerParams(vmem_limit_bytes=16 * MIB),
        cost_estimate=pl.CostEstimate(
            flops=6 * scores * HD, bytes_accessed=4 * MIB, transcendentals=scores
        ),
        name="attend",
    )(*operands)


def apply_expert(inputs, origins, gate_table, gate_up, w_down):
    features = w_down[0].shape[1]
    hidden = w_down[0].shape[0]
    rows = sum(x.shape[0] for x in inputs)
    n_ep, n_hd, n_sub = lax.axis_size("ep"), lax.axis_size("hd"), lax.axis_size("sub")
    chunks = gate_table.shape[0] // n_sub // inputs[0].shape[0]

    def kernel(*refs):
        x_refs, refs = refs[: len(inputs)], refs[len(inputs) :]
        gate_ref, refs = refs[0], refs[1:]
        gu_refs, refs = refs[: len(gate_up)], refs[len(gate_up) :]
        down_refs, out_refs = refs[: len(w_down)], refs[len(w_down) :]
        x = jnp.concatenate([x[...] for x in x_refs], axis=0)
        here = walk_place(lax.axis_index("ep"), lax.axis_index("hd"), n_ep, n_hd)
        columns = []
        for (steps, chunk), x_ref in zip(origins, x_refs):
            count = x_ref.shape[0]
            sub = (lax.axis_index("sub") + steps) % n_sub
            first = pl.multiple_of((sub * chunks + chunk) * count, count)
            table = gate_ref[pl.ds(first, count), :]
            lane = lax.broadcasted_iota(jnp.int32, table.shape, 1)
            chip = (here + steps) % (n_ep * n_hd)
            columns.append(jnp.sum(jnp.where(lane == chip, table, 0.0), axis=1, keepdims=True))
        gate = jnp.concatenate(columns, axis=0)
        total = None
        for gu, down in zip(gu_refs, down_refs):
            gate_part = lax.dot_general(
                x, gu[0], CONTRACT_LAST, preferred_element_type=jnp.float32
            )
            up_part = lax.dot_general(x, gu[1], CONTRACT_LAST, preferred_element_type=jnp.float32)
            activation = (gate_part / (1.0 + jnp.exp(-gate_part)) * up_part).astype(jnp.bfloat16)
            product = jnp.dot(activation, down[...], preferred_element_type=jnp.float32)
            total = product if total is None else total + product
        total = gate * total.astype(jnp.bfloat16).astype(jnp.float32)
        first = 0
        for out_ref in out_refs:
            out_ref[...] = total[first : first + out_ref.shape[0]]
            first += out_ref.shape[0]

    vmem = pl.BlockSpec(memory_space=pltpu.VMEM)
    operands = list(inputs) + [gate_table] + list(gate_up) + list(w_down)
    return pl.pallas_call(
        kernel,
        out_shape=[jax.ShapeDtypeStruct((x.shape[0], features), jnp.float32) for x in inputs],
        in_specs=[vmem] * len(operands),
        out_specs=[vmem] * len(inputs),
        compiler_params=pltpu.CompilerParams(vmem_limit_bytes=16 * MIB),
        cost_estimate=pl.CostEstimate(
            flops=6 * rows * hidden * len(w_down) * features,
            bytes_accessed=6 * MIB,
            transcendentals=rows * hidden * len(w_down),
        ),
        name="apply_expert",
    )(*operands)


def chip_ring(n_ep, n_hd):
    if n_hd == 2:
        return [z * 2 for z in range(n_ep)] + [z * 2 + 1 for z in reversed(range(n_ep))]
    return list(range(n_ep * n_hd))


def add_share(came, share):
    def kernel(came_ref, share_ref, out_ref):
        total = came_ref[...].astype(jnp.float32) + share_ref[...]
        out_ref[...] = total.astype(jnp.bfloat16)

    shape = jax.ShapeDtypeStruct(share.shape, jnp.bfloat16)
    return small_kernel(kernel, [shape], [came, share], "add_share")[0]


def dense_experts(own, gate_table, gate_up, w_down):
    axes = ("ep", "hd", "sub")
    walk = chip_ring(lax.axis_size("ep"), lax.axis_size("hd"))
    size, n_sub = len(walk), lax.axis_size("sub")
    ahead = [
        (walk[i] * n_sub + sub, walk[(i + 1) % size] * n_sub + (sub + 1) % n_sub)
        for i in range(size)
        for sub in range(n_sub)
    ]
    back = [(b, a) for a, b in ahead]
    reach = size // 2
    behind, before, waiting = list(own), list(own), None
    outs = [None]
    for hop in range(1, reach + 1):
        behind[0] = lax.ppermute(behind[0], axes, ahead)
        before[1] = lax.ppermute(before[1], axes, back)
        if hop < reach:
            behind[1] = lax.ppermute(behind[1], axes, ahead)
            before[0] = lax.ppermute(before[0], axes, back)
        if waiting:
            out = apply_expert(waiting, origins, gate_table, gate_up, w_down)
            late = int(hop < reach)
            behind[late], out = lax.optimization_barrier((behind[late], out))
            outs.append(out)
        waiting = [behind[0], before[1]] + ([behind[1], before[0]] if hop < reach else [])
        origins = [(-hop, 0), (hop, 1), (-hop, 1), (hop, 0)][: len(waiting)]
    outs.append(apply_expert(waiting, origins, gate_table, gate_up, w_down))
    to_back, to_ahead = [None, None], [None, None]
    for hop in range(reach, 0, -1):
        shares = outs[hop]
        for chunks, chunk, way, share in [
            (to_back, 0, back, 0),
            (to_ahead, 1, ahead, 1),
            (to_back, 1, back, 2),
            (to_ahead, 0, ahead, 3),
        ]:
            if share >= len(shares):
                continue
            if chunks[chunk] is None:
                sum_here = shares[share].astype(jnp.bfloat16)
            else:
                sum_here = add_share(chunks[chunk], shares[share])
            chunks[chunk] = lax.ppermute(sum_here, axes, way)
            if hop == min(2, reach) and share == 0:
                chunks[chunk], own = lax.optimization_barrier((chunks[chunk], own))
    mine = apply_expert(own, [(0, 0), (0, 1)], gate_table, gate_up, w_down)
    return mine, to_back, to_ahead


def sparse_experts(widened, normed, gate_up, w_down, expert_ids, gates, features):
    half_width = normed.shape[1]
    pair_weights = gate_up[0].reshape(-1, features)
    hidden_units = w_down.shape[1]
    group_total = lax.axis_size("ep")
    group_experts = lax.axis_size("hd")
    all_experts = group_total * group_experts
    block_rows = expert_ids.shape[0]
    group_slots, expert_slots = block_sizes(block_rows, group_total, group_experts)
    chosen = (
        expert_ids[:, :, None] == jnp.arange(all_experts, dtype=jnp.int32)[None, None, :]
    ).astype(jnp.int32)
    named_count = jnp.sum(chosen, axis=1)
    earlier = jnp.cumsum(named_count, axis=0) - named_count
    slot_index = jnp.sum(chosen * earlier[:, None, :], axis=2)
    position = expert_ids * expert_slots + slot_index
    slot_columns = jnp.arange(all_experts * expert_slots, dtype=jnp.int32)
    gate_table = jnp.sum(
        jnp.where(
            position[:, :, None] == slot_columns[None, None, :],
            gates.astype(jnp.float32)[:, :, None],
            0.0,
        ),
        axis=1,
    ).astype(jnp.bfloat16)
    placed = (gate_table != 0).astype(jnp.bfloat16)
    outgoing = jnp.einsum("rq,rd->qd", placed, normed, preferred_element_type=jnp.float32).astype(
        jnp.bfloat16
    )
    outgoing = outgoing.reshape(all_experts, expert_slots, normed.shape[1])
    arrived = lax.all_to_all(outgoing, ("ep", "hd"), split_axis=0, concat_axis=0, tiled=True)
    lead_shape = arrived.shape[:-1]
    rows_in = arrived.reshape(-1, arrived.shape[-1])
    rows_in = lax.all_gather(rows_in, "sub", axis=1, tiled=True)
    projected_pair = jnp.einsum(
        "rd,fd->rf", rows_in, pair_weights, preferred_element_type=jnp.float32
    )
    activation = (
        jax.nn.silu(projected_pair[:, :hidden_units]) * projected_pair[:, hidden_units:]
    ).astype(jnp.bfloat16)
    partial_out = jnp.dot(activation, w_down[0], preferred_element_type=jnp.float32)
    expert_out = lax.psum_scatter(
        partial_out.astype(jnp.bfloat16), "sub", scatter_dimension=1, tiled=True
    )
    results = expert_out.reshape(lead_shape + (expert_out.shape[1],))
    returned = lax.all_to_all(results, ("ep", "hd"), split_axis=0, concat_axis=0, tiled=True)
    mixture = jnp.dot(
        gate_table,
        returned.reshape(all_experts * expert_slots, half_width),
        preferred_element_type=jnp.float32,
    )
    return (widened + mixture).astype(jnp.bfloat16)


def shards(
    queries,
    cache_keys,
    cache_values,
    page_len,
    new_keys,
    new_values,
    out_proj,
    residual,
    norm_gain,
    gate_up,
    w_down,
    expert_ids,
    gates,
):
    n_ep, n_hd, n_sub = lax.axis_size("ep"), lax.axis_size("hd"), lax.axis_size("sub")
    query_rows = queries.shape[0]
    heads_here = queries.shape[1] // HD
    kv_heads = max(1, heads_here // (QH // KVH))
    rows = query_rows // (n_hd * n_sub)
    features = norm_gain.shape[0]
    cache_rows = cache_keys.shape[0]
    all_experts = n_ep * n_hd * gate_up.shape[0]
    dense = (
        expert_ids.shape[1] == all_experts
        and gate_up.shape[0] == 1
        and n_hd == 2
        and rows % 32 == 0
        and all_experts <= TABLE_ROWS
        and cache_rows <= HD
        and n_ep * TABLE_ROWS <= rows // 2
        and expert_ids.shape[0] == LANES
    )

    packed = pack_keys(
        cache_keys,
        cache_values,
        new_keys,
        new_values,
        page_len,
        [expert_ids.T, gates.T] if dense else [],
        kv_heads,
        heads_here,
    )
    query_rows_here = choose_queries(queries.reshape(n_hd, n_sub, rows, heads_here * HD))
    reach = n_ep // 2
    up, down = list(packed), list(packed)
    arrived = [[(0, x)] for x in packed]
    tables = {}
    states = [None] * kv_heads
    earlier = None
    for distance in range(reach + 1):
        stages = [[(hop, sub_copies(x)) for hop, x in blocks] for blocks in arrived]
        if distance == 0:
            out_proj, packed = lax.optimization_barrier((out_proj, packed))
            projections = sub_copies(out_proj)
        if distance == reach and dense:
            blocks = [x for kv_stages in stages for _, x in kv_stages]
            gate_up, w_down, blocks = lax.optimization_barrier((gate_up, w_down, blocks))
            stages = [
                [(hop, blocks.pop(0)) for hop, _ in kv_stages] for kv_stages in stages
            ]
            gate_up_parts = sub_copies(gate_up[0])
            w_down_parts = sub_copies(w_down[0])
        for hop, x in arrived[0]:
            tables[hop] = x
        onward = [[] for _ in packed]
        if distance < reach:
            opposite = 2 * (distance + 1) == n_ep
            for kv in range(kv_heads):
                if not opposite or kv % 2 == 0:
                    up[kv] = lax.ppermute(up[kv], "ep", cycle(n_ep))
                    onward[kv].append((distance + 1, up[kv]))
                if not opposite or kv % 2 == 1:
                    down[kv] = lax.ppermute(down[kv], "ep", cycle(n_ep, n_ep - 1))
                    onward[kv].append((n_ep - distance - 1, down[kv]))
        for kv in range(kv_heads):
            finish = None
            if distance == reach:
                joint = [tables[hop] for hop in range(n_ep)] if dense and kv == kv_heads - 1 else []
                finish = (projections, earlier, joint)
            states[kv] = attend(
                query_rows_here,
                kv,
                stages[kv],
                states[kv],
                cache_rows,
                kv_heads,
                n_hd,
                2 if dense else 1,
                finish,
            )
            if finish:
                earlier = states[kv][0]
                continue
            came = [x for _, x in onward[kv]]
            came, states[kv] = lax.optimization_barrier((came, states[kv]))
            onward[kv] = [(hop, x) for (hop, _), x in zip(onward[kv], came)]
            for hop, x in onward[kv]:
                if hop == distance + 1:
                    up[kv] = x
                else:
                    down[kv] = x
        if distance == 0:
            residual, states[0] = lax.optimization_barrier((residual, states[0]))
            residual_parts = hand_over(split_rows(residual, n_sub))
        arrived = onward
    parts = states[-1]
    if dense:
        *parts, own_table = parts
    if n_hd == 2:
        kept, sent = parts[: len(parts) // 2], parts[len(parts) // 2 :]
        came = [lax.ppermute(x, "hd", cycle(n_hd)) for x in sent]
        if dense:
            gate_table = gates_by_chip(own_table, came[0], n_ep, n_hd)
    else:
        kept = [None]
        came = [lax.psum_scatter(parts[0], "hd", scatter_dimension=0, tiled=True)]
    hidden, normed = [], []
    for index, (kept_chunk, came_chunk) in enumerate(zip(kept, came)):
        pair = normalise(
            kept_chunk,
            came_chunk,
            residual_parts,
            norm_gain,
            index * came_chunk.shape[0],
        )
        hidden.append(pair[0])
        normed.append(pair[1])
    if not dense:
        own_columns = [
            jnp.concatenate(by_sub(sub_exchange(x, 1)), axis=0) for x in (hidden[0], normed[0])
        ]
        return sparse_experts(
            own_columns[0].astype(jnp.float32),
            own_columns[1],
            gate_up,
            w_down,
            expert_ids,
            gates,
            features,
        )
    mine, to_back, to_ahead = dense_experts(normed, gate_table, gate_up_parts, w_down_parts)
    return stack_rows(hand_over(add_up(hidden, mine, to_back, to_ahead, n_sub)))


def solution(mesh):
    return jax.shard_map(
        shards,
        mesh=mesh,
        in_specs=(
            P(("grp", "ep"), "hd"),
            P(("grp", "ep", "sub"), None),
            P(("grp", "ep", "sub"), None),
            P(("grp", "ep", "sub")),
            P(("grp", "ep", "sub"), None),
            P(("grp", "ep", "sub"), None),
            P("hd", "sub"),
            P(("grp", "ep", "hd"), "sub"),
            P(),
            P(("ep", "hd"), None, "sub", None),
            P(("ep", "hd"), "sub", None),
            P(("grp", "ep", "hd"), None),
            P(("grp", "ep", "hd"), None),
        ),
        out_specs=P(("grp", "ep", "hd"), "sub"),
        check_vma=False,
    )
```

```python
import functools
import math

import jax
import jax.numpy as jnp
from jax import lax
from jax.experimental import pallas as pl
from jax.experimental.pallas import tpu as pltpu
from jax.sharding import PartitionSpec as P

QH = 32
KVH = 4
HD = 128
GROUPS_ROW = 4
NEG_FILL = -1e30
EPSILON = 1e-06
MASK_ROWS = 16
TABLE_ROWS = 8
LANES = 128
MIB = 1024 * 1024
CONTRACT_LAST = (((1,), (1,)), ((), ()))


def block_sizes(block_rows, group_total, experts_group):
    group_slots = min(block_rows, 3 * GROUPS_ROW * block_rows // (2 * group_total))
    return (group_slots, 2 * group_slots // experts_group)


def cycle(size, step=1):
    return [(i, (i + step) % size) for i in range(size)]


def sub_copies(x):
    size = lax.axis_size("sub")
    return [x] + [lax.ppermute(x, "sub", cycle(size, step)) for step in range(1, size)]


def by_sub(copies):
    size = len(copies)
    me = lax.axis_index("sub")
    ordered = []
    for target in range(size):
        value = copies[0]
        for step in range(1, size):
            value = jnp.where((me - step) % size == target, copies[step], value)
        ordered.append(value)
    return ordered


def sub_exchange(x, axis):
    size = lax.axis_size("sub")
    me = lax.axis_index("sub")
    length = x.shape[axis] // size

    def part(index):
        return lax.dynamic_slice_in_dim(x, index * length, length, axis)

    came = [part(me)]
    for step in range(1, size):
        came.append(lax.ppermute(part((me + step) % size), "sub", cycle(size, step)))
    return came


def pack_keys(cache_keys, cache_values, new_keys, new_values, page_len, routing, kv_heads, heads_here):
    cache_rows, new_rows = cache_keys.shape[0], new_keys.shape[0]
    group_width = QH // KVH
    rows = cache_rows + new_rows + MASK_ROWS

    def kernel(page_ref, ck_ref, cv_ref, nk_ref, nv_ref, *refs):
        routing_refs, out_refs = refs[: len(routing)], refs[len(routing) :]
        first = lax.axis_index("hd") * heads_here // group_width
        lane = lax.broadcasted_iota(jnp.int32, (MASK_ROWS, 2 * HD), 1)
        bias = jnp.where(lane < page_ref[0], 0.0, NEG_FILL).astype(jnp.bfloat16)
        for kv, out_ref in enumerate(out_refs):
            columns = pl.ds(pl.multiple_of((first + kv) * HD, HD), HD)
            out_ref[:cache_rows, :HD] = ck_ref[:, columns]
            out_ref[:cache_rows, HD:] = cv_ref[:, columns]
            out_ref[cache_rows : cache_rows + new_rows, :HD] = nk_ref[:, columns]
            out_ref[cache_rows : cache_rows + new_rows, HD:] = nv_ref[:, columns]
            out_ref[cache_rows + new_rows :, :] = bias
        if routing:
            ids = routing_refs[0][...]
            gates = routing_refs[1][...].astype(jnp.float32)
            expert = lax.broadcasted_iota(jnp.int32, (MASK_ROWS, ids.shape[1]), 0)
            table = jnp.zeros(expert.shape, jnp.float32)
            for k in range(ids.shape[0]):
                table = table + jnp.where(ids[k : k + 1, :] == expert, gates[k : k + 1, :], 0.0)
            out_refs[0][cache_rows + new_rows :, HD:] = table.astype(jnp.bfloat16)

    vmem = pl.BlockSpec(memory_space=pltpu.VMEM)
    return pl.pallas_call(
        kernel,
        out_shape=[jax.ShapeDtypeStruct((rows, 2 * HD), cache_keys.dtype)] * kv_heads,
        in_specs=[pl.BlockSpec(memory_space=pltpu.SMEM)] + [vmem] * (4 + len(routing)),
        out_specs=[vmem] * kv_heads,
        name="pack_keys",
    )(page_len, cache_keys, cache_values, new_keys, new_values, *routing)


def small_kernel(kernel, out_shape, operands, name):
    vmem = pl.BlockSpec(memory_space=pltpu.VMEM)
    return pl.pallas_call(
        kernel,
        out_shape=out_shape,
        in_specs=[vmem] * len(operands),
        out_specs=[vmem] * len(out_shape),
        compiler_params=pltpu.CompilerParams(vmem_limit_bytes=8 * MIB),
        cost_estimate=pl.CostEstimate(flops=MIB, bytes_accessed=MIB, transcendentals=0),
        name=name,
    )(*operands)


def hand_over(parts):
    size = len(parts)
    return [parts[0]] + [
        lax.ppermute(part, "sub", cycle(size, step)) for step, part in enumerate(parts) if step
    ]


def choose_queries(queries):
    n_hd, n_sub, rows, columns = queries.shape

    def kernel(in_ref, out_ref, sems):
        sub = lax.axis_index("sub")
        hd = lax.axis_index("hd")
        copies = []
        for j in range(n_hd):
            place = (hd + j) % n_hd if n_hd == 2 else j
            copies.append(
                pltpu.make_async_copy(
                    in_ref.at[place, sub], out_ref.at[pl.ds(j * rows, rows), :], sems.at[j]
                )
            )
            copies[-1].start()
        for copy in copies:
            copy.wait()

    return pl.pallas_call(
        kernel,
        out_shape=jax.ShapeDtypeStruct((n_hd * rows, columns), queries.dtype),
        in_specs=[pl.BlockSpec(memory_space=pltpu.HBM)],
        out_specs=pl.BlockSpec(memory_space=pltpu.VMEM),
        scratch_shapes=[pltpu.SemaphoreType.DMA((n_hd,))],
        compiler_params=pltpu.CompilerParams(vmem_limit_bytes=8 * MIB),
        name="choose_queries",
    )(queries)


def split_rows(residual, n_sub):
    rows, columns = residual.shape[0] // n_sub, residual.shape[1]

    def kernel(in_ref, *out_refs):
        sub = lax.axis_index("sub")
        for step, out_ref in enumerate(out_refs):
            first = pl.multiple_of((sub + step) % n_sub * rows, rows)
            out_ref[...] = in_ref[pl.ds(first, rows), :]

    shape = jax.ShapeDtypeStruct((rows, columns), residual.dtype)
    return small_kernel(kernel, [shape] * n_sub, [residual], "split_rows")


def walk_place(ep, hd, n_ep, n_hd):
    if n_hd == 2:
        return jnp.where(hd == 0, ep, 2 * n_ep - 1 - ep)
    return ep * n_hd + hd


def gates_by_chip(own, came, n_ep, n_hd):
    block_rows = own.shape[1]
    places = slice(came.shape[1] - block_rows, came.shape[1])

    def kernel(own_ref, came_ref, out_ref):
        ep, hd = lax.axis_index("ep"), lax.axis_index("hd")
        mine = ep * n_hd + hd
        expert = lax.broadcasted_iota(jnp.int32, (TABLE_ROWS, block_rows), 0)
        place = lax.broadcasted_iota(jnp.int32, (LANES, block_rows), 0)
        table = jnp.zeros((LANES, block_rows), jnp.float32)
        tables = [(own_ref[...], hd), (came_ref[: n_ep * TABLE_ROWS, places], 1 - hd)]
        for joint, other in tables:
            joint = joint.astype(jnp.float32)
            for hop in range(n_ep):
                tile = joint[hop * TABLE_ROWS : (hop + 1) * TABLE_ROWS, :]
                row = jnp.sum(jnp.where(expert == mine, tile, 0.0), axis=0, keepdims=True)
                chip = walk_place((ep - hop) % n_ep, other, n_ep, n_hd)
                table = jnp.where(place == chip, row, table)
        out_ref[...] = table.T

    shape = jax.ShapeDtypeStruct((block_rows, LANES), jnp.float32)
    return small_kernel(kernel, [shape], [own, came], "gates_by_chip")[0]


def normalise(kept, came, residual_parts, gain, first):
    n_sub = len(residual_parts)
    rows, width = came.shape[0], residual_parts[0].shape[1]
    chunk = slice(first, first + rows)
    features = n_sub * width

    def kernel(*refs):
        refs = list(refs)
        kept_ref = refs.pop(0) if kept is not None else None
        came_ref = refs.pop(0)
        part_refs = [refs.pop(0) for _ in residual_parts]
        gain_ref = refs.pop(0)
        hidden_ref, normed_ref = refs
        sub = lax.axis_index("sub")
        hidden, places, squares = [], [], 0.0
        for step, part_ref in enumerate(part_refs):
            here = slice(step * width, (step + 1) * width)
            projected = came_ref[:, here].astype(jnp.float32)
            if kept is not None:
                projected = kept_ref[:, here] + projected
            value = (part_ref[chunk, :].astype(jnp.float32) + projected).astype(jnp.bfloat16)
            hidden.append(value)
            place = pl.ds(pl.multiple_of((sub - step) % n_sub * width, width), width)
            places.append(place)
            hidden_ref[:, place] = value
            wide = value.astype(jnp.float32)
            squares = squares + jnp.sum(wide * wide, axis=1, keepdims=True)
        scale = lax.rsqrt(squares / features + EPSILON)
        for value, place in zip(hidden, places):
            normed = value.astype(jnp.float32) * scale * gain_ref[:, place].astype(jnp.float32)
            normed_ref[:, place] = normed.astype(jnp.bfloat16)

    operands = ([kept] if kept is not None else []) + [came] + list(residual_parts)
    operands.append(gain.reshape(1, features))
    out_shape = [jax.ShapeDtypeStruct((rows, features), jnp.bfloat16)] * 2
    return small_kernel(kernel, out_shape, operands, "normalise")


def add_up(hidden, mine, to_back, to_ahead, n_sub):
    chunks = len(hidden)
    rows, features = hidden[0].shape
    width = features // n_sub

    def kernel(*refs):
        terms, out_refs = refs[: 4 * chunks], refs[4 * chunks :]
        sub = lax.axis_index("sub")
        for step, out_ref in enumerate(out_refs):
            place = pl.ds(pl.multiple_of((sub + step) % n_sub * width, width), width)
            for chunk in range(chunks):
                hidden_ref, mine_ref, back_ref, ahead_ref = terms[chunk::chunks]
                mixture = mine_ref[:, place] + back_ref[:, place].astype(jnp.float32)
                mixture = mixture + ahead_ref[:, place].astype(jnp.float32)
                total = hidden_ref[:, place].astype(jnp.float32) + mixture
                out_ref[chunk * rows : (chunk + 1) * rows, :] = total.astype(jnp.bfloat16)

    shape = jax.ShapeDtypeStruct((chunks * rows, width), jnp.bfloat16)
    operands = [*hidden, *mine, *to_back, *to_ahead]
    return small_kernel(kernel, [shape] * n_sub, operands, "add_up")


def stack_rows(parts):
    n_sub = len(parts)
    rows, width = parts[0].shape

    def kernel(*refs):
        sub = lax.axis_index("sub")
        for step, part_ref in enumerate(refs[:-1]):
            first = pl.multiple_of((sub - step) % n_sub * rows, rows)
            refs[-1][pl.ds(first, rows), :] = part_ref[...]

    shape = jax.ShapeDtypeStruct((n_sub * rows, width), parts[0].dtype)
    return small_kernel(kernel, [shape], parts, "stack_rows")[0]


def attend(queries, kv, stages, state, cache_rows, kv_heads, n_hd, chunks, finish=None):
    all_rows, columns = queries.shape
    rows, n_sub = all_rows // n_hd, len(stages[0][1])
    blocks = [block for _, stage_blocks in stages for block in stage_blocks]
    origins = [(hop, step) for hop, _ in stages for step in range(n_sub)]
    per_kv = columns // HD // kv_heads
    stack = 1
    part = stack * all_rows
    new_rows = blocks[0].shape[0] - cache_rows - MASK_ROWS
    keys = cache_rows + new_rows
    factor = math.log2(math.e) / math.sqrt(HD)
    relative = n_hd == 2
    last = finish is not None
    weights, earlier, tables = finish if last else ([], [], [])
    head_columns = per_kv * HD
    final = last and kv == kv_heads - 1
    kept_rows = rows if relative else 0
    chunk_rows = rows // chunks if relative else all_rows

    def kernel(*refs):
        q_ref, refs = refs[0], refs[1:]
        block_refs, refs = refs[: len(blocks)], refs[len(blocks) :]
        if state is not None:
            (m_in, acc_in), refs = refs[:2], refs[2:]
        weight_refs, refs = refs[: len(weights)], refs[len(weights) :]
        table_refs, refs = refs[: len(tables)], refs[len(tables) :]
        earlier_refs, refs = refs[: len(earlier)], refs[len(earlier) :]
        if last:
            results = len(out_shape)
            result_refs, refs = refs[:results], refs[results:]
            head_ref, refs = refs[0], refs[1:]
            copies = []
            if tables:
                result_refs, own_table_ref = result_refs[:-1], result_refs[-1]
                held_ref, sems = refs
                for i, table_ref in enumerate(table_refs):
                    copies.append(
                        pltpu.make_async_copy(
                            table_ref.at[pl.ds(keys, MASK_ROWS), pl.ds(HD, HD)],
                            held_ref.at[pl.ds(i * MASK_ROWS, MASK_ROWS), :],
                            sems.at[i],
                        )
                    )
                    copies[-1].start()
        else:
            m_out, acc_out = refs
        sub = lax.axis_index("sub")
        ep = lax.axis_index("ep")
        hd = lax.axis_index("hd")
        places = [(hd + j) % n_hd if relative else j for j in range(n_hd)]
        biases = []
        for (hop, step), block in zip(origins, block_refs):
            cache_bias = block[keys : keys + 1, :cache_rows].astype(jnp.float32)
            if hop == 0:
                key_id = ((sub - step) % n_sub) * new_rows + lax.broadcasted_iota(
                    jnp.int32, (rows, new_rows), 1
                )
                row_id = lax.broadcasted_iota(jnp.int32, (rows, new_rows), 0)
                seen = [
                    jnp.where(
                        key_id <= row_id + (place * n_sub + sub) * rows, 0.0, NEG_FILL
                    )
                    for place in places
                ]
                new_bias = jnp.concatenate(seen * stack, axis=0)
                cache_bias = jnp.broadcast_to(cache_bias, (part, cache_rows))
            else:
                new_bias = jnp.full(
                    (1, new_rows), jnp.where(ep >= hop, 0.0, NEG_FILL), jnp.float32
                )
            biases.append(jnp.concatenate([cache_bias, new_bias], axis=1))
        ones = jnp.ones((keys, HD), jnp.bfloat16)
        key_parts = [block[:keys, :HD] for block in block_refs]
        value_parts = [
            jnp.concatenate([block[:keys, HD:], ones], axis=1) for block in block_refs
        ]
        for index in range(per_kv // stack):
            here = slice(index * part, (index + 1) * part)
            heads = range(kv * per_kv + index * stack, kv * per_kv + (index + 1) * stack)
            q = jnp.concatenate([q_ref[:, h * HD : (h + 1) * HD] for h in heads], axis=0)
            terms = [
                lax.dot_general(q, k, CONTRACT_LAST, preferred_element_type=jnp.float32) * factor
                + bias
                for k, bias in zip(key_parts, biases)
            ]
            top = jnp.max(functools.reduce(jnp.maximum, terms), axis=1, keepdims=True)
            top = jnp.broadcast_to(top, (part, LANES))
            if state is not None:
                top_in = m_in[here, :]
                top = jnp.maximum(top, top_in)
            wide_top = jnp.concatenate([top] * (keys // LANES), axis=1)
            acc = None
            for term, v in zip(terms, value_parts):
                exp_terms = jnp.exp2(term - wide_top).astype(jnp.bfloat16)
                product = jnp.dot(exp_terms, v, preferred_element_type=jnp.float32)
                acc = product if acc is None else acc + product
            if state is not None:
                scale = jnp.exp2(top_in - top)
                acc = acc + jnp.concatenate([scale, scale], axis=1) * acc_in[here, :]
            if last:
                out = (acc[:, :HD] / acc[:, HD:]).astype(jnp.bfloat16)
                for s in range(stack):
                    first = (index * stack + s) * HD
                    head_ref[:, first : first + HD] = out[s * all_rows : (s + 1) * all_rows]
            else:
                m_out[here, :] = top
                acc_out[here, :] = acc
        if last:
            source = jnp.concatenate([ref[...] for ref in earlier_refs] + [head_ref[...]], axis=1)
            for i, weight_ref in enumerate(weight_refs):
                width = weight_ref.shape[1]
                here = slice(i * width, (i + 1) * width)
                product = jnp.dot(source, weight_ref[...], preferred_element_type=jnp.float32)
                for j, result_ref in enumerate(result_refs):
                    share = product[j * chunk_rows : (j + 1) * chunk_rows]
                    result_ref[:, here] = share.astype(result_ref.dtype)
            if not final:
                result_refs[0][...] = head_ref[...]
            if tables:
                for copy in copies:
                    copy.wait()
                joint = jnp.concatenate(
                    [
                        held_ref[i * MASK_ROWS : (i + 1) * MASK_ROWS, :].astype(jnp.float32)[
                            :TABLE_ROWS
                        ]
                        for i in range(len(tables))
                    ],
                    axis=0,
                ).astype(jnp.bfloat16)
                own_table_ref[...] = joint
                result_refs[len(result_refs) // 2][: joint.shape[0], features:] = joint

    vmem = pl.BlockSpec(memory_space=pltpu.VMEM)
    scratch = []
    if last:
        features = sum(w.shape[1] for w in weights)
        if final:
            out_shape = [
                jax.ShapeDtypeStruct((chunk_rows, features), kind)
                for kind, count in [
                    (jnp.float32, kept_rows // chunk_rows),
                    (jnp.bfloat16, (all_rows - kept_rows) // chunk_rows),
                ]
                for _ in range(count)
            ]
        else:
            out_shape = [jax.ShapeDtypeStruct((all_rows, head_columns), jnp.bfloat16)]
        scratch = [pltpu.VMEM((all_rows, head_columns), jnp.bfloat16)]
        if tables:
            joint = (len(tables) * TABLE_ROWS, LANES)
            first = len(out_shape) // 2
            out_shape[first] = jax.ShapeDtypeStruct((chunk_rows, features + LANES), jnp.bfloat16)
            out_shape.append(jax.ShapeDtypeStruct(joint, jnp.bfloat16))
            scratch += [
                pltpu.VMEM((len(tables) * MASK_ROWS, LANES), jnp.bfloat16),
                pltpu.SemaphoreType.DMA((len(tables),)),
            ]
    else:
        out_shape = (
            jax.ShapeDtypeStruct((per_kv * all_rows, LANES), jnp.float32),
            jax.ShapeDtypeStruct((per_kv * all_rows, 2 * HD), jnp.float32),
        )
    operands = [queries] + list(blocks) + (list(state) if state is not None else [])
    operands += list(weights)
    in_specs = [vmem] * len(operands) + [pl.BlockSpec(memory_space=pl.ANY)] * len(tables)
    operands += list(tables)
    operands += list(earlier)
    in_specs += [vmem] * len(earlier)
    scores = all_rows * per_kv * keys * len(blocks)
    return pl.pallas_call(
        kernel,
        out_shape=out_shape,
        in_specs=in_specs,
        out_specs=tuple(vmem for _ in out_shape),
        scratch_shapes=scratch,
        compiler_params=pltpu.CompilerParams(vmem_limit_bytes=16 * MIB),
        cost_estimate=pl.CostEstimate(
            flops=6 * scores * HD, bytes_accessed=4 * MIB, transcendentals=scores
        ),
        name="attend",
    )(*operands)


def apply_expert(inputs, origins, gate_table, gate_up, w_down):
    features = w_down[0].shape[1]
    hidden = w_down[0].shape[0]
    rows = sum(x.shape[0] for x in inputs)
    n_ep, n_hd, n_sub = lax.axis_size("ep"), lax.axis_size("hd"), lax.axis_size("sub")
    chunks = gate_table.shape[0] // n_sub // inputs[0].shape[0]

    def kernel(*refs):
        x_refs, refs = refs[: len(inputs)], refs[len(inputs) :]
        gate_ref, refs = refs[0], refs[1:]
        gu_refs, refs = refs[: len(gate_up)], refs[len(gate_up) :]
        down_refs, out_refs = refs[: len(w_down)], refs[len(w_down) :]
        x = jnp.concatenate([x[...] for x in x_refs], axis=0)
        here = walk_place(lax.axis_index("ep"), lax.axis_index("hd"), n_ep, n_hd)
        columns = []
        for (steps, chunk), x_ref in zip(origins, x_refs):
            count = x_ref.shape[0]
            sub = (lax.axis_index("sub") + steps) % n_sub
            first = pl.multiple_of((sub * chunks + chunk) * count, count)
            table = gate_ref[pl.ds(first, count), :]
            lane = lax.broadcasted_iota(jnp.int32, table.shape, 1)
            chip = (here + steps) % (n_ep * n_hd)
            columns.append(jnp.sum(jnp.where(lane == chip, table, 0.0), axis=1, keepdims=True))
        gate = jnp.concatenate(columns, axis=0)
        total = None
        for gu, down in zip(gu_refs, down_refs):
            gate_part = lax.dot_general(
                x, gu[0], CONTRACT_LAST, preferred_element_type=jnp.float32
            )
            up_part = lax.dot_general(x, gu[1], CONTRACT_LAST, preferred_element_type=jnp.float32)
            activation = (gate_part / (1.0 + jnp.exp(-gate_part)) * up_part).astype(jnp.bfloat16)
            product = jnp.dot(activation, down[...], preferred_element_type=jnp.float32)
            total = product if total is None else total + product
        total = gate * total.astype(jnp.bfloat16).astype(jnp.float32)
        first = 0
        for out_ref in out_refs:
            out_ref[...] = total[first : first + out_ref.shape[0]]
            first += out_ref.shape[0]

    vmem = pl.BlockSpec(memory_space=pltpu.VMEM)
    operands = list(inputs) + [gate_table] + list(gate_up) + list(w_down)
    return pl.pallas_call(
        kernel,
        out_shape=[jax.ShapeDtypeStruct((x.shape[0], features), jnp.float32) for x in inputs],
        in_specs=[vmem] * len(operands),
        out_specs=[vmem] * len(inputs),
        compiler_params=pltpu.CompilerParams(vmem_limit_bytes=16 * MIB),
        cost_estimate=pl.CostEstimate(
            flops=6 * rows * hidden * len(w_down) * features,
            bytes_accessed=6 * MIB,
            transcendentals=rows * hidden * len(w_down),
        ),
        name="apply_expert",
    )(*operands)


def chip_ring(n_ep, n_hd):
    if n_hd == 2:
        return [z * 2 for z in range(n_ep)] + [z * 2 + 1 for z in reversed(range(n_ep))]
    return list(range(n_ep * n_hd))


def add_share(came, share):
    def kernel(came_ref, share_ref, out_ref):
        total = came_ref[...].astype(jnp.float32) + share_ref[...]
        out_ref[...] = total.astype(jnp.bfloat16)

    shape = jax.ShapeDtypeStruct(share.shape, jnp.bfloat16)
    return small_kernel(kernel, [shape], [came, share], "add_share")[0]


def dense_experts(own, gate_table, gate_up, w_down):
    axes = ("ep", "hd", "sub")
    walk = chip_ring(lax.axis_size("ep"), lax.axis_size("hd"))
    size, n_sub = len(walk), lax.axis_size("sub")
    ahead = [
        (walk[i] * n_sub + sub, walk[(i + 1) % size] * n_sub + (sub + 1) % n_sub)
        for i in range(size)
        for sub in range(n_sub)
    ]
    back = [(b, a) for a, b in ahead]
    reach = size // 2
    behind, before, waiting = list(own), list(own), None
    outs = [None]
    for hop in range(1, reach + 1):
        behind[0] = lax.ppermute(behind[0], axes, ahead)
        before[1] = lax.ppermute(before[1], axes, back)
        if hop < reach:
            behind[1] = lax.ppermute(behind[1], axes, ahead)
            before[0] = lax.ppermute(before[0], axes, back)
        if waiting:
            out = apply_expert(waiting, origins, gate_table, gate_up, w_down)
            late = int(hop < reach)
            behind[late], out = lax.optimization_barrier((behind[late], out))
            outs.append(out)
        waiting = [behind[0], before[1]] + ([behind[1], before[0]] if hop < reach else [])
        origins = [(-hop, 0), (hop, 1), (-hop, 1), (hop, 0)][: len(waiting)]
    outs.append(apply_expert(waiting, origins, gate_table, gate_up, w_down))
    to_back, to_ahead = [None, None], [None, None]
    for hop in range(reach, 0, -1):
        shares = outs[hop]
        for chunks, chunk, way, share in [
            (to_back, 0, back, 0),
            (to_ahead, 1, ahead, 1),
            (to_back, 1, back, 2),
            (to_ahead, 0, ahead, 3),
        ]:
            if share >= len(shares):
                continue
            if chunks[chunk] is None:
                sum_here = shares[share].astype(jnp.bfloat16)
            else:
                sum_here = add_share(chunks[chunk], shares[share])
            chunks[chunk] = lax.ppermute(sum_here, axes, way)
            if hop == min(2, reach) and share == 0:
                chunks[chunk], own = lax.optimization_barrier((chunks[chunk], own))
    mine = apply_expert(own, [(0, 0), (0, 1)], gate_table, gate_up, w_down)
    return mine, to_back, to_ahead


def sparse_experts(widened, normed, gate_up, w_down, expert_ids, gates, features):
    half_width = normed.shape[1]
    pair_weights = gate_up[0].reshape(-1, features)
    hidden_units = w_down.shape[1]
    group_total = lax.axis_size("ep")
    group_experts = lax.axis_size("hd")
    all_experts = group_total * group_experts
    block_rows = expert_ids.shape[0]
    group_slots, expert_slots = block_sizes(block_rows, group_total, group_experts)
    chosen = (
        expert_ids[:, :, None] == jnp.arange(all_experts, dtype=jnp.int32)[None, None, :]
    ).astype(jnp.int32)
    named_count = jnp.sum(chosen, axis=1)
    earlier = jnp.cumsum(named_count, axis=0) - named_count
    slot_index = jnp.sum(chosen * earlier[:, None, :], axis=2)
    position = expert_ids * expert_slots + slot_index
    slot_columns = jnp.arange(all_experts * expert_slots, dtype=jnp.int32)
    gate_table = jnp.sum(
        jnp.where(
            position[:, :, None] == slot_columns[None, None, :],
            gates.astype(jnp.float32)[:, :, None],
            0.0,
        ),
        axis=1,
    ).astype(jnp.bfloat16)
    placed = (gate_table != 0).astype(jnp.bfloat16)
    outgoing = jnp.einsum("rq,rd->qd", placed, normed, preferred_element_type=jnp.float32).astype(
        jnp.bfloat16
    )
    outgoing = outgoing.reshape(all_experts, expert_slots, normed.shape[1])
    arrived = lax.all_to_all(outgoing, ("ep", "hd"), split_axis=0, concat_axis=0, tiled=True)
    lead_shape = arrived.shape[:-1]
    rows_in = arrived.reshape(-1, arrived.shape[-1])
    rows_in = lax.all_gather(rows_in, "sub", axis=1, tiled=True)
    projected_pair = jnp.einsum(
        "rd,fd->rf", rows_in, pair_weights, preferred_element_type=jnp.float32
    )
    activation = (
        jax.nn.silu(projected_pair[:, :hidden_units]) * projected_pair[:, hidden_units:]
    ).astype(jnp.bfloat16)
    partial_out = jnp.dot(activation, w_down[0], preferred_element_type=jnp.float32)
    expert_out = lax.psum_scatter(
        partial_out.astype(jnp.bfloat16), "sub", scatter_dimension=1, tiled=True
    )
    results = expert_out.reshape(lead_shape + (expert_out.shape[1],))
    returned = lax.all_to_all(results, ("ep", "hd"), split_axis=0, concat_axis=0, tiled=True)
    mixture = jnp.dot(
        gate_table,
        returned.reshape(all_experts * expert_slots, half_width),
        preferred_element_type=jnp.float32,
    )
    return (widened + mixture).astype(jnp.bfloat16)


def shards(
    queries,
    cache_keys,
    cache_values,
    page_len,
    new_keys,
    new_values,
    out_proj,
    residual,
    norm_gain,
    gate_up,
    w_down,
    expert_ids,
    gates,
):
    n_ep, n_hd, n_sub = lax.axis_size("ep"), lax.axis_size("hd"), lax.axis_size("sub")
    query_rows = queries.shape[0]
    heads_here = queries.shape[1] // HD
    kv_heads = max(1, heads_here // (QH // KVH))
    rows = query_rows // (n_hd * n_sub)
    features = norm_gain.shape[0]
    cache_rows = cache_keys.shape[0]
    all_experts = n_ep * n_hd * gate_up.shape[0]
    dense = (
        expert_ids.shape[1] == all_experts
        and gate_up.shape[0] == 1
        and n_hd == 2
        and rows % 32 == 0
        and all_experts <= TABLE_ROWS
        and cache_rows <= HD
        and n_ep * TABLE_ROWS <= rows // 2
        and expert_ids.shape[0] == LANES
    )

    packed = pack_keys(
        cache_keys,
        cache_values,
        new_keys,
        new_values,
        page_len,
        [expert_ids.T, gates.T] if dense else [],
        kv_heads,
        heads_here,
    )
    query_rows_here = choose_queries(queries.reshape(n_hd, n_sub, rows, heads_here * HD))
    reach = n_ep // 2
    up, down = list(packed), list(packed)
    arrived = [[(0, x)] for x in packed]
    tables = {}
    states = [None] * kv_heads
    attended = []
    for distance in range(reach + 1):
        stages = [[(hop, sub_copies(x)) for hop, x in blocks] for blocks in arrived]
        if distance == 0:
            out_proj, packed = lax.optimization_barrier((out_proj, packed))
            projections = sub_copies(out_proj)
        if distance == reach and dense:
            blocks = [x for kv_stages in stages for _, x in kv_stages]
            gate_up, w_down, blocks = lax.optimization_barrier((gate_up, w_down, blocks))
            stages = [
                [(hop, blocks.pop(0)) for hop, _ in kv_stages] for kv_stages in stages
            ]
            gate_up_parts = sub_copies(gate_up[0])
            w_down_parts = sub_copies(w_down[0])
        for hop, x in arrived[0]:
            tables[hop] = x
        onward = [[] for _ in packed]
        if distance < reach:
            opposite = 2 * (distance + 1) == n_ep
            for kv in range(kv_heads):
                if not opposite or kv % 2 == 0:
                    up[kv] = lax.ppermute(up[kv], "ep", cycle(n_ep))
                    onward[kv].append((distance + 1, up[kv]))
                if not opposite or kv % 2 == 1:
                    down[kv] = lax.ppermute(down[kv], "ep", cycle(n_ep, n_ep - 1))
                    onward[kv].append((n_ep - distance - 1, down[kv]))
        for kv in range(kv_heads):
            finish = None
            if distance == reach:
                joint = [tables[hop] for hop in range(n_ep)] if dense and kv == kv_heads - 1 else []
                finish = (projections, list(attended), joint)
                if kv < kv_heads - 1:
                    finish = ([], [], [])
            states[kv] = attend(
                query_rows_here,
                kv,
                stages[kv],
                states[kv],
                cache_rows,
                kv_heads,
                n_hd,
                2 if dense else 1,
                finish,
            )
            if finish:
                attended.append(states[kv][0])
                continue
            came = [x for _, x in onward[kv]]
            came, states[kv] = lax.optimization_barrier((came, states[kv]))
            onward[kv] = [(hop, x) for (hop, _), x in zip(onward[kv], came)]
            for hop, x in onward[kv]:
                if hop == distance + 1:
                    up[kv] = x
                else:
                    down[kv] = x
        if distance == 0:
            residual, states[0] = lax.optimization_barrier((residual, states[0]))
            residual_parts = hand_over(split_rows(residual, n_sub))
        arrived = onward
    parts = states[-1]
    if dense:
        *parts, own_table = parts
    if n_hd == 2:
        kept, sent = parts[: len(parts) // 2], parts[len(parts) // 2 :]
        came = [lax.ppermute(x, "hd", cycle(n_hd)) for x in sent]
        if dense:
            gate_table = gates_by_chip(own_table, came[0], n_ep, n_hd)
    else:
        kept = [None]
        came = [lax.psum_scatter(parts[0], "hd", scatter_dimension=0, tiled=True)]
    hidden, normed = [], []
    for index, (kept_chunk, came_chunk) in enumerate(zip(kept, came)):
        pair = normalise(
            kept_chunk,
            came_chunk,
            residual_parts,
            norm_gain,
            index * came_chunk.shape[0],
        )
        hidden.append(pair[0])
        normed.append(pair[1])
    if not dense:
        own_columns = [
            jnp.concatenate(by_sub(sub_exchange(x, 1)), axis=0) for x in (hidden[0], normed[0])
        ]
        return sparse_experts(
            own_columns[0].astype(jnp.float32),
            own_columns[1],
            gate_up,
            w_down,
            expert_ids,
            gates,
            features,
        )
    mine, to_back, to_ahead = dense_experts(normed, gate_table, gate_up_parts, w_down_parts)
    return stack_rows(hand_over(add_up(hidden, mine, to_back, to_ahead, n_sub)))


def solution(mesh):
    return jax.shard_map(
        shards,
        mesh=mesh,
        in_specs=(
            P(("grp", "ep"), "hd"),
            P(("grp", "ep", "sub"), None),
            P(("grp", "ep", "sub"), None),
            P(("grp", "ep", "sub")),
            P(("grp", "ep", "sub"), None),
            P(("grp", "ep", "sub"), None),
            P("hd", "sub"),
            P(("grp", "ep", "hd"), "sub"),
            P(),
            P(("ep", "hd"), None, "sub", None),
            P(("ep", "hd"), "sub", None),
            P(("grp", "ep", "hd"), None),
            P(("grp", "ep", "hd"), None),
        ),
        out_specs=P(("grp", "ep", "hd"), "sub"),
        check_vma=False,
    )
```

```python
import functools
import math

import jax
import jax.numpy as jnp
from jax import lax
from jax.experimental import pallas as pl
from jax.experimental.pallas import tpu as pltpu
from jax.sharding import PartitionSpec as P

QH = 32
KVH = 4
HD = 128
GROUPS_ROW = 4
NEG_FILL = -1e30
EPSILON = 1e-06
MASK_ROWS = 16
TABLE_ROWS = 8
LANES = 128
MIB = 1024 * 1024
CONTRACT_LAST = (((1,), (1,)), ((), ()))


def block_sizes(block_rows, group_total, experts_group):
    group_slots = min(block_rows, 3 * GROUPS_ROW * block_rows // (2 * group_total))
    return (group_slots, 2 * group_slots // experts_group)


def cycle(size, step=1):
    return [(i, (i + step) % size) for i in range(size)]


def sub_copies(x):
    size = lax.axis_size("sub")
    return [x] + [lax.ppermute(x, "sub", cycle(size, step)) for step in range(1, size)]


def by_sub(copies):
    size = len(copies)
    me = lax.axis_index("sub")
    ordered = []
    for target in range(size):
        value = copies[0]
        for step in range(1, size):
            value = jnp.where((me - step) % size == target, copies[step], value)
        ordered.append(value)
    return ordered


def sub_exchange(x, axis):
    size = lax.axis_size("sub")
    me = lax.axis_index("sub")
    length = x.shape[axis] // size

    def part(index):
        return lax.dynamic_slice_in_dim(x, index * length, length, axis)

    came = [part(me)]
    for step in range(1, size):
        came.append(lax.ppermute(part((me + step) % size), "sub", cycle(size, step)))
    return came


def pack_keys(cache_keys, cache_values, new_keys, new_values, page_len, routing, kv_heads, heads_here):
    cache_rows, new_rows = cache_keys.shape[0], new_keys.shape[0]
    group_width = QH // KVH
    rows = cache_rows + new_rows + MASK_ROWS

    def kernel(page_ref, ck_ref, cv_ref, nk_ref, nv_ref, *refs):
        routing_refs, out_refs = refs[: len(routing)], refs[len(routing) :]
        first = lax.axis_index("hd") * heads_here // group_width
        lane = lax.broadcasted_iota(jnp.int32, (MASK_ROWS, 2 * HD), 1)
        bias = jnp.where(lane < page_ref[0], 0.0, NEG_FILL).astype(jnp.bfloat16)
        for kv, out_ref in enumerate(out_refs):
            columns = pl.ds(pl.multiple_of((first + kv) * HD, HD), HD)
            out_ref[:cache_rows, :HD] = ck_ref[:, columns]
            out_ref[:cache_rows, HD:] = cv_ref[:, columns]
            out_ref[cache_rows : cache_rows + new_rows, :HD] = nk_ref[:, columns]
            out_ref[cache_rows : cache_rows + new_rows, HD:] = nv_ref[:, columns]
            out_ref[cache_rows + new_rows :, :] = bias
        if routing:
            ids = routing_refs[0][...]
            gates = routing_refs[1][...].astype(jnp.float32)
            expert = lax.broadcasted_iota(jnp.int32, (MASK_ROWS, ids.shape[1]), 0)
            table = jnp.zeros(expert.shape, jnp.float32)
            for k in range(ids.shape[0]):
                table = table + jnp.where(ids[k : k + 1, :] == expert, gates[k : k + 1, :], 0.0)
            out_refs[0][cache_rows + new_rows :, HD:] = table.astype(jnp.bfloat16)

    vmem = pl.BlockSpec(memory_space=pltpu.VMEM)
    return pl.pallas_call(
        kernel,
        out_shape=[jax.ShapeDtypeStruct((rows, 2 * HD), cache_keys.dtype)] * kv_heads,
        in_specs=[pl.BlockSpec(memory_space=pltpu.SMEM)] + [vmem] * (4 + len(routing)),
        out_specs=[vmem] * kv_heads,
        name="pack_keys",
    )(page_len, cache_keys, cache_values, new_keys, new_values, *routing)


def small_kernel(kernel, out_shape, operands, name):
    vmem = pl.BlockSpec(memory_space=pltpu.VMEM)
    return pl.pallas_call(
        kernel,
        out_shape=out_shape,
        in_specs=[vmem] * len(operands),
        out_specs=[vmem] * len(out_shape),
        compiler_params=pltpu.CompilerParams(vmem_limit_bytes=8 * MIB),
        cost_estimate=pl.CostEstimate(flops=MIB, bytes_accessed=MIB, transcendentals=0),
        name=name,
    )(*operands)


def hand_over(parts):
    size = len(parts)
    return [parts[0]] + [
        lax.ppermute(part, "sub", cycle(size, step)) for step, part in enumerate(parts) if step
    ]


def choose_queries(queries):
    n_hd, n_sub, rows, columns = queries.shape

    def kernel(in_ref, out_ref, sems):
        sub = lax.axis_index("sub")
        hd = lax.axis_index("hd")
        copies = []
        for j in range(n_hd):
            place = (hd + j) % n_hd if n_hd == 2 else j
            copies.append(
                pltpu.make_async_copy(
                    in_ref.at[place, sub], out_ref.at[pl.ds(j * rows, rows), :], sems.at[j]
                )
            )
            copies[-1].start()
        for copy in copies:
            copy.wait()

    return pl.pallas_call(
        kernel,
        out_shape=jax.ShapeDtypeStruct((n_hd * rows, columns), queries.dtype),
        in_specs=[pl.BlockSpec(memory_space=pltpu.HBM)],
        out_specs=pl.BlockSpec(memory_space=pltpu.VMEM),
        scratch_shapes=[pltpu.SemaphoreType.DMA((n_hd,))],
        compiler_params=pltpu.CompilerParams(vmem_limit_bytes=8 * MIB),
        name="choose_queries",
    )(queries)


def split_rows(residual, n_sub):
    rows, columns = residual.shape[0] // n_sub, residual.shape[1]

    def kernel(in_ref, *out_refs):
        sub = lax.axis_index("sub")
        for step, out_ref in enumerate(out_refs):
            first = pl.multiple_of((sub + step) % n_sub * rows, rows)
            out_ref[...] = in_ref[pl.ds(first, rows), :]

    shape = jax.ShapeDtypeStruct((rows, columns), residual.dtype)
    return small_kernel(kernel, [shape] * n_sub, [residual], "split_rows")


def walk_place(ep, hd, n_ep, n_hd):
    if n_hd == 2:
        return jnp.where(hd == 0, ep, 2 * n_ep - 1 - ep)
    return ep * n_hd + hd


def gates_by_chip(own, came, n_ep, n_hd):
    block_rows = own.shape[1]
    places = slice(came.shape[1] - block_rows, came.shape[1])

    def kernel(own_ref, came_ref, out_ref):
        ep, hd = lax.axis_index("ep"), lax.axis_index("hd")
        mine = ep * n_hd + hd
        expert = lax.broadcasted_iota(jnp.int32, (TABLE_ROWS, block_rows), 0)
        place = lax.broadcasted_iota(jnp.int32, (LANES, block_rows), 0)
        table = jnp.zeros((LANES, block_rows), jnp.float32)
        tables = [(own_ref[...], hd), (came_ref[: n_ep * TABLE_ROWS, places], 1 - hd)]
        for joint, other in tables:
            joint = joint.astype(jnp.float32)
            for hop in range(n_ep):
                tile = joint[hop * TABLE_ROWS : (hop + 1) * TABLE_ROWS, :]
                row = jnp.sum(jnp.where(expert == mine, tile, 0.0), axis=0, keepdims=True)
                chip = walk_place((ep - hop) % n_ep, other, n_ep, n_hd)
                table = jnp.where(place == chip, row, table)
        out_ref[...] = table.T

    shape = jax.ShapeDtypeStruct((block_rows, LANES), jnp.float32)
    return small_kernel(kernel, [shape], [own, came], "gates_by_chip")[0]


def normalise(kept, came, residual_parts, gain, first):
    n_sub = len(residual_parts)
    rows, width = came.shape[0], residual_parts[0].shape[1]
    chunk = slice(first, first + rows)
    features = n_sub * width

    def kernel(*refs):
        refs = list(refs)
        kept_ref = refs.pop(0) if kept is not None else None
        came_ref = refs.pop(0)
        part_refs = [refs.pop(0) for _ in residual_parts]
        gain_ref = refs.pop(0)
        hidden_ref, normed_ref = refs
        sub = lax.axis_index("sub")
        hidden, places, squares = [], [], 0.0
        for step, part_ref in enumerate(part_refs):
            here = slice(step * width, (step + 1) * width)
            projected = came_ref[:, here].astype(jnp.float32)
            if kept is not None:
                projected = kept_ref[:, here] + projected
            value = (part_ref[chunk, :].astype(jnp.float32) + projected).astype(jnp.bfloat16)
            hidden.append(value)
            place = pl.ds(pl.multiple_of((sub - step) % n_sub * width, width), width)
            places.append(place)
            hidden_ref[:, place] = value
            wide = value.astype(jnp.float32)
            squares = squares + jnp.sum(wide * wide, axis=1, keepdims=True)
        scale = lax.rsqrt(squares / features + EPSILON)
        for value, place in zip(hidden, places):
            normed = value.astype(jnp.float32) * scale * gain_ref[:, place].astype(jnp.float32)
            normed_ref[:, place] = normed.astype(jnp.bfloat16)

    operands = ([kept] if kept is not None else []) + [came] + list(residual_parts)
    operands.append(gain.reshape(1, features))
    out_shape = [jax.ShapeDtypeStruct((rows, features), jnp.bfloat16)] * 2
    return small_kernel(kernel, out_shape, operands, "normalise")


def add_up(hidden, mine, to_back, to_ahead, n_sub):
    chunks = len(hidden)
    rows, features = hidden[0].shape
    width = features // n_sub

    def kernel(*refs):
        terms, out_refs = refs[: 4 * chunks], refs[4 * chunks :]
        sub = lax.axis_index("sub")
        for step, out_ref in enumerate(out_refs):
            place = pl.ds(pl.multiple_of((sub + step) % n_sub * width, width), width)
            for chunk in range(chunks):
                hidden_ref, mine_ref, back_ref, ahead_ref = terms[chunk::chunks]
                mixture = mine_ref[:, place] + back_ref[:, place].astype(jnp.float32)
                mixture = mixture + ahead_ref[:, place].astype(jnp.float32)
                total = hidden_ref[:, place].astype(jnp.float32) + mixture
                out_ref[chunk * rows : (chunk + 1) * rows, :] = total.astype(jnp.bfloat16)

    shape = jax.ShapeDtypeStruct((chunks * rows, width), jnp.bfloat16)
    operands = [*hidden, *mine, *to_back, *to_ahead]
    return small_kernel(kernel, [shape] * n_sub, operands, "add_up")


def stack_rows(parts):
    n_sub = len(parts)
    rows, width = parts[0].shape

    def kernel(*refs):
        sub = lax.axis_index("sub")
        for step, part_ref in enumerate(refs[:-1]):
            first = pl.multiple_of((sub - step) % n_sub * rows, rows)
            refs[-1][pl.ds(first, rows), :] = part_ref[...]

    shape = jax.ShapeDtypeStruct((n_sub * rows, width), parts[0].dtype)
    return small_kernel(kernel, [shape], parts, "stack_rows")[0]


def attend(queries, kv, stages, state, cache_rows, kv_heads, n_hd, chunks, finish=None):
    all_rows, columns = queries.shape
    rows, n_sub = all_rows // n_hd, len(stages[0][1])
    blocks = [block for _, stage_blocks in stages for block in stage_blocks]
    origins = [(hop, step) for hop, _ in stages for step in range(n_sub)]
    per_kv = columns // HD // kv_heads
    stack = 1
    part = stack * all_rows
    new_rows = blocks[0].shape[0] - cache_rows - MASK_ROWS
    keys = cache_rows + new_rows
    factor = math.log2(math.e) / math.sqrt(HD)
    relative = n_hd == 2
    last = finish is not None
    weights, earlier, tables = finish if last else ([], [], [])
    head_columns = per_kv * HD
    final = last and kv == kv_heads - 1
    kept_rows = rows if relative else 0
    chunk_rows = rows // chunks if relative else all_rows

    def kernel(*refs):
        q_ref, refs = refs[0], refs[1:]
        block_refs, refs = refs[: len(blocks)], refs[len(blocks) :]
        if state is not None:
            (m_in, acc_in), refs = refs[:2], refs[2:]
        weight_refs, refs = refs[: len(weights)], refs[len(weights) :]
        table_refs, refs = refs[: len(tables)], refs[len(tables) :]
        earlier_refs, refs = refs[: len(earlier)], refs[len(earlier) :]
        if last:
            results = len(out_shape)
            result_refs, refs = refs[:results], refs[results:]
            head_ref, refs = refs[0], refs[1:]
            copies = []
            if tables:
                result_refs, own_table_ref = result_refs[:-1], result_refs[-1]
                held_ref, sems = refs
                for i, table_ref in enumerate(table_refs):
                    copies.append(
                        pltpu.make_async_copy(
                            table_ref.at[pl.ds(keys, MASK_ROWS), pl.ds(HD, HD)],
                            held_ref.at[pl.ds(i * MASK_ROWS, MASK_ROWS), :],
                            sems.at[i],
                        )
                    )
                    copies[-1].start()
        else:
            m_out, acc_out = refs
        sub = lax.axis_index("sub")
        ep = lax.axis_index("ep")
        hd = lax.axis_index("hd")
        places = [(hd + j) % n_hd if relative else j for j in range(n_hd)]
        biases = []
        for (hop, step), block in zip(origins, block_refs):
            cache_bias = block[keys : keys + 1, :cache_rows].astype(jnp.float32)
            if hop == 0:
                key_id = ((sub - step) % n_sub) * new_rows + lax.broadcasted_iota(
                    jnp.int32, (rows, new_rows), 1
                )
                row_id = lax.broadcasted_iota(jnp.int32, (rows, new_rows), 0)
                seen = [
                    jnp.where(
                        key_id <= row_id + (place * n_sub + sub) * rows, 0.0, NEG_FILL
                    )
                    for place in places
                ]
                new_bias = jnp.concatenate(seen * stack, axis=0)
                cache_bias = jnp.broadcast_to(cache_bias, (part, cache_rows))
            else:
                new_bias = jnp.full(
                    (1, new_rows), jnp.where(ep >= hop, 0.0, NEG_FILL), jnp.float32
                )
            biases.append(jnp.concatenate([cache_bias, new_bias], axis=1))
        ones = jnp.ones((keys, HD), jnp.bfloat16)
        key_parts = [block[:keys, :HD] for block in block_refs]
        value_parts = [
            jnp.concatenate([block[:keys, HD:], ones], axis=1) for block in block_refs
        ]
        for index in range(per_kv // stack):
            here = slice(index * part, (index + 1) * part)
            heads = range(kv * per_kv + index * stack, kv * per_kv + (index + 1) * stack)
            q = jnp.concatenate([q_ref[:, h * HD : (h + 1) * HD] for h in heads], axis=0)
            terms = [
                lax.dot_general(q, k, CONTRACT_LAST, preferred_element_type=jnp.float32) * factor
                + bias
                for k, bias in zip(key_parts, biases)
            ]
            top = jnp.max(functools.reduce(jnp.maximum, terms), axis=1, keepdims=True)
            top = jnp.broadcast_to(top, (part, LANES))
            if state is not None:
                top_in = m_in[here, :]
                top = jnp.maximum(top, top_in)
            wide_top = jnp.concatenate([top] * (keys // LANES), axis=1)
            acc = None
            for term, v in zip(terms, value_parts):
                exp_terms = jnp.exp2(term - wide_top).astype(jnp.bfloat16)
                product = jnp.dot(exp_terms, v, preferred_element_type=jnp.float32)
                acc = product if acc is None else acc + product
            if state is not None:
                scale = jnp.exp2(top_in - top)
                acc = acc + jnp.concatenate([scale, scale], axis=1) * acc_in[here, :]
            if last:
                out = (acc[:, :HD] / acc[:, HD:]).astype(jnp.bfloat16)
                for s in range(stack):
                    first = (index * stack + s) * HD
                    head_ref[:, first : first + HD] = out[s * all_rows : (s + 1) * all_rows]
            else:
                m_out[here, :] = top
                acc_out[here, :] = acc
        if last:
            source = jnp.concatenate([ref[...] for ref in earlier_refs] + [head_ref[...]], axis=1)
            for i, weight_ref in enumerate(weight_refs):
                width = weight_ref.shape[1]
                here = slice(i * width, (i + 1) * width)
                product = jnp.dot(source, weight_ref[...], preferred_element_type=jnp.float32)
                for j, result_ref in enumerate(result_refs):
                    share = product[j * chunk_rows : (j + 1) * chunk_rows]
                    result_ref[:, here] = share.astype(result_ref.dtype)
            if not final:
                result_refs[0][...] = head_ref[...]
            if tables:
                for copy in copies:
                    copy.wait()
                joint = jnp.concatenate(
                    [
                        held_ref[i * MASK_ROWS : (i + 1) * MASK_ROWS, :].astype(jnp.float32)[
                            :TABLE_ROWS
                        ]
                        for i in range(len(tables))
                    ],
                    axis=0,
                ).astype(jnp.bfloat16)
                own_table_ref[...] = joint
                result_refs[len(result_refs) // 2][: joint.shape[0], features:] = joint

    vmem = pl.BlockSpec(memory_space=pltpu.VMEM)
    scratch = []
    if last:
        features = sum(w.shape[1] for w in weights)
        if final:
            out_shape = [
                jax.ShapeDtypeStruct((chunk_rows, features), kind)
                for kind, count in [
                    (jnp.float32, kept_rows // chunk_rows),
                    (jnp.bfloat16, (all_rows - kept_rows) // chunk_rows),
                ]
                for _ in range(count)
            ]
        else:
            out_shape = [jax.ShapeDtypeStruct((all_rows, head_columns), jnp.bfloat16)]
        scratch = [pltpu.VMEM((all_rows, head_columns), jnp.bfloat16)]
        if tables:
            joint = (len(tables) * TABLE_ROWS, LANES)
            first = len(out_shape) // 2
            out_shape[first] = jax.ShapeDtypeStruct((chunk_rows, features + LANES), jnp.bfloat16)
            out_shape.append(jax.ShapeDtypeStruct(joint, jnp.bfloat16))
            scratch += [
                pltpu.VMEM((len(tables) * MASK_ROWS, LANES), jnp.bfloat16),
                pltpu.SemaphoreType.DMA((len(tables),)),
            ]
    else:
        out_shape = (
            jax.ShapeDtypeStruct((per_kv * all_rows, LANES), jnp.float32),
            jax.ShapeDtypeStruct((per_kv * all_rows, 2 * HD), jnp.float32),
        )
    operands = [queries] + list(blocks) + (list(state) if state is not None else [])
    operands += list(weights)
    in_specs = [vmem] * len(operands) + [pl.BlockSpec(memory_space=pl.ANY)] * len(tables)
    operands += list(tables)
    operands += list(earlier)
    in_specs += [vmem] * len(earlier)
    scores = all_rows * per_kv * keys * len(blocks)
    return pl.pallas_call(
        kernel,
        out_shape=out_shape,
        in_specs=in_specs,
        out_specs=tuple(vmem for _ in out_shape),
        scratch_shapes=scratch,
        compiler_params=pltpu.CompilerParams(vmem_limit_bytes=16 * MIB),
        cost_estimate=pl.CostEstimate(
            flops=6 * scores * HD, bytes_accessed=4 * MIB, transcendentals=scores
        ),
        name="attend",
    )(*operands)


def apply_expert(inputs, origins, gate_table, gate_up, w_down, kind=jnp.float32):
    features = w_down[0].shape[1]
    hidden = w_down[0].shape[0]
    rows = sum(x.shape[0] for x in inputs)
    n_ep, n_hd, n_sub = lax.axis_size("ep"), lax.axis_size("hd"), lax.axis_size("sub")
    chunks = gate_table.shape[0] // n_sub // inputs[0].shape[0]

    def kernel(*refs):
        x_refs, refs = refs[: len(inputs)], refs[len(inputs) :]
        gate_ref, refs = refs[0], refs[1:]
        gu_refs, refs = refs[: len(gate_up)], refs[len(gate_up) :]
        down_refs, out_refs = refs[: len(w_down)], refs[len(w_down) :]
        x = jnp.concatenate([x[...] for x in x_refs], axis=0)
        here = walk_place(lax.axis_index("ep"), lax.axis_index("hd"), n_ep, n_hd)
        columns = []
        for (steps, chunk), x_ref in zip(origins, x_refs):
            count = x_ref.shape[0]
            sub = (lax.axis_index("sub") + steps) % n_sub
            first = pl.multiple_of((sub * chunks + chunk) * count, count)
            table = gate_ref[pl.ds(first, count), :]
            lane = lax.broadcasted_iota(jnp.int32, table.shape, 1)
            chip = (here + steps) % (n_ep * n_hd)
            columns.append(jnp.sum(jnp.where(lane == chip, table, 0.0), axis=1, keepdims=True))
        gate = jnp.concatenate(columns, axis=0)
        total = None
        for gu, down in zip(gu_refs, down_refs):
            gate_part = lax.dot_general(
                x, gu[0], CONTRACT_LAST, preferred_element_type=jnp.float32
            )
            up_part = lax.dot_general(x, gu[1], CONTRACT_LAST, preferred_element_type=jnp.float32)
            activation = (gate_part / (1.0 + jnp.exp(-gate_part)) * up_part).astype(jnp.bfloat16)
            product = jnp.dot(activation, down[...], preferred_element_type=jnp.float32)
            total = product if total is None else total + product
        total = gate * total.astype(jnp.bfloat16).astype(jnp.float32)
        first = 0
        for out_ref in out_refs:
            out_ref[...] = total[first : first + out_ref.shape[0]].astype(kind)
            first += out_ref.shape[0]

    vmem = pl.BlockSpec(memory_space=pltpu.VMEM)
    operands = list(inputs) + [gate_table] + list(gate_up) + list(w_down)
    return pl.pallas_call(
        kernel,
        out_shape=[jax.ShapeDtypeStruct((x.shape[0], features), kind) for x in inputs],
        in_specs=[vmem] * len(operands),
        out_specs=[vmem] * len(inputs),
        compiler_params=pltpu.CompilerParams(vmem_limit_bytes=16 * MIB),
        cost_estimate=pl.CostEstimate(
            flops=6 * rows * hidden * len(w_down) * features,
            bytes_accessed=6 * MIB,
            transcendentals=rows * hidden * len(w_down),
        ),
        name="apply_expert",
    )(*operands)


def chip_ring(n_ep, n_hd):
    if n_hd == 2:
        return [z * 2 for z in range(n_ep)] + [z * 2 + 1 for z in reversed(range(n_ep))]
    return list(range(n_ep * n_hd))


def add_share(came, share):
    def kernel(came_ref, share_ref, out_ref):
        total = came_ref[...].astype(jnp.float32) + share_ref[...]
        out_ref[...] = total.astype(jnp.bfloat16)

    shape = jax.ShapeDtypeStruct(share.shape, jnp.bfloat16)
    return small_kernel(kernel, [shape], [came, share], "add_share")[0]


def dense_experts(own, gate_table, gate_up, w_down):
    axes = ("ep", "hd", "sub")
    walk = chip_ring(lax.axis_size("ep"), lax.axis_size("hd"))
    size, n_sub = len(walk), lax.axis_size("sub")
    ahead = [
        (walk[i] * n_sub + sub, walk[(i + 1) % size] * n_sub + (sub + 1) % n_sub)
        for i in range(size)
        for sub in range(n_sub)
    ]
    back = [(b, a) for a, b in ahead]
    reach = size // 2
    behind, before, waiting = list(own), list(own), None
    outs = [None]
    for hop in range(1, reach + 1):
        behind[0] = lax.ppermute(behind[0], axes, ahead)
        before[1] = lax.ppermute(before[1], axes, back)
        if hop < reach:
            behind[1] = lax.ppermute(behind[1], axes, ahead)
            before[0] = lax.ppermute(before[0], axes, back)
        if waiting:
            out = apply_expert(waiting, origins, gate_table, gate_up, w_down)
            late = int(hop < reach)
            behind[late], out = lax.optimization_barrier((behind[late], out))
            outs.append(out)
        waiting = [behind[0], before[1]] + ([behind[1], before[0]] if hop < reach else [])
        origins = [(-hop, 0), (hop, 1), (-hop, 1), (hop, 0)][: len(waiting)]
    outs.append(apply_expert(waiting, origins, gate_table, gate_up, w_down, jnp.bfloat16))
    to_back, to_ahead = [None, None], [None, None]
    for hop in range(reach, 0, -1):
        shares = outs[hop]
        for chunks, chunk, way, share in [
            (to_back, 0, back, 0),
            (to_ahead, 1, ahead, 1),
            (to_back, 1, back, 2),
            (to_ahead, 0, ahead, 3),
        ]:
            if share >= len(shares):
                continue
            if chunks[chunk] is None:
                sum_here = shares[share].astype(jnp.bfloat16)
            else:
                sum_here = add_share(chunks[chunk], shares[share])
            chunks[chunk] = lax.ppermute(sum_here, axes, way)
            if hop == min(2, reach) and share == 0:
                chunks[chunk], own = lax.optimization_barrier((chunks[chunk], own))
    mine = apply_expert(own, [(0, 0), (0, 1)], gate_table, gate_up, w_down)
    return mine, to_back, to_ahead


def sparse_experts(widened, normed, gate_up, w_down, expert_ids, gates, features):
    half_width = normed.shape[1]
    pair_weights = gate_up[0].reshape(-1, features)
    hidden_units = w_down.shape[1]
    group_total = lax.axis_size("ep")
    group_experts = lax.axis_size("hd")
    all_experts = group_total * group_experts
    block_rows = expert_ids.shape[0]
    group_slots, expert_slots = block_sizes(block_rows, group_total, group_experts)
    chosen = (
        expert_ids[:, :, None] == jnp.arange(all_experts, dtype=jnp.int32)[None, None, :]
    ).astype(jnp.int32)
    named_count = jnp.sum(chosen, axis=1)
    earlier = jnp.cumsum(named_count, axis=0) - named_count
    slot_index = jnp.sum(chosen * earlier[:, None, :], axis=2)
    position = expert_ids * expert_slots + slot_index
    slot_columns = jnp.arange(all_experts * expert_slots, dtype=jnp.int32)
    gate_table = jnp.sum(
        jnp.where(
            position[:, :, None] == slot_columns[None, None, :],
            gates.astype(jnp.float32)[:, :, None],
            0.0,
        ),
        axis=1,
    ).astype(jnp.bfloat16)
    placed = (gate_table != 0).astype(jnp.bfloat16)
    outgoing = jnp.einsum("rq,rd->qd", placed, normed, preferred_element_type=jnp.float32).astype(
        jnp.bfloat16
    )
    outgoing = outgoing.reshape(all_experts, expert_slots, normed.shape[1])
    arrived = lax.all_to_all(outgoing, ("ep", "hd"), split_axis=0, concat_axis=0, tiled=True)
    lead_shape = arrived.shape[:-1]
    rows_in = arrived.reshape(-1, arrived.shape[-1])
    rows_in = lax.all_gather(rows_in, "sub", axis=1, tiled=True)
    projected_pair = jnp.einsum(
        "rd,fd->rf", rows_in, pair_weights, preferred_element_type=jnp.float32
    )
    activation = (
        jax.nn.silu(projected_pair[:, :hidden_units]) * projected_pair[:, hidden_units:]
    ).astype(jnp.bfloat16)
    partial_out = jnp.dot(activation, w_down[0], preferred_element_type=jnp.float32)
    expert_out = lax.psum_scatter(
        partial_out.astype(jnp.bfloat16), "sub", scatter_dimension=1, tiled=True
    )
    results = expert_out.reshape(lead_shape + (expert_out.shape[1],))
    returned = lax.all_to_all(results, ("ep", "hd"), split_axis=0, concat_axis=0, tiled=True)
    mixture = jnp.dot(
        gate_table,
        returned.reshape(all_experts * expert_slots, half_width),
        preferred_element_type=jnp.float32,
    )
    return (widened + mixture).astype(jnp.bfloat16)


def shards(
    queries,
    cache_keys,
    cache_values,
    page_len,
    new_keys,
    new_values,
    out_proj,
    residual,
    norm_gain,
    gate_up,
    w_down,
    expert_ids,
    gates,
):
    n_ep, n_hd, n_sub = lax.axis_size("ep"), lax.axis_size("hd"), lax.axis_size("sub")
    query_rows = queries.shape[0]
    heads_here = queries.shape[1] // HD
    kv_heads = max(1, heads_here // (QH // KVH))
    rows = query_rows // (n_hd * n_sub)
    features = norm_gain.shape[0]
    cache_rows = cache_keys.shape[0]
    all_experts = n_ep * n_hd * gate_up.shape[0]
    dense = (
        expert_ids.shape[1] == all_experts
        and gate_up.shape[0] == 1
        and n_hd == 2
        and rows % 32 == 0
        and all_experts <= TABLE_ROWS
        and cache_rows <= HD
        and n_ep * TABLE_ROWS <= rows // 2
        and expert_ids.shape[0] == LANES
    )

    packed = pack_keys(
        cache_keys,
        cache_values,
        new_keys,
        new_values,
        page_len,
        [expert_ids.T, gates.T] if dense else [],
        kv_heads,
        heads_here,
    )
    query_rows_here = choose_queries(queries.reshape(n_hd, n_sub, rows, heads_here * HD))
    reach = n_ep // 2
    up, down = list(packed), list(packed)
    arrived = [[(0, x)] for x in packed]
    tables = {}
    states = [None] * kv_heads
    attended = []
    for distance in range(reach + 1):
        stages = [[(hop, sub_copies(x)) for hop, x in blocks] for blocks in arrived]
        if distance == 0:
            out_proj, packed = lax.optimization_barrier((out_proj, packed))
            projections = sub_copies(out_proj)
        if distance == reach and dense:
            blocks = [x for kv_stages in stages for _, x in kv_stages]
            gate_up, w_down, blocks = lax.optimization_barrier((gate_up, w_down, blocks))
            stages = [
                [(hop, blocks.pop(0)) for hop, _ in kv_stages] for kv_stages in stages
            ]
            gate_up_parts = sub_copies(gate_up[0])
            w_down_parts = sub_copies(w_down[0])
        for hop, x in arrived[0]:
            tables[hop] = x
        onward = [[] for _ in packed]
        if distance < reach:
            opposite = 2 * (distance + 1) == n_ep
            for kv in range(kv_heads):
                if not opposite or kv % 2 == 0:
                    up[kv] = lax.ppermute(up[kv], "ep", cycle(n_ep))
                    onward[kv].append((distance + 1, up[kv]))
                if not opposite or kv % 2 == 1:
                    down[kv] = lax.ppermute(down[kv], "ep", cycle(n_ep, n_ep - 1))
                    onward[kv].append((n_ep - distance - 1, down[kv]))
        for kv in range(kv_heads):
            finish = None
            if distance == reach:
                joint = [tables[hop] for hop in range(n_ep)] if dense and kv == kv_heads - 1 else []
                finish = (projections, list(attended), joint)
                if kv < kv_heads - 1:
                    finish = ([], [], [])
            states[kv] = attend(
                query_rows_here,
                kv,
                stages[kv],
                states[kv],
                cache_rows,
                kv_heads,
                n_hd,
                2 if dense else 1,
                finish,
            )
            if finish:
                attended.append(states[kv][0])
                continue
            came = [x for _, x in onward[kv]]
            came, states[kv] = lax.optimization_barrier((came, states[kv]))
            onward[kv] = [(hop, x) for (hop, _), x in zip(onward[kv], came)]
            for hop, x in onward[kv]:
                if hop == distance + 1:
                    up[kv] = x
                else:
                    down[kv] = x
        if distance == 0:
            residual, states[0] = lax.optimization_barrier((residual, states[0]))
            residual_parts = hand_over(split_rows(residual, n_sub))
        arrived = onward
    parts = states[-1]
    if dense:
        *parts, own_table = parts
    if n_hd == 2:
        kept, sent = parts[: len(parts) // 2], parts[len(parts) // 2 :]
        came = [lax.ppermute(x, "hd", cycle(n_hd)) for x in sent]
        if dense:
            gate_table = gates_by_chip(own_table, came[0], n_ep, n_hd)
    else:
        kept = [None]
        came = [lax.psum_scatter(parts[0], "hd", scatter_dimension=0, tiled=True)]
    hidden, normed = [], []
    for index, (kept_chunk, came_chunk) in enumerate(zip(kept, came)):
        pair = normalise(
            kept_chunk,
            came_chunk,
            residual_parts,
            norm_gain,
            index * came_chunk.shape[0],
        )
        hidden.append(pair[0])
        normed.append(pair[1])
    if not dense:
        own_columns = [
            jnp.concatenate(by_sub(sub_exchange(x, 1)), axis=0) for x in (hidden[0], normed[0])
        ]
        return sparse_experts(
            own_columns[0].astype(jnp.float32),
            own_columns[1],
            gate_up,
            w_down,
            expert_ids,
            gates,
            features,
        )
    mine, to_back, to_ahead = dense_experts(normed, gate_table, gate_up_parts, w_down_parts)
    return stack_rows(hand_over(add_up(hidden, mine, to_back, to_ahead, n_sub)))


def solution(mesh):
    return jax.shard_map(
        shards,
        mesh=mesh,
        in_specs=(
            P(("grp", "ep"), "hd"),
            P(("grp", "ep", "sub"), None),
            P(("grp", "ep", "sub"), None),
            P(("grp", "ep", "sub")),
            P(("grp", "ep", "sub"), None),
            P(("grp", "ep", "sub"), None),
            P("hd", "sub"),
            P(("grp", "ep", "hd"), "sub"),
            P(),
            P(("ep", "hd"), None, "sub", None),
            P(("ep", "hd"), "sub", None),
            P(("grp", "ep", "hd"), None),
            P(("grp", "ep", "hd"), None),
        ),
        out_specs=P(("grp", "ep", "hd"), "sub"),
        check_vma=False,
    )
```
